32 devices in a mesh: gx: 4 (over x, core), gy: 4 (over z), gz: 2 (over y).
Axes of the slice: x: 2, y: 2, z: 4, core: 2. Of those that a mesh axis runs over, the one named last changes fastest.
Arguments:
- sketch: float32 [8, 8, 4, 64, 384], P('gx', 'gy', 'gz'), may hold values from -1200 to 1200
- test_matrix: bfloat16 [8, 8, 4, 64, 384], P('gx', 'gy', 'gz'), may hold values from -0.1796875 to 0.1796875
- offsets: bfloat16 [8, 8, 4, 3, 128], P('gx', 'gy', 'gz'), may hold values from 0 to 1
- near: int32 [8, 8, 4, 27], P('gx', 'gy', 'gz'), may hold values 0 or 1
Outputs:
- leaf_basis: float32 [8, 8, 4, 64, 384], P('gx', 'gy', 'gz')
- level1_transfer: float32 [4, 4, 2, 64, 512], P('gx', 'gy', 'gz')
- level2_basis: float32 [8, 8, 4, 64, 384], P('gx', 'gy', 'gz')
The draws below stay inside these ranges and needn't reach their ends.
All inputs are finite; a program needn't handle non-finite values. No bound on the sum of `near` on one device may be relied on, other than what follows from the above.
Results may differ from the reference program's by a relative error of at most 0.0029.
Values may be sent and summed in bfloat16 or wider, within the bound.
No kernel may reach another device: no remote copies, remote signals or barrier semaphores. Data moves between devices by JAX's collectives and lax.ppermute only.
A program may use at most 64 MiB of HBM per device.

```python
import math
import jax
import jax.numpy as jnp
from jax import lax

NODES = 128
RANK = 64
LEAF_ROWS = 384
LEAVES_X = 8
LEAVES_Y = 8
LEAVES_Z = 4
N_GX = 4
N_GY = 4
N_GZ = 2


def draw_sketch(key, part):
    key_sign = jax.random.fold_in(key, 11)
    key_size = jax.random.fold_in(key, 12)
    key_common = jax.random.fold_in(key, 13)
    key_noise = jax.random.fold_in(key, 14)
    whole_shape = (LEAVES_X, LEAVES_Y, LEAVES_Z, RANK, LEAF_ROWS)
    signs = (2 * jax.random.randint(key_sign, (RANK,), 0, 2) - 1).astype(jnp.float32)
    sizes = jax.random.uniform(key_size, (RANK,), jnp.float32, 0.5, 1.5)
    amplitude = 160.0
    noise = 2.0 * jax.random.truncated_normal(key_noise, -4.0, 4.0, whole_shape, jnp.float32)
    common = jax.random.truncated_normal(key_common, -4.0, 4.0, (LEAVES_X, LEAVES_Y, LEAVES_Z, 1, LEAF_ROWS), jnp.float32)
    coupling = (amplitude * signs * sizes)[:, None]
    return (coupling * common + noise).astype(jnp.float32)


def touch_ends(values, rng, low, largest):
    spot = [jax.random.randint(jax.random.fold_in(rng, axis), (), 0, length) for axis, length in enumerate(values.shape)]
    main_axis = values.shape.index(max(values.shape))
    neighbour = spot[:main_axis] + [(spot[main_axis] + 1) % values.shape[main_axis]] + spot[main_axis + 1:]
    return values.at[tuple(spot)].set(low).at[tuple(neighbour)].set(largest)


def levels(rng, dims, pieces, low, largest):
    def one(position, parts):
        steps = jax.random.uniform(jax.random.fold_in(jax.random.fold_in(rng, 6), position), (parts,), jnp.float32, low / len(pieces), largest / len(pieces))
        return jnp.repeat(jnp.exp(steps), dims[position] // parts).reshape((-1,) + (1,) * (len(dims) - position - 1))

    level = one(*pieces[0])
    for cut in pieces[1:]:
        level = level * one(*cut)
    return level


def gaussian(own_key, dims, scale, most, pieces=(), kind=jnp.bfloat16):
    drawn = jax.random.normal(own_key, dims, jnp.float32) * scale
    if len(pieces) > 0:
        drawn = levels(own_key, dims, pieces, -0.22, 0.18) * drawn
    return jnp.clip(drawn, min=-most, max=most).astype(kind)


def setup_inputs(seed: int = 0) -> dict:
    streams_of = jax.random.split(jax.random.key(seed), 5)
    sketch = draw_sketch(jax.random.fold_in(streams_of[4], 71), 0)
    test_matrix = gaussian(streams_of[1], (LEAVES_X, LEAVES_Y, LEAVES_Z, RANK, LEAF_ROWS), 0.03, 0.1796875, ((0, 4), (1, 4), (2, 2)))
    offsets = jnp.clip(1.0 * jax.random.uniform(streams_of[2], (LEAVES_X, LEAVES_Y, LEAVES_Z, 3, NODES), jnp.float32) ** levels(streams_of[2], (LEAVES_X, LEAVES_Y, LEAVES_Z, 3, NODES), ((0, 4), (1, 4), (2, 2)), -0.2, 0.2), 0.0, 1.0).astype(jnp.bfloat16)
    near = touch_ends((jax.random.randint(streams_of[3], (LEAVES_X, LEAVES_Y, LEAVES_Z, 27), 0, 4) < 3).astype(jnp.int32), jax.random.fold_in(streams_of[3], 1), 0, 1)
    return {"sketch": sketch, "test_matrix": test_matrix, "offsets": offsets, "near": near}


EPSILON = 0.1
HIGHEST = lax.Precision.HIGHEST

def orthonormal(rows_t):
    gram_matrix = jnp.einsum('...km,...lm->...kl', rows_t, rows_t, precision=HIGHEST)
    first_factor = jnp.linalg.cholesky(gram_matrix)
    orthogonal = lax.linalg.triangular_solve(first_factor, rows_t, left_side=True, lower=True)
    gram_matrix = jnp.einsum('...km,...lm->...kl', orthogonal, orthogonal, precision=HIGHEST)
    second = jnp.linalg.cholesky(gram_matrix)
    orthogonal = lax.linalg.triangular_solve(second, orthogonal, left_side=True, lower=True)
    return (orthogonal, jnp.matmul(first_factor, second, precision=HIGHEST))

def shift_table():
    offset_index = jnp.arange(27, dtype=jnp.int32)
    offset_steps = jnp.stack([offset_index // 9, offset_index // 3 % 3, offset_index % 3], axis=1)
    return (1 - offset_steps).astype(jnp.float32)

def kernel_tiles(own_offsets, near_offsets, shifts):
    separation = shifts[None, :, :, None, None] + own_offsets[:, None, :, :, None] - near_offsets[:, :, :, None, :]
    square = lax.optimization_barrier(jnp.sum(separation * separation, axis=2))
    softened = square + EPSILON * EPSILON
    inverse = 1.0 / (softened * jnp.sqrt(softened))
    diagonal = (square + 2.0 * EPSILON * EPSILON) * inverse
    identity = jnp.eye(3, dtype=jnp.float32)
    kernel_block = separation[:, :, :, None] * separation[:, :, None, :] * inverse[:, :, None, None] + identity[None, None, :, :, None, None] * diagonal[:, :, None, None]
    return kernel_block.astype(jnp.bfloat16)

def reference(sketch, test_matrix, offsets, near):
    leaf_rows = 3 * NODES
    padded_test = jnp.pad(test_matrix.reshape(LEAVES_X, LEAVES_Y, LEAVES_Z, RANK, 3, NODES), ((1, 1), (1, 1), (1, 1), (0, 0), (0, 0), (0, 0)))
    float_offsets = offsets.astype(jnp.float32)
    padded_offsets = jnp.pad(float_offsets, ((1, 1), (1, 1), (1, 1), (0, 0), (0, 0)))
    shifts = shift_table()

    def column_far(column_index):
        column_x = column_index // LEAVES_Y
        column_y = column_index % LEAVES_Y
        zero = jnp.zeros((), jnp.int32)
        test_block = lax.dynamic_slice(padded_test, (column_x, column_y, zero, zero, zero, zero), (3, 3, LEAVES_Z + 2, RANK, 3, NODES))
        offset_block = lax.dynamic_slice(padded_offsets, (column_x, column_y, zero, zero, zero), (3, 3, LEAVES_Z + 2, 3, NODES))
        sampled = jnp.stack([test_block[offset_index // 9, offset_index // 3 % 3, offset_index % 3:offset_index % 3 + LEAVES_Z] for offset_index in range(27)], axis=1)
        near_offsets = jnp.stack([offset_block[offset_index // 9, offset_index // 3 % 3, offset_index % 3:offset_index % 3 + LEAVES_Z] for offset_index in range(27)], axis=1)
        near_mask = lax.dynamic_slice(near, (column_x, column_y, zero, zero), (1, 1, LEAVES_Z, 27))[0, 0]
        own_offsets = lax.dynamic_slice(float_offsets, (column_x, column_y, zero, zero, zero), (1, 1, LEAVES_Z, 3, NODES))[0, 0]
        sampled = sampled * near_mask.astype(jnp.bfloat16)[:, :, None, None, None]
        kernel_block = kernel_tiles(own_offsets, near_offsets, shifts)
        correction = jnp.einsum('bkpqij,bkcqj->bcpi', kernel_block.astype(jnp.float32), sampled.astype(jnp.float32), precision=HIGHEST)
        own_sketch = lax.dynamic_slice(sketch, (column_x, column_y, zero, zero, zero), (1, 1, LEAVES_Z, RANK, leaf_rows))[0, 0]
        return own_sketch - correction.reshape(LEAVES_Z, RANK, leaf_rows)
    far_field = lax.map(column_far, jnp.arange(LEAVES_X * LEAVES_Y, dtype=jnp.int32))
    far_field = far_field.reshape(LEAVES_X, LEAVES_Y, LEAVES_Z, RANK, leaf_rows)
    leaf_t, leaf_lower = orthonormal(far_field)
    level_in = leaf_lower.reshape(N_GX, 2, N_GY, 2, N_GZ, 2, RANK, RANK).transpose(0, 2, 4, 6, 1, 3, 5, 7).reshape(N_GX, N_GY, N_GZ, RANK, 8 * RANK)
    level_t, level_lower = orthonormal(level_in)
    top_in = level_lower.reshape(N_GX // 2, 2, N_GY // 2, 2, N_GZ // 2, 2, RANK, RANK).transpose(0, 2, 4, 6, 1, 3, 5, 7).reshape(N_GX // 2, N_GY // 2, N_GZ // 2, RANK, 8 * RANK)
    top_t, top_lower = orthonormal(top_in)
    top_blocks = top_t.reshape(N_GX // 2, N_GY // 2, N_GZ // 2, RANK, 2, 2, 2, RANK).transpose(0, 4, 1, 5, 2, 6, 3, 7).reshape(N_GX, N_GY, N_GZ, RANK, RANK)
    level_blocks = level_t.reshape(N_GX, N_GY, N_GZ, RANK, 2, 2, 2, RANK).transpose(0, 4, 1, 5, 2, 6, 3, 7).reshape(LEAVES_X, LEAVES_Y, LEAVES_Z, RANK, RANK)
    top_leaf = jnp.broadcast_to(top_blocks[:, None, :, None, :, None], (N_GX, 2, N_GY, 2, N_GZ, 2, RANK, RANK)).reshape(LEAVES_X, LEAVES_Y, LEAVES_Z, RANK, RANK)
    mixing = jnp.matmul(top_leaf, level_blocks, precision=HIGHEST)
    level2_basis = jnp.matmul(mixing, leaf_t, precision=HIGHEST) * (8.0 * math.sqrt(leaf_rows))
    leaf_basis = leaf_t * math.sqrt(leaf_rows)
    level1_transfer = level_t * math.sqrt(8 * RANK)
    return (leaf_basis, level1_transfer, level2_basis)
```

```python
import math

import jax
import jax.numpy as jnp
from jax import lax
from jax.experimental import pallas as pl
from jax.experimental.pallas import tpu as pltpu
from jax.sharding import PartitionSpec as P

EPSILON = 0.1
HIGHEST = lax.Precision.HIGHEST


def with_halo(x, sides, width):
    for axis, dim in sides:
        size, length = (lax.axis_size(axis), x.shape[dim])
        up = [(i, (i + 1) % size) for i in range(size - 1)]
        down = [(j, i) for i, j in up]
        last = lax.slice_in_dim(x, length - width, length, axis=dim)
        initial = lax.slice_in_dim(x, 0, width, axis=dim)
        before = lax.ppermute(last, axis, up)
        after = lax.ppermute(initial, axis, down)
        x = jnp.concatenate([before, x, after], axis=dim)
    return x


def from_partner(x, axis, distance):
    return lax.ppermute(x, axis, [(i, i ^ 1 << distance) for i in range(lax.axis_size(axis))])


SMALL = 0.2


def matmul(a, b, precision=HIGHEST):
    return lax.dot_general(
        a, b, (((1,), (0,)), ((), ())), precision=precision, preferred_element_type=jnp.float32
    )


def matmul_t(a, b, precision=HIGHEST):
    return lax.dot_general(
        a, b, (((1,), (1,)), ((), ())), precision=precision, preferred_element_type=jnp.float32
    )


def halves(x):
    high = x.astype(jnp.bfloat16)
    return high, (x - high.astype(jnp.float32)).astype(jnp.bfloat16)


def positions(shape):
    return (
        lax.broadcasted_iota(jnp.int32, shape, 0),
        lax.broadcasted_iota(jnp.int32, shape, 1),
    )


def unit(rank):
    row, column = positions((rank, rank))
    return jnp.where(row == column, 1.0, 0.0).astype(jnp.float32)


def upper(x):
    row, column = positions(x.shape)
    return jnp.where(row <= column, x, 0.0)


def half_lower(x):
    row, column = positions(x.shape)
    return jnp.where(row > column, x, jnp.where(row == column, 0.5 * x, 0.0))


def excess_of(x):
    rank = x.shape[0]
    stacked = jnp.concatenate(halves(x), axis=0)
    products = matmul_t(stacked, stacked, None)
    crossed = products[:rank, rank:] + products[rank:, :rank]
    return products[:rank, :rank] + crossed


def near_unit_factor(excess):
    x = half_lower(excess)
    for _ in range(2):
        x = half_lower(excess - matmul_t(x, x, None))
    square = matmul(x, x, None)
    return x, x - square + matmul(square, x, None)


def batch_steps(work, rank, batch, width):
    shape = (batch, 2 * rank)

    def lane(values, index):
        return jnp.broadcast_to(values[:, rank + index : rank + index + 1], shape)

    for start in range(0, rank, width):
        rows = [work[(start + i) * batch : (start + i + 1) * batch, :] for i in range(width)]
        scalars = [
            [lane(rows[i], start + j) if j >= i else None for j in range(width)]
            for i in range(width)
        ]
        for j in range(width):
            root = lax.rsqrt(scalars[j][j])
            rows[j] = rows[j] * root
            factor = [None if i <= j else scalars[j][i] * root for i in range(width)]
            for i in range(j + 1, width):
                rows[i] = rows[i] - factor[i] * rows[j]
                for k in range(i, width):
                    scalars[i][k] = scalars[i][k] - factor[i] * factor[k]
            work[(start + j) * batch : (start + j + 1) * batch, :] = rows[j]
        for lower in range(start + width, rank):
            total = work[lower * batch : (lower + 1) * batch, :]
            for j in range(width):
                total = total - lane(rows[j], lower) * rows[j]
            work[lower * batch : (lower + 1) * batch, :] = total
        yield


def single_steps(work, rank):
    shape = (8, 2 * rank)
    row, _ = positions(shape)
    for start in range(0, rank, 8):
        z = work[start : start + 8, :]
        columns = [
            jnp.broadcast_to(z[:, rank + start + j : rank + start + j + 1], shape)
            for j in range(8)
        ]
        done = z
        for j in range(8):
            root = lax.rsqrt(columns[j][j : j + 1, :])
            scaled = z[j : j + 1, :] * root
            done = jnp.where(row == j, scaled, done)
            if j < 7:
                factor = columns[j] * root
                z = z - factor * scaled
                for i in range(j + 1, 8):
                    columns[i] = columns[i] - factor * (columns[i][j : j + 1, :] * root)
        work[start : start + 8, :] = done
        turned = done.T
        for lower in range(start + 8, rank, 8):
            total = work[lower : lower + 8, :]
            factors = turned[rank + lower : rank + lower + 8, :]
            for j in range(8):
                total = total - jnp.broadcast_to(factors[:, j : j + 1], shape) * done[j : j + 1, :]
            work[lower : lower + 8, :] = total
        yield


def run_together(*steps):
    for _ in zip(*steps):
        pass


def leaf_kernel(far, leaf_out, level_out, scaled_out, factor_out, work, single, es, xs, zs):
    count, rank, leaf_rows = far.shape
    eye = unit(rank)
    zeros = jnp.zeros((rank, leaf_rows), jnp.float32)
    left_unit = jnp.concatenate([eye, jnp.zeros_like(eye)], axis=1)
    total = left_unit
    for a in range(count):
        rows = far[a]
        gram = matmul_t(rows, jnp.concatenate([zeros, rows], axis=0))
        work[pl.ds(a, rank, stride=count), :] = left_unit + gram
        total = total + gram
    single[...] = total
    run_together(batch_steps(work, rank, count, 8), single_steps(single, rank))
    box_inverse = single[:, :rank]
    box_upper = upper(single[:, rank:])
    box_excess = -eye
    largest = jnp.zeros((1, 1), jnp.float32)
    for a in range(count):
        inverse = work[pl.ds(a, rank, stride=count), :][:, :rank]
        both = matmul(jnp.concatenate([inverse, box_inverse], axis=0), far[a])
        leaf_out[a] = both[:rank]
        scaled_out[a] = both[rank:]
        excess = excess_of(both[:rank]) - eye
        box_excess = box_excess + excess_of(both[rank:])
        xs[a], zs[a] = near_unit_factor(excess)
        es[a] = excess
        largest = jnp.maximum(largest, jnp.sum(excess * excess, keepdims=True))
    xs[count], zs[count] = near_unit_factor(box_excess)
    largest = jnp.maximum(largest, jnp.sum(box_excess * box_excess, keepdims=True))
    es[count] = box_excess
    uppers = [upper(work[pl.ds(a, rank, stride=count), :][:, rank:]) for a in range(count)]

    @pl.when(jnp.logical_not(largest[0, 0] <= SMALL * SMALL))
    def _():
        for a in range(count):
            work[pl.ds(a, rank, stride=count), :] = jnp.concatenate([eye, eye + es[a]], axis=1)
        single[...] = jnp.concatenate([eye, eye + es[count]], axis=1)
        run_together(batch_steps(work, rank, count, 8), single_steps(single, rank))
        for a in range(count + 1):
            rows = single[...] if a == count else work[pl.ds(a, rank, stride=count), :]
            xs[a] = upper(rows[:, rank:]).T - eye
            zs[a] = eye - rows[:, :rank]

    box_x, box_z = xs[count], zs[count]
    lower_box = box_upper.T
    factor_out[...] = lower_box + matmul(lower_box, box_x)
    for a in range(count):
        basis = leaf_out[a]
        leaf_out[a] = (basis - matmul(zs[a], basis)) * math.sqrt(leaf_rows)
        scaled = scaled_out[a]
        scaled_out[a] = scaled - matmul(box_z, scaled)
        block = matmul_t(box_inverse, uppers[a])
        block = block + matmul(block, xs[a])
        block = block - matmul(box_z, block)
        level_out[:, a * rank : (a + 1) * rank] = block * math.sqrt(count * rank)


def group_kernel(factors, scaled, nested_out, single, z_out):
    count, rank, _ = factors.shape
    eye = unit(rank)
    gram = jnp.zeros((rank, rank), jnp.float32)
    for b in range(count):
        gram = gram + matmul_t(factors[b], factors[b])
    single[...] = jnp.concatenate([eye, gram], axis=1)
    run_together(single_steps(single, rank))
    inverse = single[:, :rank]
    excess = -eye
    for b in range(count):
        block = matmul(inverse, factors[b])
        if b == 0:
            own = block
        excess = excess + excess_of(block)
    _, z_out[...] = near_unit_factor(excess)
    largest = jnp.sum(excess * excess, keepdims=True)

    @pl.when(jnp.logical_not(largest[0, 0] <= SMALL * SMALL))
    def _():
        single[...] = jnp.concatenate([eye, eye + excess], axis=1)
        run_together(single_steps(single, rank))
        z_out[...] = eye - single[:, :rank]

    z = z_out[...]
    mixing = (own - matmul(z, own)) * (8.0 * math.sqrt(scaled.shape[2]))
    for a in range(scaled.shape[0]):
        nested_out[a] = matmul(mixing, scaled[a])


def leaf_level(far):
    count, rank, leaf_rows = far.shape
    like = jax.ShapeDtypeStruct
    return pl.pallas_call(
        leaf_kernel,
        out_shape=(
            like(far.shape, jnp.float32),
            like((rank, count * rank), jnp.float32),
            like(far.shape, jnp.float32),
            like((rank, rank), jnp.float32),
        ),
        scratch_shapes=[
            pltpu.VMEM((rank * count, 2 * rank), jnp.float32),
            pltpu.VMEM((rank, 2 * rank), jnp.float32),
            pltpu.VMEM((count + 1, rank, rank), jnp.float32),
            pltpu.VMEM((count + 1, rank, rank), jnp.float32),
            pltpu.VMEM((count + 1, rank, rank), jnp.float32),
        ],
        compiler_params=pltpu.CompilerParams(vmem_limit_bytes=32 * 1024 * 1024),
        name="leaf_level",
    )(far)


def group_level(factors, scaled):
    rank = factors.shape[1]
    return pl.pallas_call(
        group_kernel,
        out_shape=jax.ShapeDtypeStruct(scaled.shape, jnp.float32),
        scratch_shapes=[
            pltpu.VMEM((rank, 2 * rank), jnp.float32),
            pltpu.VMEM((rank, rank), jnp.float32),
        ],
        compiler_params=pltpu.CompilerParams(vmem_limit_bytes=32 * 1024 * 1024),
        name="group_level",
    )(factors, scaled)


def shift_table():
    offset_index = jnp.arange(27, dtype=jnp.int32)
    offset_steps = jnp.stack([offset_index // 9, offset_index // 3 % 3, offset_index % 3], axis=1)
    return (1 - offset_steps).astype(jnp.float32)


def kernel_tiles(own_offsets, near_offsets, shifts):
    separation = (
        shifts[None, :, :, None, None]
        + own_offsets[:, None, :, :, None]
        - near_offsets[:, :, :, None, :]
    )
    square = jnp.sum(separation * separation, axis=2)
    softened = square + EPSILON * EPSILON
    inverse = 1.0 / (softened * jnp.sqrt(softened))
    diagonal = (square + 2.0 * EPSILON * EPSILON) * inverse
    identity = jnp.eye(3, dtype=jnp.float32)
    kernel_block = (
        separation[:, :, :, None] * separation[:, :, None, :] * inverse[:, :, None, None]
        + identity[None, None, :, :, None, None] * diagonal[:, :, None, None]
    )
    return kernel_block.astype(jnp.bfloat16)


def body(sketch, test_matrix, offsets, near):
    leaf_side = sketch.shape[0]
    basis_rank = sketch.shape[3]
    leaf_rows = sketch.shape[4]
    node_count = offsets.shape[4]
    leaf_count = leaf_side * leaf_side * leaf_side
    packed = jnp.concatenate(
        [
            test_matrix.reshape(leaf_side, leaf_side, leaf_side, basis_rank * leaf_rows),
            offsets.reshape(leaf_side, leaf_side, leaf_side, 3 * node_count),
        ],
        axis=3,
    )
    column = with_halo(packed, (("gz", 2),), 1)
    extended = with_halo(column, (("gx", 0), ("gy", 1)), 1)
    packed_width = packed.shape[3]
    sample_width = basis_rank * leaf_rows
    shifts = shift_table()
    flat_sketch = sketch.reshape(leaf_count, basis_rank, leaf_rows)
    flat_offsets = offsets.reshape(leaf_count, 3, node_count).astype(jnp.float32)
    flat_near = near.reshape(leaf_count, 27).astype(jnp.bfloat16)

    def correct(leaf_index):
        corner_x = leaf_index // (leaf_side * leaf_side)
        corner_y = leaf_index // leaf_side % leaf_side
        corner_z = leaf_index % leaf_side
        zero = jnp.zeros((), jnp.int32)
        own_offsets = flat_offsets[leaf_index][None]
        near_mask = flat_near[leaf_index]
        correction = jnp.zeros((basis_rank, 3, node_count), jnp.float32)
        for slab in range(3):
            neighbours = lax.dynamic_slice(
                extended, (corner_x + slab, corner_y, corner_z, zero), (1, 3, 3, packed_width)
            ).reshape(9, packed_width)
            sampled = neighbours[:, :sample_width].reshape(9, basis_rank, 3, node_count)
            sampled = sampled * near_mask[slab * 9 : slab * 9 + 9][:, None, None, None]
            near_offsets = (
                neighbours[:, sample_width:].reshape(9, 3, node_count).astype(jnp.float32)
            )
            kernel_block = kernel_tiles(
                own_offsets, near_offsets[None], shifts[slab * 9 : slab * 9 + 9]
            )[0]
            correction = correction + jnp.einsum(
                "kpqij,kcqj->cpi", kernel_block, sampled, preferred_element_type=jnp.float32
            )
        return flat_sketch[leaf_index] - correction.reshape(basis_rank, leaf_rows)

    far_field = lax.map(correct, jnp.arange(leaf_count, dtype=jnp.int32))
    leaf_t, level_t, scaled, factor = leaf_level(far_field)
    grouped = factor[None]
    for axis in ("gz", "gy", "gx"):
        grouped = jnp.concatenate([grouped, from_partner(grouped, axis, 0)], axis=0)
    nested = group_level(grouped, scaled)
    leaf_shape = (leaf_side, leaf_side, leaf_side, basis_rank, leaf_rows)
    return (leaf_t.reshape(leaf_shape), level_t[None, None, None], nested.reshape(leaf_shape))


def solution(mesh):
    placed = (
        P("gx", "gy", "gz", None, None),
        P("gx", "gy", "gz", None, None),
        P("gx", "gy", "gz", None, None),
        P("gx", "gy", "gz", None),
    )
    return jax.shard_map(
        body,
        mesh=mesh,
        in_specs=placed,
        out_specs=(
            P("gx", "gy", "gz", None, None),
            P("gx", "gy", "gz", None, None),
            P("gx", "gy", "gz", None, None),
        ),
        check_vma=False,
    )
```

```python
import functools
import math

import jax
import jax.numpy as jnp
from jax import lax
from jax.experimental import pallas as pl
from jax.experimental.pallas import tpu as pltpu
from jax.sharding import PartitionSpec as P

EPSILON = 0.1
GROUP = 8
SIDE = 2
HIGHEST = lax.Precision.HIGHEST


def from_partner(x, axis, distance):
    return lax.ppermute(x, axis, [(i, i ^ 1 << distance) for i in range(lax.axis_size(axis))])


SMALL = 0.2


def matmul(a, b, precision=HIGHEST):
    return lax.dot_general(
        a, b, (((1,), (0,)), ((), ())), precision=precision, preferred_element_type=jnp.float32
    )


def matmul_t(a, b, precision=HIGHEST):
    return lax.dot_general(
        a, b, (((1,), (1,)), ((), ())), precision=precision, preferred_element_type=jnp.float32
    )


def halves(x):
    high = x.astype(jnp.bfloat16)
    return high, (x - high.astype(jnp.float32)).astype(jnp.bfloat16)


def positions(shape):
    return (
        lax.broadcasted_iota(jnp.int32, shape, 0),
        lax.broadcasted_iota(jnp.int32, shape, 1),
    )


def unit(rank):
    row, column = positions((rank, rank))
    return jnp.where(row == column, 1.0, 0.0).astype(jnp.float32)


def upper(x):
    row, column = positions(x.shape)
    return jnp.where(row <= column, x, 0.0)


def half_lower(x):
    row, column = positions(x.shape)
    return jnp.where(row > column, x, jnp.where(row == column, 0.5 * x, 0.0))


def excess_of(x):
    rank = x.shape[0]
    stacked = jnp.concatenate(halves(x), axis=0)
    products = matmul_t(stacked, stacked, None)
    crossed = products[:rank, rank:] + products[rank:, :rank]
    return products[:rank, :rank] + crossed


def near_unit_factor(excess):
    x = half_lower(excess)
    for _ in range(2):
        x = half_lower(excess - matmul_t(x, x, None))
    square = matmul(x, x, None)
    return x, x - square + matmul(square, x, None)


def batch_steps(work, rank, batch, width):
    shape = (batch, 2 * rank)

    def lane(values, index):
        return jnp.broadcast_to(values[:, rank + index : rank + index + 1], shape)

    for start in range(0, rank, width):
        rows = [work[(start + i) * batch : (start + i + 1) * batch, :] for i in range(width)]
        scalars = [
            [lane(rows[i], start + j) if j >= i else None for j in range(width)]
            for i in range(width)
        ]
        for j in range(width):
            root = lax.rsqrt(scalars[j][j])
            rows[j] = rows[j] * root
            factor = [None if i <= j else scalars[j][i] * root for i in range(width)]
            for i in range(j + 1, width):
                rows[i] = rows[i] - factor[i] * rows[j]
                for k in range(i, width):
                    scalars[i][k] = scalars[i][k] - factor[i] * factor[k]
            work[(start + j) * batch : (start + j + 1) * batch, :] = rows[j]
        for lower in range(start + width, rank):
            total = work[lower * batch : (lower + 1) * batch, :]
            for j in range(width):
                total = total - lane(rows[j], lower) * rows[j]
            work[lower * batch : (lower + 1) * batch, :] = total
        yield


def single_steps(work, rank):
    shape = (8, 2 * rank)
    row, _ = positions(shape)
    for start in range(0, rank, 8):
        z = work[start : start + 8, :]
        columns = [
            jnp.broadcast_to(z[:, rank + start + j : rank + start + j + 1], shape)
            for j in range(8)
        ]
        done = z
        for j in range(8):
            root = lax.rsqrt(columns[j][j : j + 1, :])
            scaled = z[j : j + 1, :] * root
            done = jnp.where(row == j, scaled, done)
            if j < 7:
                factor = columns[j] * root
                z = z - factor * scaled
                for i in range(j + 1, 8):
                    columns[i] = columns[i] - factor * (columns[i][j : j + 1, :] * root)
        work[start : start + 8, :] = done
        turned = done.T
        for lower in range(start + 8, rank, 8):
            total = work[lower : lower + 8, :]
            factors = turned[rank + lower : rank + lower + 8, :]
            for j in range(8):
                total = total - jnp.broadcast_to(factors[:, j : j + 1], shape) * done[j : j + 1, :]
            work[lower : lower + 8, :] = total
        yield


def run_together(*steps):
    for _ in zip(*steps):
        pass


def shifted(x, axis, step):
    size = lax.axis_size(axis)
    return lax.ppermute(x, axis, [(i, i + step) for i in range(size) if 0 <= i + step < size])


def leaf_index(x, y, z):
    return (x * SIDE + y) * SIDE + z


def planes_of(gz_size):
    return {0: 0, 1: 1, -1: 2, 2: 2 if gz_size == 2 else 3}


def pair_tables(gz_size):
    planes = planes_of(gz_size)
    depth = max(planes.values()) + 1
    stages = ([], [], [])
    for a in range(SIDE**3):
        place = (a // 4, a // 2 % 2, a % 2)
        for k in range(27):
            x, y, z = (p + d for p, d in zip(place, (k // 9 - 1, k // 3 % 3 - 1, k % 3 - 1)))
            sides = tuple((axis, t) for axis, t in enumerate((x, y, z)) if t in (-1, 2))
            if x in (-1, 2):
                first = 0 if x == -1 else 4 * depth
                stages[2].append((a, k, first + (y + 1) * depth + planes[z], sides))
            elif y in (-1, 2):
                first = 4 * (depth - 2) + (0 if y == -1 else 2 * depth)
                stages[1].append((a, k, first + x * depth + planes[z], sides))
            elif z in (-1, 2):
                first = 4 * (planes[z] - 2)
                stages[1].append((a, k, first + x * 2 + y, sides))
            else:
                stages[0].append((a, k, leaf_index(x, y, z), sides))
    return stages


def side_flags():
    flags = {}
    for axis, name in enumerate(("gx", "gy", "gz")):
        place = lax.axis_index(name)
        flags[axis, -1] = (place > 0).astype(jnp.int32)
        flags[axis, 2] = (place < lax.axis_size(name) - 1).astype(jnp.int32)
    return flags


def list_pairs(pairs, near, listed, blank):
    flags = side_flags()
    joint = {(): None}
    count = jnp.int32(0)
    for a, k, source, sides in pairs:
        if sides not in joint:
            product = flags[sides[0]]
            for side in sides[1:]:
                product = product * flags[side]
            joint[sides] = product
        listed[count] = jnp.int32((source * 8 + a) * 27 + k)
        taken = near[a * 27 + k]
        if sides:
            taken = taken * joint[sides]
        count = count + taken
    for i in range(GROUP):
        listed[count + i] = jnp.int32(blank * 8 * 27 + 13)
    return lax.div(count + (GROUP - 1), jnp.int32(GROUP))


def spread_offsets(blocks, count, turned, spread):
    rank3 = blocks.shape[1] - 16
    turned[...] = jnp.zeros_like(turned)
    for s in range(count):
        turned[4 * s : 4 * s + 4, :] = blocks[s, rank3:, :].astype(jnp.float32)[:4]
    columns = turned[...].T.astype(jnp.bfloat16)
    row, lane = positions((128, 384))
    for s in range(count):
        chosen = jnp.where(row == 4 * s + lane // 128, 1.0, 0.0).astype(jnp.bfloat16)
        values = matmul(columns, chosen, None)
        for p in range(3):
            spread[s, p] = values[:, 128 * p : 128 * (p + 1)]


def tile_rows(own, spread, rows):
    r = [own[p] - spread[p, rows, :] for p in range(3)]
    squares = [v * v for v in r]
    softened = squares[0] + squares[1] + squares[2] + EPSILON * EPSILON
    lifted = softened + EPSILON * EPSILON
    root = lax.rsqrt(softened)
    h = root * root * root
    ry, rz = r[1] * h, r[2] * h
    tiles = {(p, p): (squares[p] + lifted) * h for p in range(3)}
    tiles[0, 1], tiles[0, 2], tiles[1, 2] = r[0] * ry, r[0] * rz, r[1] * rz
    return {pq: tile.astype(jnp.bfloat16) for pq, tile in tiles.items()}


def add_pairs(groups, listed, blocks, own, spread, total):
    chunk = 16

    @pl.loop(0, groups)
    def _(group):
        for u in range(GROUP):
            code = listed[group * GROUP + u]
            pair = lax.div(code, jnp.int32(27))
            k = code - pair * 27
            source = lax.shift_right_logical(pair, jnp.int32(3))
            a = lax.bitwise_and(pair, jnp.int32(7))
            dx = lax.div(k, jnp.int32(9))
            dy = lax.div(k, jnp.int32(3)) - dx * 3
            dz = k - dx * 9 - dy * 3
            own_rows = own[a]
            placed = [
                jnp.broadcast_to(
                    own_rows[p : p + 1] + (1 - step).astype(jnp.float32), (chunk, 128)
                )
                for p, step in enumerate((dx, dy, dz))
            ]
            parts = [
                tile_rows(placed, spread.at[source], pl.ds(j, chunk))
                for j in range(0, 128, chunk)
            ]
            tiles = {
                pq: jnp.concatenate([part[pq] for part in parts], axis=0) for pq in parts[0]
            }
            matrix = jnp.concatenate(
                [
                    jnp.concatenate([tiles[min(p, q), max(p, q)] for p in range(3)], axis=1)
                    for q in range(3)
                ],
                axis=0,
            )
            rank = total.shape[1]
            sampled = jnp.concatenate(
                [blocks[source, q * rank : (q + 1) * rank, :] for q in range(3)], axis=1
            )
            total[a] += matmul(sampled, matrix, None)


def fetch(parts, blocks, semaphore):
    copies = []
    first = 0
    for i, part in enumerate(parts):
        copies.append(
            pltpu.make_async_copy(
                part, blocks.at[pl.ds(first, part.shape[0])], semaphore.at[i]
            )
        )
        copies[-1].start()
        first += part.shape[0]
    return copies, first


def near_stage(pairs, near, own, parts, total, listed, blocks, turned, spread, semaphore):
    copies, count = fetch(parts, blocks, semaphore)
    groups = list_pairs(pairs, near, listed, count)
    blocks[count] = jnp.zeros_like(blocks[count])
    for copy in copies:
        copy.wait()
    spread_offsets(blocks, count, turned, spread)
    spread[count] = jnp.zeros_like(spread[count])
    add_pairs(groups, listed, blocks, own, spread, total)


def first_kernel(pairs, near, own, own_blocks, total, *scratch):
    total[...] = jnp.zeros_like(total)
    near_stage(pairs, near, own, [own_blocks], total, *scratch)


def second_kernel(pairs, near, own, before, *rest):
    *parts, total, listed, blocks, turned, spread, semaphore = rest
    total[...] = before[...]
    near_stage(pairs, near, own, parts, total, listed, blocks, turned, spread, semaphore)


def third_kernel(pairs, near, own, before, sketch, low, high, *rest):
    outs, scratch = rest[:4], rest[4:]
    total, near_scratch, leaf_scratch = scratch[0], scratch[1:6], scratch[6:]
    total[...] = before[...]
    near_stage(pairs, near, own, [low, high], total, *near_scratch)
    total[...] = sketch[...] - total[...]
    leaf_kernel(total, *outs, *leaf_scratch)


def pack_kernel(samples, offsets, packed, own, *faces):
    count, rank, leaf_rows = samples.shape
    filler = jnp.zeros((13, 128), jnp.float32)
    for a in range(count):
        for q in range(3):
            packed[a, q * rank : (q + 1) * rank, :] = samples[a, :, q * 128 : (q + 1) * 128]
        rows = jnp.concatenate([offsets[a].astype(jnp.float32), filler], axis=0)
        packed[a, 3 * rank :, :] = rows.astype(jnp.bfloat16)
        own[a] = rows[:8]
    if len(faces) == 1:
        planes = [1 - lax.axis_index("gz")]
    else:
        planes = [1, 0]
    for face, plane in zip(faces, planes):
        for column in range(SIDE * SIDE):
            face[column] = packed[column * SIDE + plane]


VMEM_LIMIT = 48 * 1024 * 1024


def near_scratch(pairs, count, block):
    return [
        pltpu.SMEM((len(pairs) + GROUP + 1,), jnp.int32),
        pltpu.VMEM((count + 1,) + block, jnp.bfloat16),
        pltpu.VMEM((128, 128), jnp.float32),
        pltpu.VMEM((count + 1, 3, 128, 128), jnp.float32),
        pltpu.SemaphoreType.DMA((4,)),
    ]


def near_cost(pairs, rank):
    return pl.CostEstimate(
        flops=len(pairs) * 2 * rank * 384 * 384 * 8, bytes_accessed=4 * 1024 * 1024, transcendentals=0
    )


IN_SMEM = pl.BlockSpec(memory_space=pltpu.SMEM)
IN_VMEM = pl.BlockSpec(memory_space=pltpu.VMEM)
ANYWHERE = pl.BlockSpec(memory_space=pl.ANY)


def leaf_kernel(far, leaf_out, level_out, scaled_out, factor_out, work, single, es, xs, zs):
    count, rank, leaf_rows = far.shape
    eye = unit(rank)
    zeros = jnp.zeros((rank, leaf_rows), jnp.float32)
    left_unit = jnp.concatenate([eye, jnp.zeros_like(eye)], axis=1)
    total = left_unit
    for a in range(count):
        rows = far[a]
        gram = matmul_t(rows, jnp.concatenate([zeros, rows], axis=0))
        work[pl.ds(a, rank, stride=count), :] = left_unit + gram
        total = total + gram
    single[...] = total
    run_together(batch_steps(work, rank, count, 8), single_steps(single, rank))
    box_inverse = single[:, :rank]
    box_upper = upper(single[:, rank:])
    box_excess = -eye
    largest = jnp.zeros((1, 1), jnp.float32)
    for a in range(count):
        inverse = work[pl.ds(a, rank, stride=count), :][:, :rank]
        both = matmul(jnp.concatenate([inverse, box_inverse], axis=0), far[a])
        leaf_out[a] = both[:rank]
        scaled_out[a] = both[rank:]
        excess = excess_of(both[:rank]) - eye
        box_excess = box_excess + excess_of(both[rank:])
        xs[a], zs[a] = near_unit_factor(excess)
        es[a] = excess
        largest = jnp.maximum(largest, jnp.sum(excess * excess, keepdims=True))
    xs[count], zs[count] = near_unit_factor(box_excess)
    largest = jnp.maximum(largest, jnp.sum(box_excess * box_excess, keepdims=True))
    es[count] = box_excess
    uppers = [upper(work[pl.ds(a, rank, stride=count), :][:, rank:]) for a in range(count)]

    @pl.when(jnp.logical_not(largest[0, 0] <= SMALL * SMALL))
    def _():
        for a in range(count):
            work[pl.ds(a, rank, stride=count), :] = jnp.concatenate([eye, eye + es[a]], axis=1)
        single[...] = jnp.concatenate([eye, eye + es[count]], axis=1)
        run_together(batch_steps(work, rank, count, 8), single_steps(single, rank))
        for a in range(count + 1):
            rows = single[...] if a == count else work[pl.ds(a, rank, stride=count), :]
            xs[a] = upper(rows[:, rank:]).T - eye
            zs[a] = eye - rows[:, :rank]

    box_x, box_z = xs[count], zs[count]
    lower_box = box_upper.T
    factor_out[...] = lower_box + matmul(lower_box, box_x)
    for a in range(count):
        basis = leaf_out[a]
        leaf_out[a] = (basis - matmul(zs[a], basis)) * math.sqrt(leaf_rows)
        scaled = scaled_out[a]
        scaled_out[a] = scaled - matmul(box_z, scaled)
        block = matmul_t(box_inverse, uppers[a])
        block = block + matmul(block, xs[a])
        block = block - matmul(box_z, block)
        level_out[:, a * rank : (a + 1) * rank] = block * math.sqrt(count * rank)


def group_kernel(factors, scaled, nested_out, single, z_out):
    count, rank, _ = factors.shape
    eye = unit(rank)
    gram = jnp.zeros((rank, rank), jnp.float32)
    for b in range(count):
        gram = gram + matmul_t(factors[b], factors[b])
    single[...] = jnp.concatenate([eye, gram], axis=1)
    run_together(single_steps(single, rank))
    inverse = single[:, :rank]
    excess = -eye
    for b in range(count):
        block = matmul(inverse, factors[b])
        if b == 0:
            own = block
        excess = excess + excess_of(block)
    _, z_out[...] = near_unit_factor(excess)
    largest = jnp.sum(excess * excess, keepdims=True)

    @pl.when(jnp.logical_not(largest[0, 0] <= SMALL * SMALL))
    def _():
        single[...] = jnp.concatenate([eye, eye + excess], axis=1)
        run_together(single_steps(single, rank))
        z_out[...] = eye - single[:, :rank]

    z = z_out[...]
    mixing = (own - matmul(z, own)) * (8.0 * math.sqrt(scaled.shape[2]))
    for a in range(scaled.shape[0]):
        nested_out[a] = matmul(mixing, scaled[a])


def leaf_scratch(count, rank):
    square = pltpu.VMEM((count + 1, rank, rank), jnp.float32)
    return [
        pltpu.VMEM((rank * count, 2 * rank), jnp.float32),
        pltpu.VMEM((rank, 2 * rank), jnp.float32),
        square,
        square,
        square,
    ]


def join(parts, axis):
    return jnp.concatenate(parts, axis=axis)


def group_level(factors, scaled):
    rank = factors.shape[1]
    return pl.pallas_call(
        group_kernel,
        out_shape=jax.ShapeDtypeStruct(scaled.shape, jnp.float32),
        scratch_shapes=[
            pltpu.VMEM((rank, 2 * rank), jnp.float32),
            pltpu.VMEM((rank, rank), jnp.float32),
        ],
        compiler_params=pltpu.CompilerParams(vmem_limit_bytes=32 * 1024 * 1024),
        name="group_level",
    )(factors, scaled)


def body(sketch, test_matrix, offsets, near):
    rank, leaf_rows = sketch.shape[3:]
    count = SIDE**3
    gz_size = lax.axis_size("gz")
    like = jax.ShapeDtypeStruct
    block = (3 * rank + 16, 128)
    params = pltpu.CompilerParams(vmem_limit_bytes=VMEM_LIMIT)
    flat_near = near.reshape(count * 27)
    flat_sketch = sketch.reshape(count, rank, leaf_rows)
    stages = pair_tables(gz_size)
    faces = 1 if gz_size == 2 else 2
    packed, own, *sent = pl.pallas_call(
        pack_kernel,
        out_shape=(
            like((count,) + block, jnp.bfloat16),
            like((count, 8, 128), jnp.float32),
        )
        + (like((SIDE * SIDE,) + block, jnp.bfloat16),) * faces,
        compiler_params=params,
        name="pack",
    )(test_matrix.reshape(count, rank, leaf_rows), offsets.reshape(count, 3, 128))
    if faces == 1:
        z_halos = [from_partner(sent[0], "gz", 0)]
    else:
        z_halos = [shifted(sent[0], "gz", 1), shifted(sent[1], "gz", -1)]
    inner = packed.reshape((SIDE, SIDE, SIDE) + block)
    columns = [h.reshape((SIDE, SIDE, 1) + block) for h in z_halos]
    extended = join([inner] + columns, 2)
    depth = extended.shape[2]
    y_low = shifted(extended[:, 1], "gy", 1)
    y_high = shifted(extended[:, 0], "gy", -1)
    wide = join([y_low[:, None], extended, y_high[:, None]], 1)
    x_low = shifted(wide[1], "gx", 1)
    x_high = shifted(wide[0], "gx", -1)

    total = pl.pallas_call(
        functools.partial(first_kernel, stages[0]),
        out_shape=like((count, rank, leaf_rows), jnp.float32),
        in_specs=[IN_SMEM, IN_VMEM, ANYWHERE],
        scratch_shapes=near_scratch(stages[0], count, block),
        cost_estimate=near_cost(stages[0], rank),
        compiler_params=params,
        name="near_inner",
    )(flat_near, own, packed)
    flat = lambda x: x.reshape((-1,) + block)
    parts = [flat(h) for h in z_halos] + [flat(y_low), flat(y_high)]
    total = pl.pallas_call(
        functools.partial(second_kernel, stages[1]),
        out_shape=like((count, rank, leaf_rows), jnp.float32),
        in_specs=[IN_SMEM, IN_VMEM, IN_VMEM] + [ANYWHERE] * len(parts),
        scratch_shapes=near_scratch(stages[1], 4 * faces + 4 * depth, block),
        cost_estimate=near_cost(stages[1], rank),
        compiler_params=params,
        name="near_columns",
    )(flat_near, own, total, *parts)
    leaf_t, level_t, scaled, factor = pl.pallas_call(
        functools.partial(third_kernel, stages[2]),
        out_shape=(
            like((count, rank, leaf_rows), jnp.float32),
            like((rank, count * rank), jnp.float32),
            like((count, rank, leaf_rows), jnp.float32),
            like((rank, rank), jnp.float32),
        ),
        in_specs=[IN_SMEM, IN_VMEM, IN_VMEM, IN_VMEM] + [ANYWHERE] * 2,
        scratch_shapes=[pltpu.VMEM((count, rank, leaf_rows), jnp.float32)]
        + near_scratch(stages[2], 8 * depth, block)
        + leaf_scratch(count, rank),
        compiler_params=params,
        name="near_sides_and_leaf_level",
    )(flat_near, own, total, flat_sketch, flat(x_low), flat(x_high))
    grouped = factor[None]
    for axis in ("gz", "gy", "gx"):
        grouped = jnp.concatenate([grouped, from_partner(grouped, axis, 0)], axis=0)
    nested = group_level(grouped, scaled)
    return (leaf_t.reshape(sketch.shape), level_t[None, None, None], nested.reshape(sketch.shape))


def solution(mesh):
    placed = (
        P("gx", "gy", "gz", None, None),
        P("gx", "gy", "gz", None, None),
        P("gx", "gy", "gz", None, None),
        P("gx", "gy", "gz", None),
    )
    return jax.shard_map(
        body,
        mesh=mesh,
        in_specs=placed,
        out_specs=(
            P("gx", "gy", "gz", None, None),
            P("gx", "gy", "gz", None, None),
            P("gx", "gy", "gz", None, None),
        ),
        check_vma=False,
    )
```

```python
import functools
import math

import jax
import jax.numpy as jnp
from jax import lax
from jax.experimental import pallas as pl
from jax.experimental.pallas import tpu as pltpu
from jax.sharding import PartitionSpec as P

EPSILON = 0.1
GROUP = 8
SIDE = 2
HIGHEST = lax.Precision.HIGHEST


def from_partner(x, axis, distance):
    return lax.ppermute(x, axis, [(i, i ^ 1 << distance) for i in range(lax.axis_size(axis))])


SMALL = 0.06


def matmul(a, b, precision=HIGHEST):
    return lax.dot_general(
        a, b, (((1,), (0,)), ((), ())), precision=precision, preferred_element_type=jnp.float32
    )


def matmul_t(a, b, precision=HIGHEST):
    return lax.dot_general(
        a, b, (((1,), (1,)), ((), ())), precision=precision, preferred_element_type=jnp.float32
    )


def join(parts, axis):
    return jnp.concatenate(parts, axis=axis)


def halves(x):
    high = x.astype(jnp.bfloat16)
    return high, (x - high.astype(jnp.float32)).astype(jnp.bfloat16)


def thirds(x):
    high = x.astype(jnp.bfloat16)
    rest = x - high.astype(jnp.float32)
    return (high,) + halves(rest)


def positions(shape):
    return (
        lax.broadcasted_iota(jnp.int32, shape, 0),
        lax.broadcasted_iota(jnp.int32, shape, 1),
    )


def unit(rank):
    row, column = positions((rank, rank))
    return jnp.where(row == column, 1.0, 0.0).astype(jnp.float32)


def upper(x):
    row, column = positions(x.shape)
    return jnp.where(row <= column, x, 0.0)


def half_lower(x):
    row, column = positions(x.shape)
    return jnp.where(row > column, x, jnp.where(row == column, 0.5 * x, 0.0))


def gram_of(parts):
    f, g, h = parts
    return matmul_t(join([f, f, g, g, f, h], 1), join([f, g, f, g, h, f], 1), None)


def right_side(parts):
    f, g, h = parts
    return join([f, f, g, g, h, f], 0)


def left_side(x):
    f, g, h = thirds(x)
    first = join([f, g], 1)
    return join([first, first, join([f, h], 1)], 1)


def near_gram(x, y):
    f, g = halves(x)
    u, v = halves(y)
    return matmul_t(join([f, f, g], 1), join([u, v, u], 1), None)


def near_unit_factor(excess):
    x = half_lower(excess)
    square = matmul(x, x, None)
    x = half_lower(excess - matmul_t(x, x, None))
    return x, x - square


def not_small(norm):
    return jnp.logical_not(norm[0, 0] <= SMALL * SMALL)


def batch_rows(work, rank, batch, low, high, width=8):
    shape = (batch, 2 * rank)

    def lane(values, index):
        return jnp.broadcast_to(values[:, rank + index : rank + index + 1], shape)

    for start in range(low, high, width):
        rows = [work[(start + i) * batch : (start + i + 1) * batch, :] for i in range(width)]
        scalars = [
            [lane(rows[i], start + j) if j >= i else None for j in range(width)]
            for i in range(width)
        ]
        for j in range(width):
            root = lax.rsqrt(scalars[j][j])
            rows[j] = rows[j] * root
            factor = [None if i <= j else scalars[j][i] * root for i in range(width)]
            for i in range(j + 1, width):
                rows[i] = rows[i] - factor[i] * rows[j]
                for k in range(i, width):
                    scalars[i][k] = scalars[i][k] - factor[i] * factor[k]
            work[(start + j) * batch : (start + j + 1) * batch, :] = rows[j]
        for lower in range(start + width, high):
            total = work[lower * batch : (lower + 1) * batch, :]
            for j in range(width):
                total = total - lane(rows[j], lower) * rows[j]
            work[lower * batch : (lower + 1) * batch, :] = total


def batch_update(work, rank, batch, low, high):
    size = high - low
    each = 128 // size
    row, column = positions((128, 128))
    for first in range(0, batch, each):
        done = join(
            [work[pl.ds(low * batch + first + i, size, stride=batch), :] for i in range(each)], 0
        )
        turned = done.T
        right = right_side(thirds(done))
        for top in range(high, rank, size):
            factor = join([turned[rank + top : rank + top + size, :]] * each, 0)
            f, g, h = thirds(jnp.where(row // size == column // size, factor, 0.0))
            change = matmul(join([f, g, f, g, f, h], 1), right, None)
            for i in range(each):
                place = pl.ds(top * batch + first + i, size, stride=batch)
                work[place, :] = work[place, :] - change[i * size : (i + 1) * size]


def eliminate_batch(work, rank, batch):
    half = rank // 2
    batch_rows(work, rank, batch, 0, half)
    batch_update(work, rank, batch, 0, half)
    batch_rows(work, rank, batch, half, rank)


def eliminate_single(work, rank):
    shape = (8, 2 * rank)
    row, _ = positions(shape)
    for start in range(0, rank, 8):
        blocks = {m: work[m : m + 8, :] for m in range(start, rank, 8)}
        columns = {
            m: [
                jnp.broadcast_to(blocks[m][:, rank + start + j : rank + start + j + 1], shape)
                for j in range(8)
            ]
            for m in blocks
        }
        done = blocks[start]
        for j in range(8):
            root = lax.rsqrt(columns[start][j][j : j + 1, :])
            line = [columns[start][i][j : j + 1, :] * root for i in range(8)]
            scaled = blocks[start][j : j + 1, :] * root
            done = jnp.where(row == j, scaled, done)
            for m in blocks:
                factor = columns[m][j] * root
                blocks[m] = blocks[m] - factor * scaled
                for i in range(j + 1, 8):
                    columns[m][i] = columns[m][i] - factor * line[i]
        work[start : start + 8, :] = done
        for m in blocks:
            if m > start:
                work[m : m + 8, :] = blocks[m]


def parity(axis):
    return lax.axis_index(axis) % 2


def to_neighbours(low, high, axis):
    size = lax.axis_size(axis)
    even = parity(axis) == 0
    pairs = [(i, i ^ 1) for i in range(size)]
    received = [lax.ppermute(jnp.where(even, high, low), axis, pairs)]
    if size > 2:
        across = [(i, i + 1) for i in range(1, size - 1, 2)]
        across = across + [(j, i) for i, j in across]
        received.insert(0, lax.ppermute(jnp.where(even, low, high), axis, across))
    return received[::-1]


def halo_count(axis):
    return 1 if lax.axis_size(axis) == 2 else 2


def leaf_index(x, y, z):
    return (x * SIDE + y) * SIDE + z


def pair_tables(halos):
    depth = SIDE + halos[2]
    stages = ([], [], [])
    for a in range(SIDE**3):
        place = (a // 4, a // 2 % 2, a % 2)
        for k in range(27):
            at = [p + d for p, d in zip(place, (k // 9 - 1, k // 3 % 3 - 1, k % 3 - 1))]
            sides = tuple((axis, t) for axis, t in enumerate(at) if t in (-1, 2))
            x, y, z = (2 if t == -1 else t for t in at)
            if x == 2:
                stages[2].append((a, k, y * depth + z, sides))
            elif y == 2:
                stages[1].append((a, k, 4 * halos[2] + x * depth + z, sides))
            elif z == 2:
                stages[1].append((a, k, x * SIDE + y, sides))
            else:
                stages[0].append((a, k, leaf_index(x, y, z), sides))
    return stages


def far_sides(halos):
    found = {}
    for axis, name in enumerate(("gx", "gy", "gz")):
        place = lax.axis_index(name)
        odd = place % 2
        other = halos[axis] - 1
        found[axis, -1] = ((place > 0).astype(jnp.int32), (1 - odd) * other)
        found[axis, 2] = ((place < lax.axis_size(name) - 1).astype(jnp.int32), odd * other)
    return found


def list_pairs(pairs, halos, near, listed, blank):
    found = far_sides(halos)
    depth = SIDE + halos[2]
    wide = SIDE + halos[1]
    joint = {}
    count = jnp.int32(0)
    for a, k, source, sides in pairs:
        if sides not in joint:
            inside, moved = jnp.int32(1), jnp.int32(0)
            first = min((axis for axis, _ in sides), default=None)
            steps = {
                0: {0: wide * depth, 1: depth, 2: 1},
                1: {1: SIDE * depth, 2: 1},
                2: {2: SIDE * SIDE},
            }
            for side in sides:
                inside = inside * found[side][0]
                moved = moved + found[side][1] * steps[first][side[0]]
            joint[sides] = (inside, moved * (8 * 27))
        code = jnp.int32((source * 8 + a) * 27 + k)
        taken = near[a * 27 + k]
        if sides:
            code = code + joint[sides][1]
            taken = taken * joint[sides][0]
        listed[count] = code
        count = count + taken
    for i in range(GROUP):
        listed[count + i] = jnp.int32(blank * 8 * 27 + 13)
    return lax.div(count + (GROUP - 1), jnp.int32(GROUP))


def spread_offsets(blocks, count, turned, spread):
    rank3 = blocks.shape[1] - 16
    turned[...] = jnp.zeros_like(turned)
    for s in range(count):
        turned[4 * s : 4 * s + 4, :] = blocks[s, rank3:, :].astype(jnp.float32)[:4]
    columns = turned[...].T.astype(jnp.bfloat16)
    row, lane = positions((128, 384))
    for s in range(count):
        chosen = jnp.where(row == 4 * s + lane // 128, 1.0, 0.0).astype(jnp.bfloat16)
        values = matmul(columns, chosen, None)
        for p in range(3):
            spread[s, p] = values[:, 128 * p : 128 * (p + 1)]


def tile_rows(own, spread, rows):
    r = [own[p] - spread[p, rows, :] for p in range(3)]
    squares = [v * v for v in r]
    softened = squares[0] + squares[1] + squares[2] + EPSILON * EPSILON
    lifted = softened + EPSILON * EPSILON
    root = lax.rsqrt(softened)
    h = root * root * root
    ry, rz = r[1] * h, r[2] * h
    tiles = {(p, p): (squares[p] + lifted) * h for p in range(3)}
    tiles[0, 1], tiles[0, 2], tiles[1, 2] = r[0] * ry, r[0] * rz, r[1] * rz
    return {pq: tile.astype(jnp.bfloat16) for pq, tile in tiles.items()}


def add_pairs(groups, listed, blocks, own, spread, total):
    chunk = 16

    @pl.loop(0, groups)
    def _(group):
        for u in range(GROUP):
            code = listed[group * GROUP + u]
            pair = lax.div(code, jnp.int32(27))
            k = code - pair * 27
            source = lax.shift_right_logical(pair, jnp.int32(3))
            a = lax.bitwise_and(pair, jnp.int32(7))
            dx = lax.div(k, jnp.int32(9))
            dy = lax.div(k, jnp.int32(3)) - dx * 3
            dz = k - dx * 9 - dy * 3
            own_rows = own[a]
            placed = [
                jnp.broadcast_to(
                    own_rows[p : p + 1] + (1 - step).astype(jnp.float32), (chunk, 128)
                )
                for p, step in enumerate((dx, dy, dz))
            ]
            parts = [
                tile_rows(placed, spread.at[source], pl.ds(j, chunk))
                for j in range(0, 128, chunk)
            ]
            tiles = {
                pq: jnp.concatenate([part[pq] for part in parts], axis=0) for pq in parts[0]
            }
            matrix = jnp.concatenate(
                [
                    jnp.concatenate([tiles[min(p, q), max(p, q)] for p in range(3)], axis=1)
                    for q in range(3)
                ],
                axis=0,
            )
            rank = total.shape[1]
            sampled = jnp.concatenate(
                [blocks[source, q * rank : (q + 1) * rank, :] for q in range(3)], axis=1
            )
            total[a] += matmul(sampled, matrix, None)


def fetch(parts, blocks, semaphore):
    copies = []
    first = 0
    for i, part in enumerate(parts):
        copies.append(
            pltpu.make_async_copy(
                part, blocks.at[pl.ds(first, part.shape[0])], semaphore.at[i]
            )
        )
        copies[-1].start()
        first += part.shape[0]
    return copies, first


def near_stage(pairs, halos, near, own, parts, total, listed, blocks, turned, spread, semaphore):
    copies, count = fetch(parts, blocks, semaphore)
    groups = list_pairs(pairs, halos, near, listed, count)
    blocks[count] = jnp.zeros_like(blocks[count])
    for copy in copies:
        copy.wait()
    spread_offsets(blocks, count, turned, spread)
    spread[count] = jnp.zeros_like(spread[count])
    add_pairs(groups, listed, blocks, own, spread, total)


def first_kernel(pairs, halos, near, own, own_blocks, total, *scratch):
    total[...] = jnp.zeros_like(total)
    near_stage(pairs, halos, near, own, [own_blocks], total, *scratch)


def second_kernel(pairs, halos, near, own, before, *rest):
    *parts, total, listed, blocks, turned, spread, semaphore = rest
    total[...] = before[...]
    near_stage(
        pairs, halos, near, own, parts, total, listed, blocks, turned, spread, semaphore
    )


def third_kernel(pairs, halos, near, own, before, sketch, *rest):
    parts, rest = rest[: halos[0]], rest[halos[0] :]
    far, *outs = rest[:5]
    listed, blocks, turned, spread, semaphore, single = rest[5:]
    far[...] = before[...]
    near_stage(
        pairs, halos, near, own, parts, far, listed, blocks, turned, spread, semaphore
    )
    far[...] = sketch[...] - far[...]
    box_level(far, *outs, single)


def pack_kernel(samples, offsets, packed, own, *faces):
    count, rank, leaf_rows = samples.shape
    filler = jnp.zeros((13, 128), jnp.float32)
    for a in range(count):
        for q in range(3):
            packed[a, q * rank : (q + 1) * rank, :] = samples[a, :, q * 128 : (q + 1) * 128]
        rows = jnp.concatenate([offsets[a].astype(jnp.float32), filler], axis=0)
        packed[a, 3 * rank :, :] = rows.astype(jnp.bfloat16)
        own[a] = rows[:8]
    planes = [1 - parity("gz"), parity("gz")]
    for face, plane in zip(faces, planes):
        for column in range(SIDE * SIDE):
            face[column] = packed[column * SIDE + plane]


VMEM_LIMIT = 48 * 1024 * 1024


def near_scratch(pairs, count, block):
    return [
        pltpu.SMEM((len(pairs) + GROUP + 1,), jnp.int32),
        pltpu.VMEM((count + 1,) + block, jnp.bfloat16),
        pltpu.VMEM((128, 128), jnp.float32),
        pltpu.VMEM((count + 1, 3, 128, 128), jnp.float32),
        pltpu.SemaphoreType.DMA((4,)),
    ]


def near_cost(pairs, rank):
    return pl.CostEstimate(
        flops=len(pairs) * 2 * rank * 384 * 384 * 8, bytes_accessed=4 * 1024 * 1024, transcendentals=0
    )


IN_SMEM = pl.BlockSpec(memory_space=pltpu.SMEM)
IN_VMEM = pl.BlockSpec(memory_space=pltpu.VMEM)
ANYWHERE = pl.BlockSpec(memory_space=pl.ANY)


def box_level(far, grams_out, factor_out, samples_out, z_out, single):
    count, rank, _ = far.shape
    eye = unit(rank)
    total = jnp.zeros_like(eye)
    for a in range(count):
        gram = gram_of(thirds(far[a]))
        grams_out[a] = gram
        total = total + gram
    single[...] = join([eye, 0.5 * (total + total.T)], 1)
    eliminate_single(single, rank)
    left = left_side(single[:, :rank])
    lower = upper(single[:, rank:]).T
    excess = -eye
    for a in range(count):
        samples = matmul(left, right_side(thirds(far[a])), None)
        samples_out[a] = samples
        excess = excess + near_gram(samples, samples)
    x, z_out[...] = near_unit_factor(excess)
    factor_out[...] = lower + matmul(lower, x)

    @pl.when(not_small(jnp.sum(excess * excess, keepdims=True)))
    def _():
        single[...] = join([eye, eye + excess], 1)
        eliminate_single(single, rank)
        factor_out[...] = matmul(lower, upper(single[:, rank:]).T)
        for a in range(count):
            samples_out[a] = matmul(single[:, :rank], samples_out[a])
        z_out[...] = jnp.zeros_like(eye)


def leaf_kernel(far, grams, samples, box_z, leaf_out, level_out, work, blocks, es, zs):
    count, rank, leaf_rows = far.shape
    eye = unit(rank)
    for a in range(count):
        work[pl.ds(a, rank, stride=count), :] = join([eye, grams[a]], 1)
    eliminate_batch(work, rank, count)
    largest = jnp.zeros((1, 1), jnp.float32)
    for a in range(count):
        inverse = work[pl.ds(a, rank, stride=count), :][:, :rank]
        basis = matmul(left_side(inverse), right_side(thirds(far[a])), None)
        leaf_out[a] = basis
        products = near_gram(join([basis, samples[a]], 0), basis)
        blocks[a] = products[rank:]
        excess = products[:rank] - eye
        es[a] = excess
        largest = jnp.maximum(largest, jnp.sum(excess * excess, keepdims=True))
    for a in range(count):
        zs[a] = near_unit_factor(es[a])[1]

    @pl.when(not_small(largest))
    def _():
        for a in range(count):
            work[pl.ds(a, rank, stride=count), :] = join([eye, eye + es[a]], 1)
        eliminate_batch(work, rank, count)
        for a in range(count):
            inverse = work[pl.ds(a, rank, stride=count), :][:, :rank]
            leaf_out[a] = matmul(inverse, leaf_out[a])
            blocks[a] = matmul_t(blocks[a], inverse)
            zs[a] = jnp.zeros_like(eye)

    for a in range(count):
        basis = leaf_out[a]
        leaf_out[a] = (basis - matmul(zs[a], basis, None)) * math.sqrt(leaf_rows)
        block = blocks[a]
        blocks[a] = (block - matmul_t(block, zs[a], None)) * math.sqrt(count * rank)
    block = join([blocks[a] for a in range(count)], 1)
    level_out[...] = block - matmul(box_z[...], block, None)


def group_kernel(factors, samples, box_z, nested_out, single, stack):
    count, rank, _ = factors.shape
    eye = unit(rank)
    for b in range(count):
        stack[:, b * rank : (b + 1) * rank] = factors[b]
    parts = thirds(stack[...])
    gram = gram_of(parts)
    single[...] = join([eye, 0.5 * (gram + gram.T)], 1)
    eliminate_single(single, rank)
    block = matmul(left_side(single[:, :rank]), right_side(parts), None)
    excess = near_gram(block, block) - eye
    own = block[:, :rank] * (8.0 * math.sqrt(samples.shape[2]))
    mixing = own - matmul(near_unit_factor(excess)[1], own, None)
    mix_samples(mixing, samples, box_z, nested_out)

    @pl.when(not_small(jnp.sum(excess * excess, keepdims=True)))
    def _():
        single[...] = join([eye, eye + excess], 1)
        eliminate_single(single, rank)
        mix_samples(matmul(single[:, :rank], own), samples, box_z, nested_out)


def mix_samples(mixing, samples, box_z, nested_out):
    mixing = mixing - matmul(mixing, box_z[...], None)
    left = join(halves(mixing) * 2, 1)
    for a in range(samples.shape[0]):
        f, g = halves(samples[a])
        nested_out[a] = matmul(left, join([f, f, g, g], 0), None)


def body(sketch, test_matrix, offsets, near):
    rank, leaf_rows = sketch.shape[3:]
    count = SIDE**3
    halos = [halo_count(axis) for axis in ("gx", "gy", "gz")]
    like = jax.ShapeDtypeStruct
    block = (3 * rank + 16, 128)
    params = pltpu.CompilerParams(vmem_limit_bytes=VMEM_LIMIT)
    flat_near = near.reshape(count * 27)
    flat_sketch = sketch.reshape(count, rank, leaf_rows)
    stages = pair_tables(halos)
    faces = halos[2]
    packed, own, *sent = pl.pallas_call(
        pack_kernel,
        out_shape=(
            like((count,) + block, jnp.bfloat16),
            like((count, 8, 128), jnp.float32),
        )
        + (like((SIDE * SIDE,) + block, jnp.bfloat16),) * faces,
        compiler_params=params,
        name="pack",
    )(test_matrix.reshape(count, rank, leaf_rows), offsets.reshape(count, 3, 128))
    z_halos = [from_partner(sent[0], "gz", 0)]
    if faces == 2:
        size = lax.axis_size("gz")
        across = [(i, i + 1) for i in range(1, size - 1, 2)]
        across = across + [(j, i) for i, j in across]
        z_halos.append(lax.ppermute(sent[1], "gz", across))
    inner = packed.reshape((SIDE, SIDE, SIDE) + block)
    columns = [h.reshape((SIDE, SIDE, 1) + block) for h in z_halos]
    extended = join([inner] + columns, 2)
    depth = extended.shape[2]
    y_halos = to_neighbours(extended[:, 0], extended[:, 1], "gy")
    wide = join([extended] + [h[:, None] for h in y_halos], 1)
    x_halos = to_neighbours(wide[0], wide[1], "gx")

    total = pl.pallas_call(
        functools.partial(first_kernel, stages[0], halos),
        out_shape=like((count, rank, leaf_rows), jnp.float32),
        in_specs=[IN_SMEM, IN_VMEM, ANYWHERE],
        scratch_shapes=near_scratch(stages[0], count, block),
        cost_estimate=near_cost(stages[0], rank),
        compiler_params=params,
        name="near_inner",
    )(flat_near, own, packed)
    flat = lambda x: x.reshape((-1,) + block)
    parts = [flat(h) for h in z_halos + y_halos]
    total = pl.pallas_call(
        functools.partial(second_kernel, stages[1], halos),
        out_shape=like((count, rank, leaf_rows), jnp.float32),
        in_specs=[IN_SMEM, IN_VMEM, IN_VMEM] + [ANYWHERE] * len(parts),
        scratch_shapes=near_scratch(stages[1], 4 * faces + SIDE * depth * halos[1], block),
        cost_estimate=near_cost(stages[1], rank),
        compiler_params=params,
        name="near_columns",
    )(flat_near, own, total, *parts)
    whole = like((count, rank, leaf_rows), jnp.float32)
    squares = like((count, rank, rank), jnp.float32)
    square = like((rank, rank), jnp.float32)
    single_scratch = pltpu.VMEM((rank, 2 * rank), jnp.float32)
    far, grams, factor, samples, box_z = pl.pallas_call(
        functools.partial(third_kernel, stages[2], halos),
        out_shape=(whole, squares, square, whole, square),
        in_specs=[IN_SMEM, IN_VMEM, IN_VMEM, IN_VMEM] + [ANYWHERE] * halos[0],
        scratch_shapes=near_scratch(stages[2], halos[0] * (SIDE + halos[1]) * depth, block)
        + [single_scratch],
        compiler_params=params,
        name="near_sides_and_box_level",
    )(flat_near, own, total, flat_sketch, *[flat(h) for h in x_halos])
    grouped = factor[None]
    for axis in ("gz", "gy", "gx"):
        grouped = jnp.concatenate([grouped, from_partner(grouped, axis, 0)], axis=0)
    leaf_t, level_t = pl.pallas_call(
        leaf_kernel,
        out_shape=(whole, like((rank, count * rank), jnp.float32)),
        scratch_shapes=[pltpu.VMEM((rank * count, 2 * rank), jnp.float32)]
        + [pltpu.VMEM((count, rank, rank), jnp.float32)] * 3,
        cost_estimate=pl.CostEstimate(
            flops=8 * 1000 * 1000 * 1000, bytes_accessed=4 * 1024 * 1024, transcendentals=0
        ),
        compiler_params=params,
        name="leaf_level",
    )(far, grams, samples, box_z)
    nested = pl.pallas_call(
        group_kernel,
        out_shape=whole,
        scratch_shapes=[
            single_scratch,
            pltpu.VMEM((rank, count * rank), jnp.float32),
        ],
        compiler_params=params,
        name="group_level",
    )(grouped, samples, box_z)
    return (leaf_t.reshape(sketch.shape), level_t[None, None, None], nested.reshape(sketch.shape))


def solution(mesh):
    placed = (
        P("gx", "gy", "gz", None, None),
        P("gx", "gy", "gz", None, None),
        P("gx", "gy", "gz", None, None),
        P("gx", "gy", "gz", None),
    )
    return jax.shard_map(
        body,
        mesh=mesh,
        in_specs=placed,
        out_specs=(
            P("gx", "gy", "gz", None, None),
            P("gx", "gy", "gz", None, None),
            P("gx", "gy", "gz", None, None),
        ),
        check_vma=False,
    )
```

```python
import functools
import math

import jax
import jax.numpy as jnp
from jax import lax
from jax.experimental import pallas as pl
from jax.experimental.pallas import tpu as pltpu
from jax.sharding import PartitionSpec as P

EPSILON = 0.1
GROUP = 8
SIDE = 2
HIGHEST = lax.Precision.HIGHEST


def from_partner(x, axis, distance):
    return lax.ppermute(x, axis, [(i, i ^ 1 << distance) for i in range(lax.axis_size(axis))])


SMALL = 0.06


def matmul(a, b, precision=HIGHEST):
    return lax.dot_general(
        a, b, (((1,), (0,)), ((), ())), precision=precision, preferred_element_type=jnp.float32
    )


def matmul_t(a, b, precision=HIGHEST):
    return lax.dot_general(
        a, b, (((1,), (1,)), ((), ())), precision=precision, preferred_element_type=jnp.float32
    )


def join(parts, axis):
    return jnp.concatenate(parts, axis=axis)


def halves(x):
    high = x.astype(jnp.bfloat16)
    return high, (x - high.astype(jnp.float32)).astype(jnp.bfloat16)


def thirds(x):
    high = x.astype(jnp.bfloat16)
    rest = x - high.astype(jnp.float32)
    return (high,) + halves(rest)


def positions(shape):
    return (
        lax.broadcasted_iota(jnp.int32, shape, 0),
        lax.broadcasted_iota(jnp.int32, shape, 1),
    )


def unit(rank):
    row, column = positions((rank, rank))
    return jnp.where(row == column, 1.0, 0.0).astype(jnp.float32)


def upper(x):
    row, column = positions(x.shape)
    return jnp.where(row <= column, x, 0.0)


def half_lower(x):
    row, column = positions(x.shape)
    return jnp.where(row > column, x, jnp.where(row == column, 0.5 * x, 0.0))


def gram_of(parts):
    f, g, h = parts
    return matmul_t(join([f, f, g, g, f, h], 1), join([f, g, f, g, h, f], 1), None)


def right_side(parts):
    f, g, h = parts
    return join([f, f, g, g, h, f], 0)


def left_side(x):
    f, g, h = thirds(x)
    first = join([f, g], 1)
    return join([first, first, join([f, h], 1)], 1)


def near_gram(x, y):
    f, g = halves(x)
    u, v = halves(y)
    return matmul_t(join([f, f, g], 1), join([u, v, u], 1), None)


def near_unit_factor(excess):
    x = half_lower(excess)
    square = matmul(x, x, None)
    x = half_lower(excess - matmul_t(x, x, None))
    return x, x - square


def not_small(norm):
    return jnp.logical_not(norm[0, 0] <= SMALL * SMALL)


def batch_rows(work, rank, batch, low, high, width=8):
    shape = (batch, 2 * rank)

    def lane(values, index):
        return jnp.broadcast_to(values[:, rank + index : rank + index + 1], shape)

    for start in range(low, high, width):
        rows = [work[(start + i) * batch : (start + i + 1) * batch, :] for i in range(width)]
        scalars = [
            [lane(rows[i], start + j) if j >= i else None for j in range(width)]
            for i in range(width)
        ]
        for j in range(width):
            root = lax.rsqrt(scalars[j][j])
            rows[j] = rows[j] * root
            factor = [None if i <= j else scalars[j][i] * root for i in range(width)]
            for i in range(j + 1, width):
                rows[i] = rows[i] - factor[i] * rows[j]
                for k in range(i, width):
                    scalars[i][k] = scalars[i][k] - factor[i] * factor[k]
            work[(start + j) * batch : (start + j + 1) * batch, :] = rows[j]
        for lower in range(start + width, high):
            total = work[lower * batch : (lower + 1) * batch, :]
            for j in range(width):
                total = total - lane(rows[j], lower) * rows[j]
            work[lower * batch : (lower + 1) * batch, :] = total


def batch_update(work, rank, batch, low, high):
    size = high - low
    each = 128 // size
    row, column = positions((128, 128))
    for first in range(0, batch, each):
        done = join(
            [work[pl.ds(low * batch + first + i, size, stride=batch), :] for i in range(each)], 0
        )
        turned = done.T
        right = right_side(thirds(done))
        for top in range(high, rank, size):
            factor = join([turned[rank + top : rank + top + size, :]] * each, 0)
            f, g, h = thirds(jnp.where(row // size == column // size, factor, 0.0))
            change = matmul(join([f, g, f, g, f, h], 1), right, None)
            for i in range(each):
                place = pl.ds(top * batch + first + i, size, stride=batch)
                work[place, :] = work[place, :] - change[i * size : (i + 1) * size]


def eliminate_batch(work, rank, batch):
    half = rank // 2
    batch_rows(work, rank, batch, 0, half)
    batch_update(work, rank, batch, 0, half)
    batch_rows(work, rank, batch, half, rank)


def eliminate_single(work, rank):
    shape = (8, 2 * rank)
    row, _ = positions(shape)
    for start in range(0, rank, 8):
        blocks = {m: work[m : m + 8, :] for m in range(start, rank, 8)}
        columns = {
            m: [
                jnp.broadcast_to(blocks[m][:, rank + start + j : rank + start + j + 1], shape)
                for j in range(8)
            ]
            for m in blocks
        }
        done = blocks[start]
        for j in range(8):
            root = lax.rsqrt(columns[start][j][j : j + 1, :])
            line = [columns[start][i][j : j + 1, :] * root for i in range(8)]
            scaled = blocks[start][j : j + 1, :] * root
            done = jnp.where(row == j, scaled, done)
            for m in blocks:
                factor = columns[m][j] * root
                blocks[m] = blocks[m] - factor * scaled
                for i in range(j + 1, 8):
                    columns[m][i] = columns[m][i] - factor * line[i]
        work[start : start + 8, :] = done
        for m in blocks:
            if m > start:
                work[m : m + 8, :] = blocks[m]


def parity(axis):
    return lax.axis_index(axis) % 2


def to_neighbours(low, high, axis):
    size = lax.axis_size(axis)
    even = parity(axis) == 0
    pairs = [(i, i ^ 1) for i in range(size)]
    received = [lax.ppermute(jnp.where(even, high, low), axis, pairs)]
    if size > 2:
        across = [(i, i + 1) for i in range(1, size - 1, 2)]
        across = across + [(j, i) for i, j in across]
        received.insert(0, lax.ppermute(jnp.where(even, low, high), axis, across))
    return received[::-1]


def halo_count(axis):
    return 1 if lax.axis_size(axis) == 2 else 2


def leaf_index(x, y, z):
    return (x * SIDE + y) * SIDE + z


def pair_tables(halos):
    depth = SIDE + halos[2]
    stages = ([], [], [], [])
    for a in range(SIDE**3):
        place = (a // 4, a // 2 % 2, a % 2)
        for k in range(27):
            at = [p + d for p, d in zip(place, (k // 9 - 1, k // 3 % 3 - 1, k % 3 - 1))]
            sides = tuple((axis, t) for axis, t in enumerate(at) if t in (-1, 2))
            x, y, z = (2 if t == -1 else t for t in at)
            if at[0] == -1:
                stages[3].append((a, k, y * depth + z, sides[1:], True))
            elif at[0] == 2:
                continue
            elif y == 2:
                stages[2].append((a, k, x * depth + z, sides, False))
            elif z == 2:
                stages[1].append((a, k, SIDE**3 + x * SIDE + y, sides, False))
            else:
                stages[a * 2 // SIDE**3].append((a, k, leaf_index(x, y, z), sides, False))
    return stages


def far_sides(halos):
    found = {}
    for axis, name in enumerate(("gx", "gy", "gz")):
        place = lax.axis_index(name)
        odd = place % 2
        other = halos[axis] - 1
        found[axis, -1] = ((place > 0).astype(jnp.int32), (1 - odd) * other)
        found[axis, 2] = ((place < lax.axis_size(name) - 1).astype(jnp.int32), odd * other)
    return found


def list_pairs(pairs, halos, near, listed, count, x_side):
    found = far_sides(halos)
    depth = SIDE + halos[2]
    joint = {}
    for a, k, source, sides, across in pairs:
        key = (sides, across)
        if key not in joint:
            inside, moved, entry = jnp.int32(1), jnp.int32(0), jnp.int32(0)
            if across:
                steps = {1: depth, 2: 1}
                inside = x_side[1]
                entry = x_side[0] * (4 * 27 + 18)
            elif any(axis == 1 for axis, _ in sides):
                steps = {1: SIDE * depth, 2: 1}
            else:
                steps = {2: SIDE * SIDE}
            for side in sides:
                inside = inside * found[side][0]
                moved = moved + found[side][1] * steps[side[0]]
            joint[key] = (inside, moved * (8 * 27) + entry, entry)
        inside, moved, entry = joint[key]
        code = jnp.int32((source * 8 + a) * 27 + k)
        if sides or across:
            taken = near[a * 27 + k + entry] * inside
            code = code + moved
        else:
            taken = near[a * 27 + k]
        listed[count] = code
        count = count + taken
    return count


def close_list(listed, count, blank):
    for i in range(GROUP):
        listed[count + i] = jnp.int32(blank * 8 * 27 + 13)
    return lax.div(count + (GROUP - 1), jnp.int32(GROUP))


def spread_offsets(blocks, count, turned, spread):
    rank3 = blocks.shape[1] - 16
    turned[...] = jnp.zeros_like(turned)
    for s in range(count):
        turned[4 * s : 4 * s + 4, :] = blocks[s, rank3:, :].astype(jnp.float32)[:4]
    columns = turned[...].T.astype(jnp.bfloat16)
    row, lane = positions((128, 384))
    for s in range(count):
        chosen = jnp.where(row == 4 * s + lane // 128, 1.0, 0.0).astype(jnp.bfloat16)
        values = matmul(columns, chosen, None)
        for p in range(3):
            spread[s, p] = values[:, 128 * p : 128 * (p + 1)]


def tile_rows(own, spread, rows):
    r = [own[p] - spread[p, rows, :] for p in range(3)]
    squares = [v * v for v in r]
    softened = squares[0] + squares[1] + squares[2] + EPSILON * EPSILON
    lifted = softened + EPSILON * EPSILON
    root = lax.rsqrt(softened)
    h = root * root * root
    ry, rz = r[1] * h, r[2] * h
    tiles = {(p, p): (squares[p] + lifted) * h for p in range(3)}
    tiles[0, 1], tiles[0, 2], tiles[1, 2] = r[0] * ry, r[0] * rz, r[1] * rz
    return {pq: tile.astype(jnp.bfloat16) for pq, tile in tiles.items()}


def add_pairs(groups, listed, blocks, own, spread, total):
    chunk = 16

    @pl.loop(0, groups)
    def _(group):
        for u in range(GROUP):
            code = listed[group * GROUP + u]
            pair = lax.div(code, jnp.int32(27))
            k = code - pair * 27
            source = lax.shift_right_logical(pair, jnp.int32(3))
            a = lax.bitwise_and(pair, jnp.int32(7))
            dx = lax.div(k, jnp.int32(9))
            dy = lax.div(k, jnp.int32(3)) - dx * 3
            dz = k - dx * 9 - dy * 3
            own_rows = own[a]
            placed = [
                jnp.broadcast_to(
                    own_rows[p : p + 1] + (1 - step).astype(jnp.float32), (chunk, 128)
                )
                for p, step in enumerate((dx, dy, dz))
            ]
            parts = [
                tile_rows(placed, spread.at[source], pl.ds(j, chunk))
                for j in range(0, 128, chunk)
            ]
            tiles = {
                pq: jnp.concatenate([part[pq] for part in parts], axis=0) for pq in parts[0]
            }
            matrix = jnp.concatenate(
                [
                    jnp.concatenate([tiles[min(p, q), max(p, q)] for p in range(3)], axis=1)
                    for q in range(3)
                ],
                axis=0,
            )
            rank = total.shape[1]
            sampled = jnp.concatenate(
                [blocks[source, q * rank : (q + 1) * rank, :] for q in range(3)], axis=1
            )
            total[a] += matmul(sampled, matrix, None)


def fetch(parts, blocks, semaphore):
    copies = []
    first = 0
    for i, part in enumerate(parts):
        copies.append(
            pltpu.make_async_copy(
                part, blocks.at[pl.ds(first, part.shape[0])], semaphore.at[i]
            )
        )
        copies[-1].start()
        first += part.shape[0]
    return copies, first


def near_stage(stage, near, own, parts, total, listed, blocks, turned, spread, semaphore):
    halos, lists = stage
    copies, count = fetch(parts, blocks, semaphore)
    odd = lax.axis_index("gx") % 2
    size = lax.axis_size("gx")
    start = jnp.int32(0)
    for pairs, first, within in lists:
        pairs = [(a, k, source + first, sides, across) for a, k, source, sides, across in pairs]
        x_side = None
        if within is True:
            x_side = (1 - odd, jnp.int32(1))
        elif within is False:
            place = lax.axis_index("gx")
            inside = jnp.logical_and(place > 0, place < size - 1).astype(jnp.int32)
            x_side = (odd, inside)
        start = list_pairs(pairs, halos, near, listed, start, x_side)
    groups = close_list(listed, start, count)
    blocks[count] = jnp.zeros_like(blocks[count])
    for copy in copies:
        copy.wait()
    spread_offsets(blocks, count, turned, spread)
    spread[count] = jnp.zeros_like(spread[count])
    add_pairs(groups, listed, blocks, own, spread, total)


def first_kernel(stage, near, own, own_blocks, total, *scratch):
    total[...] = jnp.zeros_like(total)
    near_stage(stage, near, own, [own_blocks], total, *scratch)


def next_kernel(stage, near, own, before, *rest):
    *parts, total, listed, blocks, turned, spread, semaphore = rest
    total[...] = before[...]
    near_stage(stage, near, own, parts, total, listed, blocks, turned, spread, semaphore)


def last_kernel(stage, near, own, before, sketch, *rest):
    *parts, far, grams, factor, samples, z_out = rest[:-6]
    listed, blocks, turned, spread, semaphore, single = rest[-6:]
    far[...] = before[...]
    near_stage(stage, near, own, parts, far, listed, blocks, turned, spread, semaphore)
    far[...] = sketch[...] - far[...]
    box_level(far, grams, factor, samples, z_out, single)


def pack_kernel(samples, offsets, packed, own, *faces):
    count, rank, leaf_rows = samples.shape
    filler = jnp.zeros((13, 128), jnp.float32)
    for a in range(count):
        for q in range(3):
            packed[a, q * rank : (q + 1) * rank, :] = samples[a, :, q * 128 : (q + 1) * 128]
        rows = jnp.concatenate([offsets[a].astype(jnp.float32), filler], axis=0)
        packed[a, 3 * rank :, :] = rows.astype(jnp.bfloat16)
        own[a] = rows[:8]
    planes = [1 - parity("gz"), parity("gz")]
    for face, plane in zip(faces, planes):
        for column in range(SIDE * SIDE):
            face[column] = packed[column * SIDE + plane]


VMEM_LIMIT = 48 * 1024 * 1024


def near_scratch(stage, count, block):
    length = sum(len(pairs) for pairs, _, _ in stage[1])
    return [
        pltpu.SMEM((length + GROUP + 1,), jnp.int32),
        pltpu.VMEM((count + 1,) + block, jnp.bfloat16),
        pltpu.VMEM((128, 128), jnp.float32),
        pltpu.VMEM((count + 1, 3, 128, 128), jnp.float32),
        pltpu.SemaphoreType.DMA((4,)),
    ]


def cost(microseconds):
    return pl.CostEstimate(
        flops=microseconds * 1000 * 1000 * 1000, bytes_accessed=4 * 1024 * 1024, transcendentals=0
    )


IN_SMEM = pl.BlockSpec(memory_space=pltpu.SMEM)
IN_VMEM = pl.BlockSpec(memory_space=pltpu.VMEM)
ANYWHERE = pl.BlockSpec(memory_space=pl.ANY)


def box_level(far, grams_out, factor_out, samples_out, z_out, single):
    count, rank, _ = far.shape
    eye = unit(rank)
    total = jnp.zeros_like(eye)
    for a in range(count):
        gram = gram_of(thirds(far[a]))
        grams_out[a] = gram
        total = total + gram
    single[...] = join([eye, 0.5 * (total + total.T)], 1)
    eliminate_single(single, rank)
    left = left_side(single[:, :rank])
    lower = upper(single[:, rank:]).T
    excess = -eye
    for a in range(count):
        samples = matmul(left, right_side(thirds(far[a])), None)
        samples_out[a] = samples
        excess = excess + near_gram(samples, samples)
    x, z_out[...] = near_unit_factor(excess)
    factor_out[...] = lower + matmul(lower, x)

    @pl.when(not_small(jnp.sum(excess * excess, keepdims=True)))
    def _():
        single[...] = join([eye, eye + excess], 1)
        eliminate_single(single, rank)
        factor_out[...] = matmul(lower, upper(single[:, rank:]).T)
        for a in range(count):
            samples_out[a] = matmul(single[:, :rank], samples_out[a])
        z_out[...] = jnp.zeros_like(eye)


def leaf_factors(grams, work):
    count, rank, _ = grams.shape
    eye = unit(rank)
    for a in range(count):
        work[pl.ds(a, rank, stride=count), :] = join([eye, grams[a]], 1)
    eliminate_batch(work, rank, count)


def leaf_kernel(far, factors, samples, box_z, leaf_out, level_out, work, blocks, es, zs):
    count, rank, leaf_rows = far.shape
    eye = unit(rank)
    largest = jnp.zeros((1, 1), jnp.float32)
    for a in range(count):
        inverse = factors[pl.ds(a, rank, stride=count), :][:, :rank]
        basis = matmul(left_side(inverse), right_side(thirds(far[a])), None)
        leaf_out[a] = basis
        products = near_gram(join([basis, samples[a]], 0), basis)
        blocks[a] = products[rank:]
        excess = products[:rank] - eye
        es[a] = excess
        largest = jnp.maximum(largest, jnp.sum(excess * excess, keepdims=True))
    for a in range(count):
        zs[a] = near_unit_factor(es[a])[1]

    @pl.when(not_small(largest))
    def _():
        for a in range(count):
            work[pl.ds(a, rank, stride=count), :] = join([eye, eye + es[a]], 1)
        eliminate_batch(work, rank, count)
        for a in range(count):
            inverse = work[pl.ds(a, rank, stride=count), :][:, :rank]
            leaf_out[a] = matmul(inverse, leaf_out[a])
            blocks[a] = matmul_t(blocks[a], inverse)
            zs[a] = jnp.zeros_like(eye)

    for a in range(count):
        basis = leaf_out[a]
        leaf_out[a] = (basis - matmul(zs[a], basis, None)) * math.sqrt(leaf_rows)
        block = blocks[a]
        blocks[a] = (block - matmul_t(block, zs[a], None)) * math.sqrt(count * rank)
    block = join([blocks[a] for a in range(count)], 1)
    level_out[...] = block - matmul(box_z[...], block, None)


def group_kernel(factors, samples, box_z, nested_out, single, stack):
    count, rank, _ = factors.shape
    eye = unit(rank)
    for b in range(count):
        stack[:, b * rank : (b + 1) * rank] = factors[b]
    parts = thirds(stack[...])
    gram = gram_of(parts)
    single[...] = join([eye, 0.5 * (gram + gram.T)], 1)
    eliminate_single(single, rank)
    block = matmul(left_side(single[:, :rank]), right_side(parts), None)
    excess = near_gram(block, block) - eye
    own = block[:, :rank] * (8.0 * math.sqrt(samples.shape[2]))
    mixing = own - matmul(near_unit_factor(excess)[1], own, None)
    mix_samples(mixing, samples, box_z, nested_out)

    @pl.when(not_small(jnp.sum(excess * excess, keepdims=True)))
    def _():
        single[...] = join([eye, eye + excess], 1)
        eliminate_single(single, rank)
        mix_samples(matmul(single[:, :rank], own), samples, box_z, nested_out)


def mix_samples(mixing, samples, box_z, nested_out):
    mixing = mixing - matmul(mixing, box_z[...], None)
    left = join(halves(mixing) * 2, 1)
    for a in range(samples.shape[0]):
        f, g = halves(samples[a])
        nested_out[a] = matmul(left, join([f, f, g, g], 0), None)


def body(sketch, test_matrix, offsets, near):
    rank, leaf_rows = sketch.shape[3:]
    count = SIDE**3
    halos = [halo_count(axis) for axis in ("gx", "gy", "gz")]
    like = jax.ShapeDtypeStruct
    block = (3 * rank + 16, 128)
    params = pltpu.CompilerParams(vmem_limit_bytes=VMEM_LIMIT)
    flat_near = near.reshape(count * 27)
    flat_sketch = sketch.reshape(count, rank, leaf_rows)
    stages = pair_tables(halos)
    faces = halos[2]
    packed, own, *sent = pl.pallas_call(
        pack_kernel,
        out_shape=(
            like((count,) + block, jnp.bfloat16),
            like((count, 8, 128), jnp.float32),
        )
        + (like((SIDE * SIDE,) + block, jnp.bfloat16),) * faces,
        compiler_params=params,
        name="pack",
    )(test_matrix.reshape(count, rank, leaf_rows), offsets.reshape(count, 3, 128))
    z_halos = [from_partner(sent[0], "gz", 0)]
    if faces == 2:
        size = lax.axis_size("gz")
        across = [(i, i + 1) for i in range(1, size - 1, 2)]
        across = across + [(j, i) for i, j in across]
        z_halos.append(lax.ppermute(sent[1], "gz", across))
    inner = packed.reshape((SIDE, SIDE, SIDE) + block)
    columns = [h.reshape((SIDE, SIDE, 1) + block) for h in z_halos]
    extended = join([inner] + columns, 2)
    depth = extended.shape[2]
    flat = lambda parts: [x.reshape((-1,) + block) for x in parts]
    column = (SIDE + halos[1]) * depth
    y_blocks = SIDE * depth * halos[1]
    whole = like((count, rank, leaf_rows), jnp.float32)
    squares = like((count, rank, rank), jnp.float32)
    square = like((rank, rank), jnp.float32)
    single_scratch = pltpu.VMEM((rank, 2 * rank), jnp.float32)

    stage = (halos, [(stages[0], 0, None)])
    total = pl.pallas_call(
        functools.partial(first_kernel, stage),
        out_shape=whole,
        in_specs=[IN_SMEM, IN_VMEM, ANYWHERE],
        scratch_shapes=near_scratch(stage, count, block),
        cost_estimate=cost(4),
        compiler_params=params,
        name="near_inner",
    )(flat_near, own, packed)

    extended, total = lax.optimization_barrier((extended, total))
    y_halos = to_neighbours(extended[:, 0], extended[:, 1], "gy")

    def add_stage(stage, total, parts, name, time):
        return pl.pallas_call(
            functools.partial(next_kernel, stage),
            out_shape=whole,
            in_specs=[IN_SMEM, IN_VMEM, IN_VMEM] + [ANYWHERE] * len(parts),
            scratch_shapes=near_scratch(stage, sum(part.shape[0] for part in parts), block),
            cost_estimate=cost(time),
            compiler_params=params,
            name=name,
        )(flat_near, own, total, *parts)

    stage = (halos, [(stages[1], 0, None)])
    total = add_stage(stage, total, [packed] + flat(z_halos), "near_inner_and_z", 5)
    wide = join([extended] + [h[:, None] for h in y_halos], 1)
    wide, total = lax.optimization_barrier((wide, total))
    x_halos = to_neighbours(wide[0], wide[1], "gx")
    stage = (halos, [(stages[2], 0, None), (stages[3], y_blocks, True)])
    total = add_stage(stage, total, flat(y_halos) + flat(x_halos[:1]), "near_y_and_x", 7)
    stage = (halos, [(stages[3], 0, False)] if halos[0] == 2 else [])
    parts = flat(x_halos[1:])
    far, grams, factor, samples, box_z = pl.pallas_call(
        functools.partial(last_kernel, stage),
        out_shape=(whole, squares, square, whole, square),
        in_specs=[IN_SMEM, IN_VMEM, IN_VMEM, IN_VMEM] + [ANYWHERE] * len(parts),
        scratch_shapes=near_scratch(stage, column * len(parts), block) + [single_scratch],
        compiler_params=params,
        name="near_x_and_box_level",
    )(flat_near, own, total, flat_sketch, *parts)
    grouped = factor[None]
    grouped = join([grouped, from_partner(grouped, "gz", 0)], 0)
    factors = pl.pallas_call(
        leaf_factors,
        out_shape=like((rank * count, 2 * rank), jnp.float32),
        cost_estimate=cost(3),
        compiler_params=params,
        name="leaf_factors",
    )(grams)
    grouped, factors = lax.optimization_barrier((grouped, factors))
    grouped = join([grouped, from_partner(grouped, "gy", 0)], 0)
    leaf_t, level_t = pl.pallas_call(
        leaf_kernel,
        out_shape=(whole, like((rank, count * rank), jnp.float32)),
        scratch_shapes=[pltpu.VMEM((rank * count, 2 * rank), jnp.float32)]
        + [pltpu.VMEM((count, rank, rank), jnp.float32)] * 3,
        cost_estimate=cost(4),
        compiler_params=params,
        name="leaf_level",
    )(far, factors, samples, box_z)
    grouped, leaf_t, level_t = lax.optimization_barrier((grouped, leaf_t, level_t))
    grouped = join([grouped, from_partner(grouped, "gx", 0)], 0)
    nested = pl.pallas_call(
        group_kernel,
        out_shape=whole,
        scratch_shapes=[
            single_scratch,
            pltpu.VMEM((rank, count * rank), jnp.float32),
        ],
        compiler_params=params,
        name="group_level",
    )(grouped, samples, box_z)
    return (leaf_t.reshape(sketch.shape), level_t[None, None, None], nested.reshape(sketch.shape))


def solution(mesh):
    placed = (
        P("gx", "gy", "gz", None, None),
        P("gx", "gy", "gz", None, None),
        P("gx", "gy", "gz", None, None),
        P("gx", "gy", "gz", None),
    )
    return jax.shard_map(
        body,
        mesh=mesh,
        in_specs=placed,
        out_specs=(
            P("gx", "gy", "gz", None, None),
            P("gx", "gy", "gz", None, None),
            P("gx", "gy", "gz", None, None),
        ),
        check_vma=False,
    )
```

```python
import functools
import math

import jax
import jax.numpy as jnp
from jax import lax
from jax.experimental import pallas as pl
from jax.experimental.pallas import tpu as pltpu
from jax.sharding import PartitionSpec as P

EPSILON = 0.1
GROUP = 8
SIDE = 2
HIGHEST = lax.Precision.HIGHEST


def from_partner(x, axis, distance):
    return lax.ppermute(x, axis, [(i, i ^ 1 << distance) for i in range(lax.axis_size(axis))])


SMALL = 0.06


def matmul(a, b, precision=HIGHEST):
    return lax.dot_general(
        a, b, (((1,), (0,)), ((), ())), precision=precision, preferred_element_type=jnp.float32
    )


def matmul_t(a, b, precision=HIGHEST):
    return lax.dot_general(
        a, b, (((1,), (1,)), ((), ())), precision=precision, preferred_element_type=jnp.float32
    )


def join(parts, axis):
    return jnp.concatenate(parts, axis=axis)


def halves(x):
    high = x.astype(jnp.bfloat16)
    return high, (x - high.astype(jnp.float32)).astype(jnp.bfloat16)


def thirds(x):
    high = x.astype(jnp.bfloat16)
    rest = x - high.astype(jnp.float32)
    return (high,) + halves(rest)


def positions(shape):
    return (
        lax.broadcasted_iota(jnp.int32, shape, 0),
        lax.broadcasted_iota(jnp.int32, shape, 1),
    )


def unit(rank):
    row, column = positions((rank, rank))
    return jnp.where(row == column, 1.0, 0.0).astype(jnp.float32)


def upper(x):
    row, column = positions(x.shape)
    return jnp.where(row <= column, x, 0.0)


def half_lower(x):
    row, column = positions(x.shape)
    return jnp.where(row > column, x, jnp.where(row == column, 0.5 * x, 0.0))


def gram_of(parts):
    f, g, h = parts
    return matmul_t(join([f, f, g, g, f, h], 1), join([f, g, f, g, h, f], 1), None)


def right_side(parts):
    f, g, h = parts
    return join([f, f, g, g, h, f], 0)


def left_side(x):
    f, g, h = thirds(x)
    first = join([f, g], 1)
    return join([first, first, join([f, h], 1)], 1)


def near_gram(x, y):
    f, g = halves(x)
    u, v = halves(y)
    return matmul_t(join([f, f, g], 1), join([u, v, u], 1), None)


def near_unit_factor(excess):
    x = half_lower(excess)
    square = matmul(x, x, None)
    x = half_lower(excess - matmul_t(x, x, None))
    return x, x - square


def not_small(norm):
    return jnp.logical_not(norm[0, 0] <= SMALL * SMALL)


def batch_rows(work, rank, batch, low, high, width=8):
    shape = (batch, 2 * rank)

    def lane(values, index):
        return jnp.broadcast_to(values[:, rank + index : rank + index + 1], shape)

    for start in range(low, high, width):
        rows = [work[(start + i) * batch : (start + i + 1) * batch, :] for i in range(width)]
        scalars = [
            [lane(rows[i], start + j) if j >= i else None for j in range(width)]
            for i in range(width)
        ]
        for j in range(width):
            root = lax.rsqrt(scalars[j][j])
            rows[j] = rows[j] * root
            factor = [None if i <= j else scalars[j][i] * root for i in range(width)]
            for i in range(j + 1, width):
                rows[i] = rows[i] - factor[i] * rows[j]
                for k in range(i, width):
                    scalars[i][k] = scalars[i][k] - factor[i] * factor[k]
            work[(start + j) * batch : (start + j + 1) * batch, :] = rows[j]
        for lower in range(start + width, high):
            total = work[lower * batch : (lower + 1) * batch, :]
            for j in range(width):
                total = total - lane(rows[j], lower) * rows[j]
            work[lower * batch : (lower + 1) * batch, :] = total


def batch_update(work, rank, batch, low, high):
    size = high - low
    each = 128 // size
    row, column = positions((128, 128))
    for first in range(0, batch, each):
        done = join(
            [work[pl.ds(low * batch + first + i, size, stride=batch), :] for i in range(each)], 0
        )
        turned = done.T
        right = right_side(thirds(done))
        for top in range(high, rank, size):
            factor = join([turned[rank + top : rank + top + size, :]] * each, 0)
            f, g, h = thirds(jnp.where(row // size == column // size, factor, 0.0))
            change = matmul(join([f, g, f, g, f, h], 1), right, None)
            for i in range(each):
                place = pl.ds(top * batch + first + i, size, stride=batch)
                work[place, :] = work[place, :] - change[i * size : (i + 1) * size]


def eliminate_batch(work, rank, batch):
    half = rank // 2
    batch_rows(work, rank, batch, 0, half)
    batch_update(work, rank, batch, 0, half)
    batch_rows(work, rank, batch, half, rank)


def eliminate_single(work, rank):
    shape = (8, 2 * rank)
    row, _ = positions(shape)
    for start in range(0, rank, 8):
        blocks = {m: work[m : m + 8, :] for m in range(start, rank, 8)}
        columns = {
            m: [
                jnp.broadcast_to(blocks[m][:, rank + start + j : rank + start + j + 1], shape)
                for j in range(8)
            ]
            for m in blocks
        }
        done = blocks[start]
        for j in range(8):
            root = lax.rsqrt(columns[start][j][j : j + 1, :])
            line = [columns[start][i][j : j + 1, :] * root for i in range(8)]
            scaled = blocks[start][j : j + 1, :] * root
            done = jnp.where(row == j, scaled, done)
            for m in blocks:
                factor = columns[m][j] * root
                blocks[m] = blocks[m] - factor * scaled
                for i in range(j + 1, 8):
                    columns[m][i] = columns[m][i] - factor * line[i]
        work[start : start + 8, :] = done
        for m in blocks:
            if m > start:
                work[m : m + 8, :] = blocks[m]


def parity(axis):
    return lax.axis_index(axis) % 2


def to_neighbours(low, high, axis):
    size = lax.axis_size(axis)
    even = parity(axis) == 0
    pairs = [(i, i ^ 1) for i in range(size)]
    received = [lax.ppermute(jnp.where(even, high, low), axis, pairs)]
    if size > 2:
        across = [(i, i + 1) for i in range(1, size - 1, 2)]
        across = across + [(j, i) for i, j in across]
        received.insert(0, lax.ppermute(jnp.where(even, low, high), axis, across))
    return received[::-1]


def halo_count(axis):
    return 1 if lax.axis_size(axis) == 2 else 2


def leaf_index(x, y, z):
    return (x * SIDE + y) * SIDE + z


def pair_tables(halos):
    planes = halos[2]
    tables = {}
    for a in range(SIDE**3):
        place = (a // 4, a // 2 % 2, a % 2)
        for k in range(27):
            at = [p + d for p, d in zip(place, (k // 9 - 1, k // 3 % 3 - 1, k % 3 - 1))]
            sides = tuple((axis, t) for axis, t in enumerate(at) if t in (-1, 2) and axis > 0)
            key = tuple(t in (-1, 2) for t in at)
            if at[0] == 2:
                continue
            x, y, z = at
            source = {
                (False, False, False): leaf_index(x, y, z),
                (False, False, True): x * SIDE + y,
                (False, True, False): x * SIDE + z,
                (False, True, True): x,
                (True, False, False): y * SIDE + z,
                (True, False, True): y,
                (True, True, False): SIDE * planes + z,
                (True, True, True): 0,
            }[key]
            tables.setdefault(key, []).append((a, k, source, sides))
    return tables


def side_steps(key, planes):
    return {
        (False, False, False): {},
        (False, False, True): {2: SIDE * SIDE},
        (False, True, False): {1: SIDE * SIDE},
        (False, True, True): {1: SIDE * planes, 2: SIDE},
        (True, False, False): {},
        (True, False, True): {2: SIDE},
        (True, True, False): {1: SIDE},
        (True, True, True): {1: planes, 2: 1},
    }[key]


def far_sides(halos):
    found = {}
    for axis, name in enumerate(("gx", "gy", "gz")):
        place = lax.axis_index(name)
        odd = place % 2
        other = halos[axis] - 1
        found[axis, -1] = ((place > 0).astype(jnp.int32), (1 - odd) * other)
        found[axis, 2] = ((place < lax.axis_size(name) - 1).astype(jnp.int32), odd * other)
    return found


def list_pairs(pairs, steps, first, found, near, listed, count, x_side):
    joint = {}
    entry = None
    if x_side is not None:
        entry = x_side[0] * (4 * 27 + 18)
    for a, k, source, sides in pairs:
        if sides not in joint:
            inside, moved = jnp.int32(1), jnp.int32(0)
            if x_side is not None:
                inside, moved = x_side[1], entry
            for side in sides:
                inside = inside * found[side][0]
                moved = moved + found[side][1] * (steps[side[0]] * 8 * 27)
            joint[sides] = (inside, moved)
        inside, moved = joint[sides]
        code = jnp.int32(((first + source) * 8 + a) * 27 + k)
        taken = near[a * 27 + k] if entry is None else near[a * 27 + k + entry]
        if sides or entry is not None:
            code = code + moved
            taken = taken * inside
        listed[count] = code
        count = count + taken
    return count


def close_list(listed, count, blank):
    for i in range(GROUP):
        listed[count + i] = jnp.int32(blank * 8 * 27 + 13)
    return lax.div(count + (GROUP - 1), jnp.int32(GROUP))


def spread_offsets(blocks, count, turned, spread):
    rank3 = blocks.shape[1] - 16
    turned[...] = jnp.zeros_like(turned)
    for s in range(count):
        turned[4 * s : 4 * s + 4, :] = blocks[s, rank3:, :].astype(jnp.float32)[:4]
    columns = turned[...].T.astype(jnp.bfloat16)
    row, lane = positions((128, 384))
    for s in range(count):
        chosen = jnp.where(row == 4 * s + lane // 128, 1.0, 0.0).astype(jnp.bfloat16)
        values = matmul(columns, chosen, None)
        for p in range(3):
            spread[s, p] = values[:, 128 * p : 128 * (p + 1)]


def tile_rows(own, spread, rows):
    r = [own[p] - spread[p, rows, :] for p in range(3)]
    squares = [v * v for v in r]
    softened = squares[0] + squares[1] + squares[2] + EPSILON * EPSILON
    lifted = softened + EPSILON * EPSILON
    root = lax.rsqrt(softened)
    h = root * root * root
    ry, rz = r[1] * h, r[2] * h
    tiles = {(p, p): (squares[p] + lifted) * h for p in range(3)}
    tiles[0, 1], tiles[0, 2], tiles[1, 2] = r[0] * ry, r[0] * rz, r[1] * rz
    return {pq: tile.astype(jnp.bfloat16) for pq, tile in tiles.items()}


def add_pairs(groups, listed, blocks, own, spread, total):
    chunk = 16

    @pl.loop(0, groups)
    def _(group):
        for u in range(GROUP):
            code = listed[group * GROUP + u]
            pair = lax.div(code, jnp.int32(27))
            k = code - pair * 27
            source = lax.shift_right_logical(pair, jnp.int32(3))
            a = lax.bitwise_and(pair, jnp.int32(7))
            dx = lax.div(k, jnp.int32(9))
            dy = lax.div(k, jnp.int32(3)) - dx * 3
            dz = k - dx * 9 - dy * 3
            own_rows = own[a]
            placed = [
                jnp.broadcast_to(
                    own_rows[p : p + 1] + (1 - step).astype(jnp.float32), (chunk, 128)
                )
                for p, step in enumerate((dx, dy, dz))
            ]
            parts = [
                tile_rows(placed, spread.at[source], pl.ds(j, chunk))
                for j in range(0, 128, chunk)
            ]
            tiles = {
                pq: jnp.concatenate([part[pq] for part in parts], axis=0) for pq in parts[0]
            }
            matrix = jnp.concatenate(
                [
                    jnp.concatenate([tiles[min(p, q), max(p, q)] for p in range(3)], axis=1)
                    for q in range(3)
                ],
                axis=0,
            )
            rank = total.shape[1]
            sampled = jnp.concatenate(
                [blocks[source, q * rank : (q + 1) * rank, :] for q in range(3)], axis=1
            )
            total[a] += matmul(sampled, matrix, None)


def fetch(parts, blocks, semaphore):
    copies = []
    first = 0
    for i, part in enumerate(parts):
        copies.append(
            pltpu.make_async_copy(
                part, blocks.at[pl.ds(first, part.shape[0])], semaphore.at[i]
            )
        )
        copies[-1].start()
        first += part.shape[0]
    return copies, first


def near_stage(stage, near, own, parts, total, listed, blocks, turned, spread, semaphore):
    halos, lists = stage
    copies, count = fetch(parts, blocks, semaphore)
    found = far_sides(halos)
    odd = lax.axis_index("gx") % 2
    size = lax.axis_size("gx")
    start = jnp.int32(0)
    for pairs, steps, first, within in lists:
        x_side = None
        if within is True:
            x_side = (1 - odd, jnp.int32(1))
        elif within is False:
            place = lax.axis_index("gx")
            inside = jnp.logical_and(place > 0, place < size - 1).astype(jnp.int32)
            x_side = (odd, inside)
        start = list_pairs(pairs, steps, first, found, near, listed, start, x_side)
    groups = close_list(listed, start, count)
    blocks[count] = jnp.zeros_like(blocks[count])
    for copy in copies:
        copy.wait()
    spread_offsets(blocks, count, turned, spread)
    spread[count] = jnp.zeros_like(spread[count])
    add_pairs(groups, listed, blocks, own, spread, total)


def first_kernel(stage, near, own, own_blocks, total, *scratch):
    total[...] = jnp.zeros_like(total)
    near_stage(stage, near, own, [own_blocks], total, *scratch)


def next_kernel(stage, near, own, before, *rest):
    *parts, total, listed, blocks, turned, spread, semaphore = rest
    total[...] = before[...]
    near_stage(stage, near, own, parts, total, listed, blocks, turned, spread, semaphore)


def last_kernel(stage, near, own, before, sketch, *rest):
    *parts, far, grams, factor, samples, z_out = rest[:-6]
    listed, blocks, turned, spread, semaphore, single = rest[-6:]
    far[...] = before[...]
    near_stage(stage, near, own, parts, far, listed, blocks, turned, spread, semaphore)
    far[...] = sketch[...] - far[...]
    box_level(far, grams, factor, samples, z_out, single)


def pack_kernel(samples, offsets, packed, own, *faces):
    count, rank, leaf_rows = samples.shape
    filler = jnp.zeros((13, 128), jnp.float32)
    for a in range(count):
        for q in range(3):
            packed[a, q * rank : (q + 1) * rank, :] = samples[a, :, q * 128 : (q + 1) * 128]
        rows = jnp.concatenate([offsets[a].astype(jnp.float32), filler], axis=0)
        packed[a, 3 * rank :, :] = rows.astype(jnp.bfloat16)
        own[a] = rows[:8]
    planes = [1 - parity("gz"), parity("gz")]
    for face, plane in zip(faces, planes):
        for column in range(SIDE * SIDE):
            face[column] = packed[column * SIDE + plane]


VMEM_LIMIT = 48 * 1024 * 1024


def near_scratch(stage, count, block):
    length = sum(len(pairs) for pairs, _, _, _ in stage[1])
    return [
        pltpu.SMEM((length + GROUP + 1,), jnp.int32),
        pltpu.VMEM((count + 1,) + block, jnp.bfloat16),
        pltpu.VMEM((128, 128), jnp.float32),
        pltpu.VMEM((count + 1, 3, 128, 128), jnp.float32),
        pltpu.SemaphoreType.DMA((8,)),
    ]


def cost(microseconds):
    return pl.CostEstimate(
        flops=microseconds * 1000 * 1000 * 1000, bytes_accessed=4 * 1024 * 1024, transcendentals=0
    )


IN_SMEM = pl.BlockSpec(memory_space=pltpu.SMEM)
IN_VMEM = pl.BlockSpec(memory_space=pltpu.VMEM)
ANYWHERE = pl.BlockSpec(memory_space=pl.ANY)


def box_level(far, grams_out, factor_out, samples_out, z_out, single):
    count, rank, _ = far.shape
    eye = unit(rank)
    total = jnp.zeros_like(eye)
    for a in range(count):
        gram = gram_of(thirds(far[a]))
        grams_out[a] = gram
        total = total + gram
    single[...] = join([eye, 0.5 * (total + total.T)], 1)
    eliminate_single(single, rank)
    left = left_side(single[:, :rank])
    lower = upper(single[:, rank:]).T
    excess = -eye
    for a in range(count):
        samples = matmul(left, right_side(thirds(far[a])), None)
        samples_out[a] = samples
        excess = excess + near_gram(samples, samples)
    x, z_out[...] = near_unit_factor(excess)
    factor_out[...] = lower + matmul(lower, x)

    @pl.when(not_small(jnp.sum(excess * excess, keepdims=True)))
    def _():
        single[...] = join([eye, eye + excess], 1)
        eliminate_single(single, rank)
        factor_out[...] = matmul(lower, upper(single[:, rank:]).T)
        for a in range(count):
            samples_out[a] = matmul(single[:, :rank], samples_out[a])
        z_out[...] = jnp.zeros_like(eye)


def leaf_factors(grams, work):
    count, rank, _ = grams.shape
    eye = unit(rank)
    for a in range(count):
        work[pl.ds(a, rank, stride=count), :] = join([eye, grams[a]], 1)
    eliminate_batch(work, rank, count)


def leaf_kernel(far, factors, samples, box_z, leaf_out, level_out, work, blocks, es, zs):
    count, rank, leaf_rows = far.shape
    eye = unit(rank)
    largest = jnp.zeros((1, 1), jnp.float32)
    for a in range(count):
        inverse = factors[pl.ds(a, rank, stride=count), :][:, :rank]
        basis = matmul(left_side(inverse), right_side(thirds(far[a])), None)
        leaf_out[a] = basis
        products = near_gram(join([basis, samples[a]], 0), basis)
        blocks[a] = products[rank:]
        excess = products[:rank] - eye
        es[a] = excess
        largest = jnp.maximum(largest, jnp.sum(excess * excess, keepdims=True))
    for a in range(count):
        zs[a] = near_unit_factor(es[a])[1]

    @pl.when(not_small(largest))
    def _():
        for a in range(count):
            work[pl.ds(a, rank, stride=count), :] = join([eye, eye + es[a]], 1)
        eliminate_batch(work, rank, count)
        for a in range(count):
            inverse = work[pl.ds(a, rank, stride=count), :][:, :rank]
            leaf_out[a] = matmul(inverse, leaf_out[a])
            blocks[a] = matmul_t(blocks[a], inverse)
            zs[a] = jnp.zeros_like(eye)

    for a in range(count):
        basis = leaf_out[a]
        leaf_out[a] = (basis - matmul(zs[a], basis, None)) * math.sqrt(leaf_rows)
        block = blocks[a]
        blocks[a] = (block - matmul_t(block, zs[a], None)) * math.sqrt(count * rank)
    block = join([blocks[a] for a in range(count)], 1)
    level_out[...] = block - matmul(box_z[...], block, None)


def group_kernel(factors, samples, box_z, nested_out, single, stack):
    count, rank, _ = factors.shape
    eye = unit(rank)
    for b in range(count):
        stack[:, b * rank : (b + 1) * rank] = factors[b]
    parts = thirds(stack[...])
    gram = gram_of(parts)
    single[...] = join([eye, 0.5 * (gram + gram.T)], 1)
    eliminate_single(single, rank)
    block = matmul(left_side(single[:, :rank]), right_side(parts), None)
    excess = near_gram(block, block) - eye
    own = block[:, :rank] * (8.0 * math.sqrt(samples.shape[2]))
    mixing = own - matmul(near_unit_factor(excess)[1], own, None)
    mix_samples(mixing, samples, box_z, nested_out)

    @pl.when(not_small(jnp.sum(excess * excess, keepdims=True)))
    def _():
        single[...] = join([eye, eye + excess], 1)
        eliminate_single(single, rank)
        mix_samples(matmul(single[:, :rank], own), samples, box_z, nested_out)


def mix_samples(mixing, samples, box_z, nested_out):
    mixing = mixing - matmul(mixing, box_z[...], None)
    left = join(halves(mixing) * 2, 1)
    for a in range(samples.shape[0]):
        f, g = halves(samples[a])
        nested_out[a] = matmul(left, join([f, f, g, g], 0), None)


def body(sketch, test_matrix, offsets, near):
    rank, leaf_rows = sketch.shape[3:]
    count = SIDE**3
    halos = [halo_count(axis) for axis in ("gx", "gy", "gz")]
    like = jax.ShapeDtypeStruct
    block = (3 * rank + 16, 128)
    params = pltpu.CompilerParams(vmem_limit_bytes=VMEM_LIMIT)
    flat_near = near.reshape(count * 27)
    flat_sketch = sketch.reshape(count, rank, leaf_rows)
    tables = pair_tables(halos)
    planes = halos[2]
    packed, own, *sent = pl.pallas_call(
        pack_kernel,
        out_shape=(
            like((count,) + block, jnp.bfloat16),
            like((count, 8, 128), jnp.float32),
        )
        + (like((SIDE * SIDE,) + block, jnp.bfloat16),) * planes,
        compiler_params=params,
        name="pack",
    )(test_matrix.reshape(count, rank, leaf_rows), offsets.reshape(count, 3, 128))
    z_halos = [from_partner(sent[0], "gz", 0)]
    if planes == 2:
        size = lax.axis_size("gz")
        across = [(i, i + 1) for i in range(1, size - 1, 2)]
        across = across + [(j, i) for i, j in across]
        z_halos.append(lax.ppermute(sent[1], "gz", across))
    inner = packed.reshape((SIDE, SIDE, SIDE) + block)
    z_planes = join([h.reshape((1, SIDE, SIDE) + block) for h in z_halos], 0)
    y_halos = to_neighbours(inner[:, 0], inner[:, 1], "gy")
    x_halos = to_neighbours(inner[0], inner[1], "gx")
    whole = like((count, rank, leaf_rows), jnp.float32)
    squares = like((count, rank, rank), jnp.float32)
    square = like((rank, rank), jnp.float32)
    single_scratch = pltpu.VMEM((rank, 2 * rank), jnp.float32)

    def blocks_of(parts):
        return join([x.reshape((-1,) + block) for x in parts], 0)

    def make_stage(entries):
        lists, parts, first = [], [], 0
        for key, arrays, within in entries:
            lists.append((tables[key], side_steps(key, halos[2]), first, within))
            if arrays is not None:
                parts.extend(x.reshape((-1,) + block) for x in arrays)
                first = sum(part.shape[0] for part in parts)
        return (halos, lists), parts

    def across_x(key, arrays):
        return [(key, [x], i == 0) for i, x in enumerate(arrays)]

    def add_stage(entries, total, name, time):
        stage, parts = make_stage(entries)
        return pl.pallas_call(
            functools.partial(next_kernel, stage),
            out_shape=whole,
            in_specs=[IN_SMEM, IN_VMEM, IN_VMEM] + [ANYWHERE] * len(parts),
            scratch_shapes=near_scratch(stage, sum(part.shape[0] for part in parts), block),
            cost_estimate=cost(time),
            compiler_params=params,
            name=name,
        )(flat_near, own, total, *parts)

    stage, parts = make_stage([((False, False, False), [packed], None)])
    total = pl.pallas_call(
        functools.partial(first_kernel, stage),
        out_shape=whole,
        in_specs=[IN_SMEM, IN_VMEM, ANYWHERE],
        scratch_shapes=near_scratch(stage, count, block),
        cost_estimate=cost(6),
        compiler_params=params,
        name="near_inner",
    )(flat_near, own, packed)
    z_planes, y_halos, total = lax.optimization_barrier((z_planes, y_halos, total))
    zy_halos = to_neighbours(z_planes[:, :, 0], z_planes[:, :, 1], "gy")
    faces = [blocks_of([z_planes[:, i]] + [h[i] for h in y_halos]) for i in range(SIDE)]
    x_edges = to_neighbours(faces[0], faces[1], "gx")
    entries = [((False, False, True), [z_planes], None), ((False, True, False), y_halos, None)]
    entries += across_x((True, False, False), x_halos)
    total = add_stage(entries, total, "near_faces", 7)
    zy_halos, total = lax.optimization_barrier((zy_halos, total))
    faces = [blocks_of([h[:, i] for h in zy_halos]) for i in range(SIDE)]
    x_corners = to_neighbours(faces[0], faces[1], "gx")
    entries = [((False, True, True), zy_halos, None)]
    for i, x in enumerate(x_edges):
        entries += [((True, False, True), None, i == 0), ((True, True, False), [x], i == 0)]
    total = add_stage(entries, total, "near_edges", 4)
    stage, parts = make_stage(across_x((True, True, True), x_corners))
    sources = sum(part.shape[0] for part in parts)
    far, grams, factor, samples, box_z = pl.pallas_call(
        functools.partial(last_kernel, stage),
        out_shape=(whole, squares, square, whole, square),
        in_specs=[IN_SMEM, IN_VMEM, IN_VMEM, IN_VMEM] + [ANYWHERE] * len(parts),
        scratch_shapes=near_scratch(stage, sources, block) + [single_scratch],
        compiler_params=params,
        name="near_corners_and_box_level",
    )(flat_near, own, total, flat_sketch, *parts)
    grouped = factor[None]
    grouped = join([grouped, from_partner(grouped, "gz", 0)], 0)
    factors = pl.pallas_call(
        leaf_factors,
        out_shape=like((rank * count, 2 * rank), jnp.float32),
        cost_estimate=cost(3),
        compiler_params=params,
        name="leaf_factors",
    )(grams)
    grouped, factors = lax.optimization_barrier((grouped, factors))
    grouped = join([grouped, from_partner(grouped, "gy", 0)], 0)
    leaf_t, level_t = pl.pallas_call(
        leaf_kernel,
        out_shape=(whole, like((rank, count * rank), jnp.float32)),
        scratch_shapes=[pltpu.VMEM((rank * count, 2 * rank), jnp.float32)]
        + [pltpu.VMEM((count, rank, rank), jnp.float32)] * 3,
        cost_estimate=cost(4),
        compiler_params=params,
        name="leaf_level",
    )(far, factors, samples, box_z)
    grouped, leaf_t, level_t = lax.optimization_barrier((grouped, leaf_t, level_t))
    grouped = join([grouped, from_partner(grouped, "gx", 0)], 0)
    nested = pl.pallas_call(
        group_kernel,
        out_shape=whole,
        scratch_shapes=[
            single_scratch,
            pltpu.VMEM((rank, count * rank), jnp.float32),
        ],
        compiler_params=params,
        name="group_level",
    )(grouped, samples, box_z)
    return (leaf_t.reshape(sketch.shape), level_t[None, None, None], nested.reshape(sketch.shape))


def solution(mesh):
    placed = (
        P("gx", "gy", "gz", None, None),
        P("gx", "gy", "gz", None, None),
        P("gx", "gy", "gz", None, None),
        P("gx", "gy", "gz", None),
    )
    return jax.shard_map(
        body,
        mesh=mesh,
        in_specs=placed,
        out_specs=(
            P("gx", "gy", "gz", None, None),
            P("gx", "gy", "gz", None, None),
            P("gx", "gy", "gz", None, None),
        ),
        check_vma=False,
    )
```

```python
import functools
import math

import jax
import jax.numpy as jnp
from jax import lax
from jax.experimental import pallas as pl
from jax.experimental.pallas import tpu as pltpu
from jax.sharding import PartitionSpec as P

EPSILON = 0.1
GROUP = 8
SIDE = 2
HIGHEST = lax.Precision.HIGHEST


def from_partner(x, axis, distance):
    return lax.ppermute(x, axis, [(i, i ^ 1 << distance) for i in range(lax.axis_size(axis))])


SMALL = 0.06


def matmul(a, b, precision=HIGHEST):
    return lax.dot_general(
        a, b, (((1,), (0,)), ((), ())), precision=precision, preferred_element_type=jnp.float32
    )


def matmul_t(a, b, precision=HIGHEST):
    return lax.dot_general(
        a, b, (((1,), (1,)), ((), ())), precision=precision, preferred_element_type=jnp.float32
    )


def join(parts, axis):
    return jnp.concatenate(parts, axis=axis)


def halves(x):
    high = x.astype(jnp.bfloat16)
    return high, (x - high.astype(jnp.float32)).astype(jnp.bfloat16)


def thirds(x):
    high = x.astype(jnp.bfloat16)
    rest = x - high.astype(jnp.float32)
    return (high,) + halves(rest)


def positions(shape):
    return (
        lax.broadcasted_iota(jnp.int32, shape, 0),
        lax.broadcasted_iota(jnp.int32, shape, 1),
    )


def unit(rank):
    row, column = positions((rank, rank))
    return jnp.where(row == column, 1.0, 0.0).astype(jnp.float32)


def upper(x):
    row, column = positions(x.shape)
    return jnp.where(row <= column, x, 0.0)


def half_lower(x):
    row, column = positions(x.shape)
    return jnp.where(row > column, x, jnp.where(row == column, 0.5 * x, 0.0))


def gram_of(parts):
    f, g, h = parts
    return matmul_t(join([f, f, g, g, f, h], 1), join([f, g, f, g, h, f], 1), None)


def right_side(parts):
    f, g, h = parts
    return join([f, f, g, g, h, f], 0)


def left_side(x):
    f, g, h = thirds(x)
    first = join([f, g], 1)
    return join([first, first, join([f, h], 1)], 1)


def near_gram(x, y):
    f, g = halves(x)
    u, v = halves(y)
    return matmul_t(join([f, f, g], 1), join([u, v, u], 1), None)


def near_unit_factor(excess):
    x = half_lower(excess)
    square = matmul(x, x, None)
    x = half_lower(excess - matmul_t(x, x, None))
    return x, x - square


def sum_of(parts):
    while len(parts) > 1:
        parts = [sum(parts[i : i + 2]) for i in range(0, len(parts), 2)]
    return parts[0]


def not_small(norm):
    return jnp.logical_not(norm[0, 0] <= SMALL * SMALL)


def batch_rows(work, rank, batch, low, high, width=8):
    shape = (batch, 2 * rank)

    def lane(values, index):
        return jnp.broadcast_to(values[:, rank + index : rank + index + 1], shape)

    for start in range(low, high, width):
        rows = [work[(start + i) * batch : (start + i + 1) * batch, :] for i in range(width)]
        scalars = [
            [lane(rows[i], start + j) if j >= i else None for j in range(width)]
            for i in range(width)
        ]
        for j in range(width):
            root = lax.rsqrt(scalars[j][j])
            rows[j] = rows[j] * root
            factor = [None if i <= j else scalars[j][i] * root for i in range(width)]
            for i in range(j + 1, width):
                rows[i] = rows[i] - factor[i] * rows[j]
                for k in range(i, width):
                    scalars[i][k] = scalars[i][k] - factor[i] * factor[k]
            work[(start + j) * batch : (start + j + 1) * batch, :] = rows[j]
        for lower in range(start + width, high):
            total = work[lower * batch : (lower + 1) * batch, :]
            for j in range(width):
                total = total - lane(rows[j], lower) * rows[j]
            work[lower * batch : (lower + 1) * batch, :] = total


def batch_update(work, rank, batch, low, high):
    size = high - low
    each = 128 // size
    row, column = positions((128, 128))
    for first in range(0, batch, each):
        done = join(
            [work[pl.ds(low * batch + first + i, size, stride=batch), :] for i in range(each)], 0
        )
        turned = done.T
        right = right_side(thirds(done))
        for top in range(high, rank, size):
            factor = join([turned[rank + top : rank + top + size, :]] * each, 0)
            f, g, h = thirds(jnp.where(row // size == column // size, factor, 0.0))
            change = matmul(join([f, g, f, g, f, h], 1), right, None)
            for i in range(each):
                place = pl.ds(top * batch + first + i, size, stride=batch)
                work[place, :] = work[place, :] - change[i * size : (i + 1) * size]


def eliminate_batch(work, rank, batch):
    half = rank // 2
    batch_rows(work, rank, batch, 0, half)
    batch_update(work, rank, batch, 0, half)
    batch_rows(work, rank, batch, half, rank)


def eliminate_single(work, rank):
    shape = (8, 2 * rank)
    row, _ = positions(shape)
    for start in range(0, rank, 8):
        blocks = {m: work[m : m + 8, :] for m in range(start, rank, 8)}
        columns = {
            m: [
                jnp.broadcast_to(blocks[m][:, rank + start + j : rank + start + j + 1], shape)
                for j in range(8)
            ]
            for m in blocks
        }
        done = blocks[start]
        for j in range(8):
            root = lax.rsqrt(columns[start][j][j : j + 1, :])
            line = [columns[start][i][j : j + 1, :] * root for i in range(8)]
            scaled = blocks[start][j : j + 1, :] * root
            done = jnp.where(row == j, scaled, done)
            for m in blocks:
                factor = columns[m][j] * root
                blocks[m] = blocks[m] - factor * scaled
                for i in range(j + 1, 8):
                    columns[m][i] = columns[m][i] - factor * line[i]
        work[start : start + 8, :] = done
        for m in blocks:
            if m > start:
                work[m : m + 8, :] = blocks[m]


def parity(axis):
    return lax.axis_index(axis) % 2


def to_neighbours(low, high, axis):
    size = lax.axis_size(axis)
    even = parity(axis) == 0
    received = []
    if size > 2:
        across = [(i, i + 1) for i in range(1, size - 1, 2)]
        across = across + [(j, i) for i, j in across]
        received.append(lax.ppermute(jnp.where(even, low, high), axis, across))
    pairs = [(i, i ^ 1) for i in range(size)]
    received.append(lax.ppermute(jnp.where(even, high, low), axis, pairs))
    return received[::-1]


def halo_count(axis):
    return 1 if lax.axis_size(axis) == 2 else 2


def leaf_index(x, y, z):
    return (x * SIDE + y) * SIDE + z


def pair_tables(halos):
    depth = SIDE + halos[2]
    stages = ([], [], [], [])
    for a in range(SIDE**3):
        place = (a // 4, a // 2 % 2, a % 2)
        for k in range(27):
            at = [p + d for p, d in zip(place, (k // 9 - 1, k // 3 % 3 - 1, k % 3 - 1))]
            sides = tuple((axis, t) for axis, t in enumerate(at) if t in (-1, 2))
            x, y, z = (2 if t == -1 else t for t in at)
            if at[0] == -1:
                stages[3].append((a, k, y * depth + z, sides[1:], True))
            elif at[0] == 2:
                continue
            elif y == 2:
                stages[2].append((a, k, x * depth + z, sides, False))
            elif z == 2:
                stages[1].append((a, k, SIDE**3 + x * SIDE + y, sides, False))
            else:
                stages[a * 2 // SIDE**3].append((a, k, leaf_index(x, y, z), sides, False))
    return stages


def far_sides(halos):
    found = {}
    for axis, name in enumerate(("gx", "gy", "gz")):
        place = lax.axis_index(name)
        odd = place % 2
        other = halos[axis] - 1
        found[axis, -1] = ((place > 0).astype(jnp.int32), (1 - odd) * other)
        found[axis, 2] = ((place < lax.axis_size(name) - 1).astype(jnp.int32), odd * other)
    return found


def list_pairs(pairs, halos, near, listed, count, x_side):
    found = far_sides(halos)
    depth = SIDE + halos[2]
    joint = {}
    for a, k, source, sides, across in pairs:
        key = (sides, across)
        if key not in joint:
            inside, moved, entry = jnp.int32(1), jnp.int32(0), jnp.int32(0)
            if across:
                steps = {1: depth, 2: 1}
                inside = x_side[1]
                entry = x_side[0] * (4 * 27 + 18)
            elif any(axis == 1 for axis, _ in sides):
                steps = {1: SIDE * depth, 2: 1}
            else:
                steps = {2: SIDE * SIDE}
            for side in sides:
                inside = inside * found[side][0]
                moved = moved + found[side][1] * steps[side[0]]
            joint[key] = (inside, moved * (16 * 27) + entry, entry)
        inside, moved, entry = joint[key]
        code = jnp.int32((source * 16 + a) * 27 + k)
        if sides or across:
            taken = near[a * 27 + k + entry] * inside
            code = code + moved
        else:
            taken = near[a * 27 + k]
        listed[count] = code
        count = count + taken
    return count


def close_list(listed, count, blank):
    for i in range(GROUP):
        listed[count + i] = jnp.int32(blank)
    return lax.div(count + (GROUP - 1), jnp.int32(GROUP))


def spread_offsets(blocks, count, turned, spread):
    rank3 = blocks.shape[1] - 16
    turned[...] = jnp.zeros_like(turned)
    for s in range(count):
        turned[4 * s : 4 * s + 4, :] = blocks[s, rank3:, :].astype(jnp.float32)[:4]
    columns = turned[...].T.astype(jnp.bfloat16)
    row, lane = positions((128, 384))
    for s in range(count):
        chosen = jnp.where(row == 4 * s + lane // 128, 1.0, 0.0).astype(jnp.bfloat16)
        values = matmul(columns, chosen, None)
        for p in range(3):
            spread[s, p] = values[:, 128 * p : 128 * (p + 1)]


def tile_rows(own, spread, rows):
    r = [own[p] - spread[p, rows, :] for p in range(3)]
    squares = [v * v for v in r]
    softened = squares[0] + squares[1] + squares[2] + EPSILON * EPSILON
    lifted = softened + EPSILON * EPSILON
    root = lax.rsqrt(softened)
    h = root * root * root
    ry, rz = r[1] * h, r[2] * h
    tiles = {(p, p): (squares[p] + lifted) * h for p in range(3)}
    tiles[0, 1], tiles[0, 2], tiles[1, 2] = r[0] * ry, r[0] * rz, r[1] * rz
    return {pq: tile.astype(jnp.bfloat16) for pq, tile in tiles.items()}


def add_pairs(groups, listed, blocks, own, spread, total):
    chunk = 16

    @pl.loop(0, groups)
    def _(group):
        for u in range(GROUP):
            code = listed[group * GROUP + u]
            pair = lax.div(code, jnp.int32(27))
            k = code - pair * 27
            source = lax.shift_right_logical(pair, jnp.int32(4))
            a = lax.bitwise_and(pair, jnp.int32(15))
            dx = lax.div(k, jnp.int32(9))
            dy = lax.div(k, jnp.int32(3)) - dx * 3
            dz = k - dx * 9 - dy * 3
            own_rows = own[a]
            placed = [
                jnp.broadcast_to(
                    own_rows[p : p + 1] + (1 - step).astype(jnp.float32), (chunk, 128)
                )
                for p, step in enumerate((dx, dy, dz))
            ]
            parts = [
                tile_rows(placed, spread.at[source], pl.ds(j, chunk))
                for j in range(0, 128, chunk)
            ]
            tiles = {
                pq: jnp.concatenate([part[pq] for part in parts], axis=0) for pq in parts[0]
            }
            matrix = jnp.concatenate(
                [
                    jnp.concatenate([tiles[min(p, q), max(p, q)] for p in range(3)], axis=1)
                    for q in range(3)
                ],
                axis=0,
            )
            rank = total.shape[1]
            sampled = jnp.concatenate(
                [blocks[source, q * rank : (q + 1) * rank, :] for q in range(3)], axis=1
            )
            total[a] += matmul(sampled, matrix, None)


def fetch(parts, blocks, semaphore):
    copies = []
    first = 0
    for i, part in enumerate(parts):
        copies.append(
            pltpu.make_async_copy(
                part, blocks.at[pl.ds(first, part.shape[0])], semaphore.at[i]
            )
        )
        copies[-1].start()
        first += part.shape[0]
    return copies, first


def list_stage(stage, near, listed, blank):
    halos, lists = stage
    odd = lax.axis_index("gx") % 2
    size = lax.axis_size("gx")
    start = jnp.int32(0)
    for pairs, first, within in lists:
        pairs = [(a, k, source + first, sides, across) for a, k, source, sides, across in pairs]
        x_side = None
        if within is True:
            x_side = (1 - odd, jnp.int32(1))
        elif within is False:
            place = lax.axis_index("gx")
            inside = jnp.logical_and(place > 0, place < size - 1).astype(jnp.int32)
            x_side = (odd, inside)
        start = list_pairs(pairs, halos, near, listed, start, x_side)
    return close_list(listed, start, blank)


def near_stage(stage, near, own, parts, total, listed, blocks, turned, spread, semaphore):
    copies, count = fetch(parts, blocks, semaphore)
    groups = list_stage(stage, near, listed, count * 16 * 27 + 13)
    blocks[count] = jnp.zeros_like(blocks[count])
    for copy in copies:
        copy.wait()
    spread_offsets(blocks, count, turned, spread)
    spread[count] = jnp.zeros_like(spread[count])
    add_pairs(groups, listed, blocks, own, spread, total)


def first_kernel(stage, near, own, own_blocks, total, *scratch):
    total[...] = jnp.zeros_like(total)
    near_stage(stage, near, own, [own_blocks], total, *scratch)


def next_kernel(stage, near, own, before, *rest):
    *parts, total, listed, blocks, turned, spread, semaphore = rest
    total[...] = before[...]
    near_stage(stage, near, own, parts, total, listed, blocks, turned, spread, semaphore)


def last_kernel(stage, near, own, before, sketch, *rest):
    *parts, far, grams, factor, samples, z_out = rest[:-5]
    listed, turned, spread, total, single = rest[-5:]
    count = far.shape[0]
    total[:count] = before[...]
    for blocks in parts:
        groups = list_stage(stage, near, listed, count * 27 + 13)
        spread_offsets(blocks, blocks.shape[0], turned, spread)
        add_pairs(groups, listed, blocks, own, spread, total)
    far[...] = sketch[...] - total[:count]
    box_level(far, grams, factor, samples, z_out, single)


def pack_kernel(samples, offsets, packed, own, *faces):
    count, rank, leaf_rows = samples.shape
    filler = jnp.zeros((13, 128), jnp.float32)
    for a in range(count):
        for q in range(3):
            packed[a, q * rank : (q + 1) * rank, :] = samples[a, :, q * 128 : (q + 1) * 128]
        rows = jnp.concatenate([offsets[a].astype(jnp.float32), filler], axis=0)
        packed[a, 3 * rank :, :] = rows.astype(jnp.bfloat16)
        own[a] = rows[:8]
    own[count] = jnp.zeros_like(own[count])
    planes = [1 - parity("gz"), parity("gz")]
    for face, plane in zip(faces, planes):
        for column in range(SIDE * SIDE):
            face[column] = packed[column * SIDE + plane]


VMEM_LIMIT = 48 * 1024 * 1024


def near_scratch(stage, count, block):
    length = sum(len(pairs) for pairs, _, _ in stage[1])
    return [
        pltpu.SMEM((length + GROUP + 1,), jnp.int32),
        pltpu.VMEM((count + 1,) + block, jnp.bfloat16),
        pltpu.VMEM((128, 128), jnp.float32),
        pltpu.VMEM((count + 1, 3, 128, 128), jnp.float32),
        pltpu.SemaphoreType.DMA((4,)),
    ]


def cost(microseconds):
    return pl.CostEstimate(
        flops=microseconds * 1000 * 1000 * 1000, bytes_accessed=4 * 1024 * 1024, transcendentals=0
    )


IN_SMEM = pl.BlockSpec(memory_space=pltpu.SMEM)
IN_VMEM = pl.BlockSpec(memory_space=pltpu.VMEM)
ANYWHERE = pl.BlockSpec(memory_space=pl.ANY)


def box_level(far, grams_out, factor_out, samples_out, z_out, single):
    count, rank, _ = far.shape
    eye = unit(rank)
    grams = [gram_of(thirds(far[a])) for a in range(count)]
    for a in range(count):
        grams_out[a] = grams[a]
    total = sum_of(grams)
    single[...] = join([eye, 0.5 * (total + total.T)], 1)
    eliminate_single(single, rank)
    left = left_side(single[:, :rank])
    lower = upper(single[:, rank:]).T
    samples = [matmul(left, right_side(thirds(far[a])), None) for a in range(count)]
    grams = [near_gram(rows, rows) for rows in samples]
    for a in range(count):
        samples_out[a] = samples[a]
    excess = sum_of(grams) - eye
    x, z_out[...] = near_unit_factor(excess)
    factor_out[...] = lower + matmul(left_side(lower), right_side(thirds(x)), None)

    @pl.when(not_small(jnp.sum(excess * excess, keepdims=True)))
    def _():
        single[...] = join([eye, eye + excess], 1)
        eliminate_single(single, rank)
        factor_out[...] = matmul(lower, upper(single[:, rank:]).T)
        for a in range(count):
            samples_out[a] = matmul(single[:, :rank], samples_out[a])
        z_out[...] = jnp.zeros_like(eye)


def leaf_factors(grams, work):
    count, rank, _ = grams.shape
    eye = unit(rank)
    for a in range(count):
        work[pl.ds(a, rank, stride=count), :] = join([eye, grams[a]], 1)
    eliminate_batch(work, rank, count)


def leaf_kernel(far, factors, samples, box_z, leaf_out, level_out, work, blocks, es, zs):
    count, rank, leaf_rows = far.shape
    eye = unit(rank)
    inverses = [factors[pl.ds(a, rank, stride=count), :][:, :rank] for a in range(count)]
    bases = [
        matmul(left_side(inverses[a]), right_side(thirds(far[a])), None) for a in range(count)
    ]
    products = [near_gram(join([bases[a], samples[a]], 0), bases[a]) for a in range(count)]
    excesses = [product[:rank] - eye for product in products]
    for a in range(count):
        leaf_out[a] = bases[a]
        blocks[a] = products[a][rank:]
        es[a] = excesses[a]
    inverse_parts = [near_unit_factor(excess)[1] for excess in excesses]
    for a in range(count):
        zs[a] = inverse_parts[a]
    norms = [jnp.sum(excess * excess, keepdims=True) for excess in excesses]
    largest = functools.reduce(jnp.maximum, norms)

    @pl.when(not_small(largest))
    def _():
        for a in range(count):
            work[pl.ds(a, rank, stride=count), :] = join([eye, eye + es[a]], 1)
        eliminate_batch(work, rank, count)
        for a in range(count):
            inverse = work[pl.ds(a, rank, stride=count), :][:, :rank]
            leaf_out[a] = matmul(inverse, leaf_out[a])
            blocks[a] = matmul_t(blocks[a], inverse)
            zs[a] = jnp.zeros_like(eye)

    bases = [leaf_out[a] for a in range(count)]
    bases = [basis - matmul(zs[a], basis, None) for a, basis in enumerate(bases)]
    crossed = [blocks[a] for a in range(count)]
    crossed = [block - matmul_t(block, zs[a], None) for a, block in enumerate(crossed)]
    for a in range(count):
        leaf_out[a] = bases[a] * math.sqrt(leaf_rows)
    block = join(crossed, 1) * math.sqrt(count * rank)
    level_out[...] = block - matmul(box_z[...], block, None)


def group_kernel(factors, samples, box_z, nested_out, single, stack):
    count, rank, _ = factors.shape
    eye = unit(rank)
    for b in range(count):
        stack[:, b * rank : (b + 1) * rank] = factors[b]
    parts = thirds(stack[...])
    gram = gram_of(parts)
    single[...] = join([eye, 0.5 * (gram + gram.T)], 1)
    eliminate_single(single, rank)
    block = matmul(left_side(single[:, :rank]), right_side(parts), None)
    excess = near_gram(block, block) - eye
    own = block[:, :rank] * (8.0 * math.sqrt(samples.shape[2]))
    own = own - matmul(own, box_z[...], None)
    left = join(halves(own) * 2, 1)
    leaves = range(samples.shape[0])
    parts = [halves(samples[a]) for a in leaves]
    mixed = [matmul(left, join([f, f, g, g], 0), None) for f, g in parts]
    z = near_unit_factor(excess)[1]
    nested = [rows - matmul(z, rows, None) for rows in mixed]
    for a in leaves:
        nested_out[a] = nested[a]

    @pl.when(not_small(jnp.sum(excess * excess, keepdims=True)))
    def _():
        single[...] = join([eye, eye + excess], 1)
        eliminate_single(single, rank)
        left = join(halves(matmul(single[:, :rank], own)) * 2, 1)
        for a in leaves:
            f, g = halves(samples[a])
            nested_out[a] = matmul(left, join([f, f, g, g], 0), None)


def body(sketch, test_matrix, offsets, near):
    rank, leaf_rows = sketch.shape[3:]
    count = SIDE**3
    halos = [halo_count(axis) for axis in ("gx", "gy", "gz")]
    like = jax.ShapeDtypeStruct
    block = (3 * rank + 16, 128)
    params = pltpu.CompilerParams(vmem_limit_bytes=VMEM_LIMIT)
    flat_near = near.reshape(count * 27)
    flat_sketch = sketch.reshape(count, rank, leaf_rows)
    stages = pair_tables(halos)
    faces = halos[2]
    packed, own, *sent = pl.pallas_call(
        pack_kernel,
        out_shape=(
            like((count,) + block, jnp.bfloat16),
            like((count + 1, 8, 128), jnp.float32),
        )
        + (like((SIDE * SIDE,) + block, jnp.bfloat16),) * faces,
        compiler_params=params,
        name="pack",
    )(test_matrix.reshape(count, rank, leaf_rows), offsets.reshape(count, 3, 128))
    z_halos = [from_partner(sent[0], "gz", 0)]
    if faces == 2:
        size = lax.axis_size("gz")
        across = [(i, i + 1) for i in range(1, size - 1, 2)]
        across = across + [(j, i) for i, j in across]
        z_halos.append(lax.ppermute(sent[1], "gz", across))
    inner = packed.reshape((SIDE, SIDE, SIDE) + block)
    columns = [h.reshape((SIDE, SIDE, 1) + block) for h in z_halos]
    extended = join([inner] + columns, 2)
    depth = extended.shape[2]
    flat = lambda parts: [x.reshape((-1,) + block) for x in parts]
    column = (SIDE + halos[1]) * depth
    y_blocks = SIDE * depth * halos[1]
    whole = like((count, rank, leaf_rows), jnp.float32)
    squares = like((count, rank, rank), jnp.float32)
    square = like((rank, rank), jnp.float32)
    single_scratch = pltpu.VMEM((rank, 2 * rank), jnp.float32)

    stage = (halos, [(stages[0], 0, None)])
    total = pl.pallas_call(
        functools.partial(first_kernel, stage),
        out_shape=whole,
        in_specs=[IN_SMEM, IN_VMEM, ANYWHERE],
        scratch_shapes=near_scratch(stage, count, block),
        cost_estimate=cost(4),
        compiler_params=params,
        name="near_inner",
    )(flat_near, own, packed)

    extended, total = lax.optimization_barrier((extended, total))
    y_halos = to_neighbours(extended[:, 0], extended[:, 1], "gy")

    def add_stage(stage, total, parts, name, time):
        return pl.pallas_call(
            functools.partial(next_kernel, stage),
            out_shape=whole,
            in_specs=[IN_SMEM, IN_VMEM, IN_VMEM] + [ANYWHERE] * len(parts),
            scratch_shapes=near_scratch(stage, sum(part.shape[0] for part in parts), block),
            cost_estimate=cost(time),
            compiler_params=params,
            name=name,
        )(flat_near, own, total, *parts)

    stage = (halos, [(stages[1], 0, None)])
    total = add_stage(stage, total, [packed] + flat(z_halos), "near_inner_and_z", 5)
    wide = join([extended] + [h[:, None] for h in y_halos], 1)
    wide, total = lax.optimization_barrier((wide, total))
    x_halos = to_neighbours(wide[0], wide[1], "gx")
    stage = (halos, [(stages[2], 0, None), (stages[3], y_blocks, True)])
    total = add_stage(stage, total, flat(y_halos) + flat(x_halos[:1]), "near_y_and_x", 7)
    stage = (halos, [(stages[3], 0, False)] if halos[0] == 2 else [])
    parts = flat(x_halos[1:])
    far, grams, factor, samples, box_z = pl.pallas_call(
        functools.partial(last_kernel, stage),
        out_shape=(whole, squares, square, whole, square),
        in_specs=[IN_SMEM, IN_VMEM, IN_VMEM, IN_VMEM] + [IN_VMEM] * len(parts),
        scratch_shapes=[
            pltpu.SMEM((len(stages[3]) + GROUP + 1,), jnp.int32),
            pltpu.VMEM((128, 128), jnp.float32),
            pltpu.VMEM((column, 3, 128, 128), jnp.float32),
            pltpu.VMEM((count + 1, rank, leaf_rows), jnp.float32),
            single_scratch,
        ],
        compiler_params=params,
        name="near_x_and_box_level",
    )(flat_near, own, total, flat_sketch, *parts)
    grouped = factor[None]
    grouped = join([grouped, from_partner(grouped, "gz", 0)], 0)
    factors = pl.pallas_call(
        leaf_factors,
        out_shape=like((rank * count, 2 * rank), jnp.float32),
        cost_estimate=cost(3),
        compiler_params=params,
        name="leaf_factors",
    )(grams)
    grouped, factors = lax.optimization_barrier((grouped, factors))
    grouped = join([grouped, from_partner(grouped, "gy", 0)], 0)
    leaf_t, level_t = pl.pallas_call(
        leaf_kernel,
        out_shape=(whole, like((rank, count * rank), jnp.float32)),
        scratch_shapes=[pltpu.VMEM((rank * count, 2 * rank), jnp.float32)]
        + [pltpu.VMEM((count, rank, rank), jnp.float32)] * 3,
        cost_estimate=cost(4),
        compiler_params=params,
        name="leaf_level",
    )(far, factors, samples, box_z)
    grouped, leaf_t, level_t = lax.optimization_barrier((grouped, leaf_t, level_t))
    grouped = join([grouped, from_partner(grouped, "gx", 0)], 0)
    nested = pl.pallas_call(
        group_kernel,
        out_shape=whole,
        scratch_shapes=[
            single_scratch,
            pltpu.VMEM((rank, count * rank), jnp.float32),
        ],
        compiler_params=params,
        name="group_level",
    )(grouped, samples, box_z)
    return (leaf_t.reshape(sketch.shape), level_t[None, None, None], nested.reshape(sketch.shape))


def solution(mesh):
    placed = (
        P("gx", "gy", "gz", None, None),
        P("gx", "gy", "gz", None, None),
        P("gx", "gy", "gz", None, None),
        P("gx", "gy", "gz", None),
    )
    return jax.shard_map(
        body,
        mesh=mesh,
        in_specs=placed,
        out_specs=(
            P("gx", "gy", "gz", None, None),
            P("gx", "gy", "gz", None, None),
            P("gx", "gy", "gz", None, None),
        ),
        check_vma=False,
    )
```

```python
import functools
import math

import jax
import jax.numpy as jnp
from jax import lax
from jax.experimental import pallas as pl
from jax.experimental.pallas import tpu as pltpu
from jax.sharding import PartitionSpec as P

EPSILON = 0.1
GROUP = 8
SIDE = 2
HIGHEST = lax.Precision.HIGHEST


def from_partner(x, axis, distance):
    return lax.ppermute(x, axis, [(i, i ^ 1 << distance) for i in range(lax.axis_size(axis))])


SMALL = 0.06


def matmul(a, b, precision=HIGHEST):
    return lax.dot_general(
        a, b, (((1,), (0,)), ((), ())), precision=precision, preferred_element_type=jnp.float32
    )


def matmul_t(a, b, precision=HIGHEST):
    return lax.dot_general(
        a, b, (((1,), (1,)), ((), ())), precision=precision, preferred_element_type=jnp.float32
    )


def join(parts, axis):
    return jnp.concatenate(parts, axis=axis)


def halves(x):
    high = x.astype(jnp.bfloat16)
    return high, (x - high.astype(jnp.float32)).astype(jnp.bfloat16)


def thirds(x):
    high = x.astype(jnp.bfloat16)
    rest = x - high.astype(jnp.float32)
    return (high,) + halves(rest)


def positions(shape):
    return (
        lax.broadcasted_iota(jnp.int32, shape, 0),
        lax.broadcasted_iota(jnp.int32, shape, 1),
    )


def unit(rank):
    row, column = positions((rank, rank))
    return jnp.where(row == column, 1.0, 0.0).astype(jnp.float32)


def upper(x):
    row, column = positions(x.shape)
    return jnp.where(row <= column, x, 0.0)


def half_lower(x):
    row, column = positions(x.shape)
    return jnp.where(row > column, x, jnp.where(row == column, 0.5 * x, 0.0))


def gram_of(parts):
    f, g, h = parts
    return matmul_t(join([f, f, g, g, f, h], 1), join([f, g, f, g, h, f], 1), None)


def right_side(parts):
    f, g, h = parts
    return join([f, f, g, g, h, f], 0)


def left_side(x):
    f, g, h = thirds(x)
    first = join([f, g], 1)
    return join([first, first, join([f, h], 1)], 1)


def near_gram(x, y):
    f, g = halves(x)
    u, v = halves(y)
    return matmul_t(join([f, f, g], 1), join([u, v, u], 1), None)


def near_unit_factor(excess):
    x = half_lower(excess)
    square = matmul(x, x, None)
    x = half_lower(excess - matmul_t(x, x, None))
    return x, x - square


def sum_of(parts):
    while len(parts) > 1:
        parts = [sum(parts[i : i + 2]) for i in range(0, len(parts), 2)]
    return parts[0]


def not_small(norm):
    return jnp.logical_not(norm[0, 0] <= SMALL * SMALL)


def batch_rows(work, rank, batch, low, high, width=8):
    shape = (batch, 2 * rank)

    def lane(values, index):
        return jnp.broadcast_to(values[:, rank + index : rank + index + 1], shape)

    for start in range(low, high, width):
        rows = [work[(start + i) * batch : (start + i + 1) * batch, :] for i in range(width)]
        scalars = [
            [lane(rows[i], start + j) if j >= i else None for j in range(width)]
            for i in range(width)
        ]
        for j in range(width):
            root = lax.rsqrt(scalars[j][j])
            rows[j] = rows[j] * root
            factor = [None if i <= j else scalars[j][i] * root for i in range(width)]
            for i in range(j + 1, width):
                rows[i] = rows[i] - factor[i] * rows[j]
                for k in range(i, width):
                    scalars[i][k] = scalars[i][k] - factor[i] * factor[k]
            work[(start + j) * batch : (start + j + 1) * batch, :] = rows[j]
        for lower in range(start + width, high):
            total = work[lower * batch : (lower + 1) * batch, :]
            for j in range(width):
                total = total - lane(rows[j], lower) * rows[j]
            work[lower * batch : (lower + 1) * batch, :] = total


def batch_update(work, rank, batch, low, high):
    size = high - low
    each = 128 // size
    row, column = positions((128, 128))
    for first in range(0, batch, each):
        done = join(
            [work[pl.ds(low * batch + first + i, size, stride=batch), :] for i in range(each)], 0
        )
        turned = done.T
        right = right_side(thirds(done))
        for top in range(high, rank, size):
            factor = join([turned[rank + top : rank + top + size, :]] * each, 0)
            f, g, h = thirds(jnp.where(row // size == column // size, factor, 0.0))
            change = matmul(join([f, g, f, g, f, h], 1), right, None)
            for i in range(each):
                place = pl.ds(top * batch + first + i, size, stride=batch)
                work[place, :] = work[place, :] - change[i * size : (i + 1) * size]


def eliminate_batch(work, rank, batch):
    half = rank // 2
    batch_rows(work, rank, batch, 0, half)
    batch_update(work, rank, batch, 0, half)
    batch_rows(work, rank, batch, half, rank)


def eliminate_single(work, rank):
    shape = (8, 2 * rank)
    row, _ = positions(shape)
    for start in range(0, rank, 8):
        blocks = {m: work[m : m + 8, :] for m in range(start, rank, 8)}
        columns = {
            m: [
                jnp.broadcast_to(blocks[m][:, rank + start + j : rank + start + j + 1], shape)
                for j in range(8)
            ]
            for m in blocks
        }
        done = blocks[start]
        for j in range(8):
            root = lax.rsqrt(columns[start][j][j : j + 1, :])
            line = [columns[start][i][j : j + 1, :] * root for i in range(8)]
            scaled = blocks[start][j : j + 1, :] * root
            done = jnp.where(row == j, scaled, done)
            for m in blocks:
                factor = columns[m][j] * root
                blocks[m] = blocks[m] - factor * scaled
                for i in range(j + 1, 8):
                    columns[m][i] = columns[m][i] - factor * line[i]
        work[start : start + 8, :] = done
        for m in blocks:
            if m > start:
                work[m : m + 8, :] = blocks[m]


def parity(axis):
    return lax.axis_index(axis) % 2


def to_neighbours(low, high, axis):
    size = lax.axis_size(axis)
    even = parity(axis) == 0
    received = []
    if size > 2:
        across = [(i, i + 1) for i in range(1, size - 1, 2)]
        across = across + [(j, i) for i, j in across]
        received.append(lax.ppermute(jnp.where(even, low, high), axis, across))
    pairs = [(i, i ^ 1) for i in range(size)]
    received.append(lax.ppermute(jnp.where(even, high, low), axis, pairs))
    return received[::-1]


def halo_count(axis):
    return 1 if lax.axis_size(axis) == 2 else 2


def leaf_index(x, y, z):
    return (x * SIDE + y) * SIDE + z


def pair_tables(halos):
    depth = SIDE + halos[2]
    wide = SIDE + halos[1]
    stages = ([], [], [], [])
    for a in range(SIDE**3):
        place = (a // 4, a // 2 % 2, a % 2)
        for k in range(27):
            at = [p + d for p, d in zip(place, (k // 9 - 1, k // 3 % 3 - 1, k % 3 - 1))]
            sides = tuple((axis, t) for axis, t in enumerate(at) if t in (-1, 2) and axis > 0)
            x, y, z = (2 if t == -1 else t for t in at)
            if at[0] == -1:
                stages[3].append((a, k, y * depth + z, sides, True))
            elif at[0] == 2:
                continue
            elif sides:
                stages[2].append((a, k, (x * wide + y) * depth + z, sides, False))
            else:
                stages[a * 2 // SIDE**3].append((a, k, leaf_index(x, y, z), sides, False))
    return stages


def far_sides(halos):
    found = {}
    for axis, name in enumerate(("gx", "gy", "gz")):
        place = lax.axis_index(name)
        odd = place % 2
        other = halos[axis] - 1
        found[axis, -1] = ((place > 0).astype(jnp.int32), (1 - odd) * other)
        found[axis, 2] = ((place < lax.axis_size(name) - 1).astype(jnp.int32), odd * other)
    return found


def list_pairs(pairs, halos, near, listed, count, x_side):
    found = far_sides(halos)
    depth = SIDE + halos[2]
    joint = {}
    for a, k, source, sides, across in pairs:
        key = (sides, across)
        if key not in joint:
            inside, moved, entry = jnp.int32(1), jnp.int32(0), jnp.int32(0)
            if across:
                inside = x_side[1]
                entry = x_side[0] * (4 * 27 + 18)
            steps = {1: depth, 2: 1}
            for side in sides:
                inside = inside * found[side][0]
                moved = moved + found[side][1] * steps[side[0]]
            joint[key] = (inside, moved * (16 * 27) + entry, entry)
        inside, moved, entry = joint[key]
        code = jnp.int32((source * 16 + a) * 27 + k)
        if sides or across:
            taken = near[a * 27 + k + entry] * inside
            code = code + moved
        else:
            taken = near[a * 27 + k]
        listed[count] = code
        count = count + taken
    return count


def close_list(listed, count, blank):
    for i in range(GROUP):
        listed[count + i] = jnp.int32(blank)
    return lax.div(count + (GROUP - 1), jnp.int32(GROUP))


def spread_offsets(blocks, places, turned, spread):
    rank3 = blocks.shape[1] - 16
    row, lane = positions((128, 384))
    for first in range(0, len(places), 32):
        chunk = places[first : first + 32]
        turned[...] = jnp.zeros_like(turned)
        for i, s in enumerate(chunk):
            turned[4 * i : 4 * i + 4, :] = blocks[s, rank3:, :].astype(jnp.float32)[:4]
        columns = turned[...].T.astype(jnp.bfloat16)
        for i, s in enumerate(chunk):
            chosen = jnp.where(row == 4 * i + lane // 128, 1.0, 0.0).astype(jnp.bfloat16)
            values = matmul(columns, chosen, None)
            for p in range(3):
                spread[s, p] = values[:, 128 * p : 128 * (p + 1)]


def tile_rows(own, spread, rows):
    r = [own[p] - spread[p, rows, :] for p in range(3)]
    squares = [v * v for v in r]
    softened = squares[0] + squares[1] + squares[2] + EPSILON * EPSILON
    lifted = softened + EPSILON * EPSILON
    root = lax.rsqrt(softened)
    h = root * root * root
    ry, rz = r[1] * h, r[2] * h
    tiles = {(p, p): (squares[p] + lifted) * h for p in range(3)}
    tiles[0, 1], tiles[0, 2], tiles[1, 2] = r[0] * ry, r[0] * rz, r[1] * rz
    return {pq: tile.astype(jnp.bfloat16) for pq, tile in tiles.items()}


def add_pairs(groups, listed, blocks, own, spread, total):
    chunk = 16

    @pl.loop(0, groups)
    def _(group):
        for u in range(GROUP):
            code = listed[group * GROUP + u]
            pair = lax.div(code, jnp.int32(27))
            k = code - pair * 27
            source = lax.shift_right_logical(pair, jnp.int32(4))
            a = lax.bitwise_and(pair, jnp.int32(15))
            dx = lax.div(k, jnp.int32(9))
            dy = lax.div(k, jnp.int32(3)) - dx * 3
            dz = k - dx * 9 - dy * 3
            own_rows = own[a]
            placed = [
                jnp.broadcast_to(
                    own_rows[p : p + 1] + (1 - step).astype(jnp.float32), (chunk, 128)
                )
                for p, step in enumerate((dx, dy, dz))
            ]
            parts = [
                tile_rows(placed, spread.at[source], pl.ds(j, chunk))
                for j in range(0, 128, chunk)
            ]
            tiles = {
                pq: jnp.concatenate([part[pq] for part in parts], axis=0) for pq in parts[0]
            }
            matrix = jnp.concatenate(
                [
                    jnp.concatenate([tiles[min(p, q), max(p, q)] for p in range(3)], axis=1)
                    for q in range(3)
                ],
                axis=0,
            )
            rank = total.shape[1]
            sampled = jnp.concatenate(
                [blocks[source, q * rank : (q + 1) * rank, :] for q in range(3)], axis=1
            )
            total[a] += matmul(sampled, matrix, None)


def list_stage(stage, near, listed, blank):
    halos, lists = stage
    odd = lax.axis_index("gx") % 2
    size = lax.axis_size("gx")
    start = jnp.int32(0)
    for pairs, first, within in lists:
        pairs = [(a, k, source + first, sides, across) for a, k, source, sides, across in pairs]
        x_side = None
        if within is True:
            x_side = (1 - odd, jnp.int32(1))
        elif within is False:
            place = lax.axis_index("gx")
            inside = jnp.logical_and(place > 0, place < size - 1).astype(jnp.int32)
            x_side = (odd, inside)
        start = list_pairs(pairs, halos, near, listed, start, x_side)
    return close_list(listed, start, blank)


def near_stage(stage, near, own, blocks, total, listed, turned, spread):
    groups = list_stage(stage, near, listed, (total.shape[0] - 1) * 27 + 13)
    places = sorted({first + pair[2] for pairs, first, _ in stage[1] for pair in pairs})
    spread_offsets(blocks, with_far_places(places, stage), turned, spread)
    add_pairs(groups, listed, blocks, own, spread, total)


def with_far_places(places, stage):
    halos, lists = stage
    depth = SIDE + halos[2]
    found = set(places)
    for pairs, first, _ in lists:
        for _, _, source, sides, _ in pairs:
            moves = [0]
            for axis, _ in sides:
                step = {1: depth, 2: 1}[axis] * (halos[axis] - 1)
                moves = moves + [move + step for move in moves]
            found.update(first + source + move for move in moves)
    return sorted(found)


def first_kernel(stage, near, own, blocks, total, *scratch):
    total[...] = jnp.zeros_like(total)
    near_stage(stage, near, own, blocks, total, *scratch)


def next_kernel(stage, near, own, blocks, before, total, *scratch):
    total[...] = before[...]
    near_stage(stage, near, own, blocks, total, *scratch)


def last_kernel(stage, near, own, before, sketch, *rest):
    *parts, far, grams, factor, samples, z_out = rest[:-5]
    total, single, *scratch = rest[-5:]
    total[...] = before[...]
    for blocks in parts:
        near_stage(stage, near, own, blocks, total, *scratch)
    far[...] = sketch[...] - total[: far.shape[0]]
    box_level(far, grams, factor, samples, z_out, single)


def pack_kernel(samples, offsets, packed, own, *faces):
    count, rank, leaf_rows = samples.shape
    filler = jnp.zeros((13, 128), jnp.float32)
    for a in range(count):
        for q in range(3):
            packed[a, q * rank : (q + 1) * rank, :] = samples[a, :, q * 128 : (q + 1) * 128]
        rows = jnp.concatenate([offsets[a].astype(jnp.float32), filler], axis=0)
        packed[a, 3 * rank :, :] = rows.astype(jnp.bfloat16)
        own[a] = rows[:8]
    own[count] = jnp.zeros_like(own[count])
    planes = [1 - parity("gz"), parity("gz")]
    for face, plane in zip(faces, planes):
        for column in range(SIDE * SIDE):
            face[column] = packed[column * SIDE + plane]


VMEM_LIMIT = 48 * 1024 * 1024


def near_scratch(stage, count):
    length = sum(len(pairs) for pairs, _, _ in stage[1])
    return [
        pltpu.SMEM((length + GROUP + 1,), jnp.int32),
        pltpu.VMEM((128, 128), jnp.float32),
        pltpu.VMEM((count, 3, 128, 128), jnp.float32),
    ]


def cost(microseconds):
    return pl.CostEstimate(
        flops=microseconds * 1000 * 1000 * 1000, bytes_accessed=4 * 1024 * 1024, transcendentals=0
    )


IN_SMEM = pl.BlockSpec(memory_space=pltpu.SMEM)
IN_VMEM = pl.BlockSpec(memory_space=pltpu.VMEM)


def box_level(far, grams_out, factor_out, samples_out, z_out, single):
    count, rank, _ = far.shape
    eye = unit(rank)
    grams = [gram_of(thirds(far[a])) for a in range(count)]
    for a in range(count):
        grams_out[a] = grams[a]
    total = sum_of(grams)
    single[...] = join([eye, 0.5 * (total + total.T)], 1)
    eliminate_single(single, rank)
    left = left_side(single[:, :rank])
    lower = upper(single[:, rank:]).T
    samples = [matmul(left, right_side(thirds(far[a])), None) for a in range(count)]
    grams = [near_gram(rows, rows) for rows in samples]
    for a in range(count):
        samples_out[a] = samples[a]
    excess = sum_of(grams) - eye
    x, z_out[...] = near_unit_factor(excess)
    factor_out[...] = lower + matmul(left_side(lower), right_side(thirds(x)), None)

    @pl.when(not_small(jnp.sum(excess * excess, keepdims=True)))
    def _():
        single[...] = join([eye, eye + excess], 1)
        eliminate_single(single, rank)
        factor_out[...] = matmul(lower, upper(single[:, rank:]).T)
        for a in range(count):
            samples_out[a] = matmul(single[:, :rank], samples_out[a])
        z_out[...] = jnp.zeros_like(eye)


def leaf_factors(grams, work):
    count, rank, _ = grams.shape
    eye = unit(rank)
    for a in range(count):
        work[pl.ds(a, rank, stride=count), :] = join([eye, grams[a]], 1)
    eliminate_batch(work, rank, count)


def leaf_kernel(far, factors, samples, box_z, leaf_out, level_out, work, blocks, es, zs):
    count, rank, leaf_rows = far.shape
    eye = unit(rank)
    inverses = [factors[pl.ds(a, rank, stride=count), :][:, :rank] for a in range(count)]
    bases = [
        matmul(left_side(inverses[a]), right_side(thirds(far[a])), None) for a in range(count)
    ]
    products = [near_gram(join([bases[a], samples[a]], 0), bases[a]) for a in range(count)]
    excesses = [product[:rank] - eye for product in products]
    for a in range(count):
        leaf_out[a] = bases[a]
        blocks[a] = products[a][rank:]
        es[a] = excesses[a]
    inverse_parts = [near_unit_factor(excess)[1] for excess in excesses]
    for a in range(count):
        zs[a] = inverse_parts[a]
    norms = [jnp.sum(excess * excess, keepdims=True) for excess in excesses]
    largest = functools.reduce(jnp.maximum, norms)

    @pl.when(not_small(largest))
    def _():
        for a in range(count):
            work[pl.ds(a, rank, stride=count), :] = join([eye, eye + es[a]], 1)
        eliminate_batch(work, rank, count)
        for a in range(count):
            inverse = work[pl.ds(a, rank, stride=count), :][:, :rank]
            leaf_out[a] = matmul(inverse, leaf_out[a])
            blocks[a] = matmul_t(blocks[a], inverse)
            zs[a] = jnp.zeros_like(eye)

    bases = [leaf_out[a] for a in range(count)]
    bases = [basis - matmul(zs[a], basis, None) for a, basis in enumerate(bases)]
    crossed = [blocks[a] for a in range(count)]
    crossed = [block - matmul_t(block, zs[a], None) for a, block in enumerate(crossed)]
    for a in range(count):
        leaf_out[a] = bases[a] * math.sqrt(leaf_rows)
    block = join(crossed, 1) * math.sqrt(count * rank)
    level_out[...] = block - matmul(box_z[...], block, None)


def group_kernel(factors, samples, box_z, nested_out, single, stack):
    count, rank, _ = factors.shape
    eye = unit(rank)
    for b in range(count):
        stack[:, b * rank : (b + 1) * rank] = factors[b]
    parts = thirds(stack[...])
    gram = gram_of(parts)
    single[...] = join([eye, 0.5 * (gram + gram.T)], 1)
    eliminate_single(single, rank)
    block = matmul(left_side(single[:, :rank]), right_side(parts), None)
    excess = near_gram(block, block) - eye
    own = block[:, :rank] * (8.0 * math.sqrt(samples.shape[2]))
    own = own - matmul(own, box_z[...], None)
    left = join(halves(own) * 2, 1)
    leaves = range(samples.shape[0])
    parts = [halves(samples[a]) for a in leaves]
    mixed = [matmul(left, join([f, f, g, g], 0), None) for f, g in parts]
    z = near_unit_factor(excess)[1]
    nested = [rows - matmul(z, rows, None) for rows in mixed]
    for a in leaves:
        nested_out[a] = nested[a]

    @pl.when(not_small(jnp.sum(excess * excess, keepdims=True)))
    def _():
        single[...] = join([eye, eye + excess], 1)
        eliminate_single(single, rank)
        left = join(halves(matmul(single[:, :rank], own)) * 2, 1)
        for a in leaves:
            f, g = halves(samples[a])
            nested_out[a] = matmul(left, join([f, f, g, g], 0), None)


def body(sketch, test_matrix, offsets, near):
    rank, leaf_rows = sketch.shape[3:]
    count = SIDE**3
    halos = [halo_count(axis) for axis in ("gx", "gy", "gz")]
    like = jax.ShapeDtypeStruct
    block = (3 * rank + 16, 128)
    params = pltpu.CompilerParams(vmem_limit_bytes=VMEM_LIMIT)
    flat_near = near.reshape(count * 27)
    flat_sketch = sketch.reshape(count, rank, leaf_rows)
    stages = pair_tables(halos)
    faces = halos[2]
    packed, own, *sent = pl.pallas_call(
        pack_kernel,
        out_shape=(
            like((count,) + block, jnp.bfloat16),
            like((count + 1, 8, 128), jnp.float32),
        )
        + (like((SIDE * SIDE,) + block, jnp.bfloat16),) * faces,
        compiler_params=params,
        name="pack",
    )(test_matrix.reshape(count, rank, leaf_rows), offsets.reshape(count, 3, 128))
    z_halos = [from_partner(sent[0], "gz", 0)]
    if faces == 2:
        size = lax.axis_size("gz")
        across = [(i, i + 1) for i in range(1, size - 1, 2)]
        across = across + [(j, i) for i, j in across]
        z_halos.append(lax.ppermute(sent[1], "gz", across))
    inner = packed.reshape((SIDE, SIDE, SIDE) + block)
    columns = [h.reshape((SIDE, SIDE, 1) + block) for h in z_halos]
    extended = join([inner] + columns, 2)
    depth = extended.shape[2]
    flat = lambda parts: [x.reshape((-1,) + block) for x in parts]
    column = (SIDE + halos[1]) * depth
    whole = like((count, rank, leaf_rows), jnp.float32)
    sums = like((count + 1, rank, leaf_rows), jnp.float32)
    squares = like((count, rank, rank), jnp.float32)
    square = like((rank, rank), jnp.float32)
    single_scratch = pltpu.VMEM((rank, 2 * rank), jnp.float32)

    def add_stage(stage, blocks, before, name, time):
        kernel = first_kernel if before is None else next_kernel
        before = [] if before is None else [before]
        return pl.pallas_call(
            functools.partial(kernel, stage),
            out_shape=sums,
            in_specs=[IN_SMEM, IN_VMEM, IN_VMEM] + [IN_VMEM] * len(before),
            scratch_shapes=near_scratch(stage, blocks.shape[0]),
            cost_estimate=cost(time),
            compiler_params=params,
            name=name,
        )(flat_near, own, blocks, *before)

    total = add_stage((halos, [(stages[0], 0, None)]), packed, None, "near_inner", 4)
    extended, total = lax.optimization_barrier((extended, total))
    y_halos = to_neighbours(extended[:, 0], extended[:, 1], "gy")
    total = add_stage((halos, [(stages[1], 0, None)]), packed, total, "near_inner_rest", 4)
    wide = join([extended] + [h[:, None] for h in y_halos], 1)
    wide, total = lax.optimization_barrier((wide, total))
    x_halos = to_neighbours(wide[0], wide[1], "gx")
    stage = (halos, [(stages[2], 0, None), (stages[3], SIDE * column, True)])
    blocks = join(flat([wide, x_halos[0]]), 0)
    total = add_stage(stage, blocks, total, "near_z_y_and_x", 9)
    stage = (halos, [(stages[3], 0, False)])
    parts = flat(x_halos[1:])
    far, grams, factor, samples, box_z = pl.pallas_call(
        functools.partial(last_kernel, stage),
        out_shape=(whole, squares, square, whole, square),
        in_specs=[IN_SMEM, IN_VMEM, IN_VMEM, IN_VMEM] + [IN_VMEM] * len(parts),
        scratch_shapes=[pltpu.VMEM(sums.shape, jnp.float32), single_scratch]
        + near_scratch(stage, column),
        compiler_params=params,
        name="near_x_and_box_level",
    )(flat_near, own, total, flat_sketch, *parts)
    grouped = factor[None]
    grouped = join([grouped, from_partner(grouped, "gz", 0)], 0)
    factors = pl.pallas_call(
        leaf_factors,
        out_shape=like((rank * count, 2 * rank), jnp.float32),
        cost_estimate=cost(3),
        compiler_params=params,
        name="leaf_factors",
    )(grams)
    grouped, factors = lax.optimization_barrier((grouped, factors))
    grouped = join([grouped, from_partner(grouped, "gy", 0)], 0)
    leaf_t, level_t = pl.pallas_call(
        leaf_kernel,
        out_shape=(whole, like((rank, count * rank), jnp.float32)),
        scratch_shapes=[pltpu.VMEM((rank * count, 2 * rank), jnp.float32)]
        + [pltpu.VMEM((count, rank, rank), jnp.float32)] * 3,
        cost_estimate=cost(4),
        compiler_params=params,
        name="leaf_level",
    )(far, factors, samples, box_z)
    grouped, leaf_t, level_t = lax.optimization_barrier((grouped, leaf_t, level_t))
    grouped = join([grouped, from_partner(grouped, "gx", 0)], 0)
    nested = pl.pallas_call(
        group_kernel,
        out_shape=whole,
        scratch_shapes=[
            single_scratch,
            pltpu.VMEM((rank, count * rank), jnp.float32),
        ],
        compiler_params=params,
        name="group_level",
    )(grouped, samples, box_z)
    return (leaf_t.reshape(sketch.shape), level_t[None, None, None], nested.reshape(sketch.shape))


def solution(mesh):
    placed = (
        P("gx", "gy", "gz", None, None),
        P("gx", "gy", "gz", None, None),
        P("gx", "gy", "gz", None, None),
        P("gx", "gy", "gz", None),
    )
    return jax.shard_map(
        body,
        mesh=mesh,
        in_specs=placed,
        out_specs=(
            P("gx", "gy", "gz", None, None),
            P("gx", "gy", "gz", None, None),
            P("gx", "gy", "gz", None, None),
        ),
        check_vma=False,
    )
```

```python
import functools
import math

import jax
import jax.numpy as jnp
from jax import lax
from jax.experimental import pallas as pl
from jax.experimental.pallas import tpu as pltpu
from jax.sharding import PartitionSpec as P

EPSILON = 0.1
GROUP = 8
SIDE = 2
HIGHEST = lax.Precision.HIGHEST


def from_partner(x, axis, distance):
    return lax.ppermute(x, axis, [(i, i ^ 1 << distance) for i in range(lax.axis_size(axis))])


SMALL = 0.06


def matmul(a, b, precision=HIGHEST):
    return lax.dot_general(
        a, b, (((1,), (0,)), ((), ())), precision=precision, preferred_element_type=jnp.float32
    )


def matmul_t(a, b, precision=HIGHEST):
    return lax.dot_general(
        a, b, (((1,), (1,)), ((), ())), precision=precision, preferred_element_type=jnp.float32
    )


def join(parts, axis):
    return jnp.concatenate(parts, axis=axis)


def halves(x):
    high = x.astype(jnp.bfloat16)
    return high, (x - high.astype(jnp.float32)).astype(jnp.bfloat16)


def thirds(x):
    high = x.astype(jnp.bfloat16)
    rest = x - high.astype(jnp.float32)
    return (high,) + halves(rest)


def positions(shape):
    return (
        lax.broadcasted_iota(jnp.int32, shape, 0),
        lax.broadcasted_iota(jnp.int32, shape, 1),
    )


def unit(rank):
    row, column = positions((rank, rank))
    return jnp.where(row == column, 1.0, 0.0).astype(jnp.float32)


def upper(x):
    row, column = positions(x.shape)
    return jnp.where(row <= column, x, 0.0)


def half_lower(x):
    row, column = positions(x.shape)
    return jnp.where(row > column, x, jnp.where(row == column, 0.5 * x, 0.0))


def gram_of(parts):
    f, g, h = parts
    return matmul_t(join([f, f, g, g, f, h], 1), join([f, g, f, g, h, f], 1), None)


def right_side(parts):
    f, g, h = parts
    return join([f, f, g, g, h, f], 0)


def left_side(x):
    f, g, h = thirds(x)
    first = join([f, g], 1)
    return join([first, first, join([f, h], 1)], 1)


def near_gram(x, y):
    f, g = halves(x)
    u, v = halves(y)
    return matmul_t(join([f, f, g], 1), join([u, v, u], 1), None)


def near_unit_factor(excess):
    x = half_lower(excess)
    square = matmul(x, x, None)
    x = half_lower(excess - matmul_t(x, x, None))
    return x, x - square


def sum_of(parts):
    while len(parts) > 1:
        parts = [sum(parts[i : i + 2]) for i in range(0, len(parts), 2)]
    return parts[0]


def not_small(norm):
    return jnp.logical_not(norm[0, 0] <= SMALL * SMALL)


def batch_rows(work, rank, batch, low, high, width=8):
    shape = (batch, 2 * rank)

    def lane(values, index):
        return jnp.broadcast_to(values[:, rank + index : rank + index + 1], shape)

    for start in range(low, high, width):
        rows = [work[(start + i) * batch : (start + i + 1) * batch, :] for i in range(width)]
        scalars = [
            [lane(rows[i], start + j) if j >= i else None for j in range(width)]
            for i in range(width)
        ]
        for j in range(width):
            root = lax.rsqrt(scalars[j][j])
            rows[j] = rows[j] * root
            factor = [None if i <= j else scalars[j][i] * root for i in range(width)]
            for i in range(j + 1, width):
                rows[i] = rows[i] - factor[i] * rows[j]
                for k in range(i, width):
                    scalars[i][k] = scalars[i][k] - factor[i] * factor[k]
            work[(start + j) * batch : (start + j + 1) * batch, :] = rows[j]
        for lower in range(start + width, high):
            total = work[lower * batch : (lower + 1) * batch, :]
            for j in range(width):
                total = total - lane(rows[j], lower) * rows[j]
            work[lower * batch : (lower + 1) * batch, :] = total


def batch_update(work, rank, batch, low, high):
    size = high - low
    each = 128 // size
    row, column = positions((128, 128))
    for first in range(0, batch, each):
        done = join(
            [work[pl.ds(low * batch + first + i, size, stride=batch), :] for i in range(each)], 0
        )
        turned = done.T
        right = right_side(thirds(done))
        for top in range(high, rank, size):
            factor = join([turned[rank + top : rank + top + size, :]] * each, 0)
            f, g, h = thirds(jnp.where(row // size == column // size, factor, 0.0))
            change = matmul(join([f, g, f, g, f, h], 1), right, None)
            for i in range(each):
                place = pl.ds(top * batch + first + i, size, stride=batch)
                work[place, :] = work[place, :] - change[i * size : (i + 1) * size]


def eliminate_batch(work, rank, batch):
    half = rank // 2
    batch_rows(work, rank, batch, 0, half)
    batch_update(work, rank, batch, 0, half)
    batch_rows(work, rank, batch, half, rank)


def eliminate_single(work, rank):
    shape = (8, 2 * rank)
    row, _ = positions(shape)
    for start in range(0, rank, 8):
        blocks = {m: work[m : m + 8, :] for m in range(start, rank, 8)}
        columns = {
            m: [
                jnp.broadcast_to(blocks[m][:, rank + start + j : rank + start + j + 1], shape)
                for j in range(8)
            ]
            for m in blocks
        }
        done = blocks[start]
        for j in range(8):
            root = lax.rsqrt(columns[start][j][j : j + 1, :])
            line = [columns[start][i][j : j + 1, :] * root for i in range(8)]
            scaled = blocks[start][j : j + 1, :] * root
            done = jnp.where(row == j, scaled, done)
            for m in blocks:
                factor = columns[m][j] * root
                blocks[m] = blocks[m] - factor * scaled
                for i in range(j + 1, 8):
                    columns[m][i] = columns[m][i] - factor * line[i]
        work[start : start + 8, :] = done
        for m in blocks:
            if m > start:
                work[m : m + 8, :] = blocks[m]


def parity(axis):
    return lax.axis_index(axis) % 2


def swap_within(low, high, axis):
    pairs = [(i, i ^ 1) for i in range(lax.axis_size(axis))]
    return lax.ppermute(jnp.where(parity(axis) == 0, high, low), axis, pairs)


def swap_across(low, high, axis):
    size = lax.axis_size(axis)
    if size == 2:
        return []
    across = [(i, i + 1) for i in range(1, size - 1, 2)]
    across = across + [(j, i) for i, j in across]
    return [lax.ppermute(jnp.where(parity(axis) == 0, low, high), axis, across)]


def to_neighbours(low, high, axis):
    return [swap_within(low, high, axis)] + swap_across(low, high, axis)


def halo_count(axis):
    return 1 if lax.axis_size(axis) == 2 else 2


def leaf_index(x, y, z):
    return (x * SIDE + y) * SIDE + z


def pair_tables(halos):
    depth = SIDE + halos[2]
    wide = SIDE + halos[1]
    stages = ([], [], [], [])
    for a in range(SIDE**3):
        place = (a // 4, a // 2 % 2, a % 2)
        for k in range(27):
            at = [p + d for p, d in zip(place, (k // 9 - 1, k // 3 % 3 - 1, k % 3 - 1))]
            sides = tuple((axis, t) for axis, t in enumerate(at) if t in (-1, 2) and axis > 0)
            x, y, z = (2 if t == -1 else t for t in at)
            if at[0] == -1:
                stages[3].append((a, k, y * depth + z, sides, True))
            elif at[0] == 2:
                continue
            elif y == 2:
                stages[2].append((a, k, (x * wide + y) * depth + z, sides, False))
            elif sides or a * 2 >= SIDE**3:
                stages[1].append((a, k, (x * SIDE + y) * depth + z, sides, False))
            else:
                stages[0].append((a, k, leaf_index(x, y, z), sides, False))
    return stages


def far_sides(halos):
    found = {}
    for axis, name in enumerate(("gx", "gy", "gz")):
        place = lax.axis_index(name)
        odd = place % 2
        other = halos[axis] - 1
        found[axis, -1] = ((place > 0).astype(jnp.int32), (1 - odd) * other)
        found[axis, 2] = ((place < lax.axis_size(name) - 1).astype(jnp.int32), odd * other)
    return found


def list_pairs(pairs, halos, near, listed, count, x_side):
    found = far_sides(halos)
    depth = SIDE + halos[2]
    joint = {}
    for a, k, source, sides, across in pairs:
        key = (sides, across)
        if key not in joint:
            inside, moved, entry = jnp.int32(1), jnp.int32(0), jnp.int32(0)
            if across:
                inside = x_side[1]
                entry = x_side[0] * (4 * 27 + 18)
            steps = {1: depth, 2: 1}
            for side in sides:
                inside = inside * found[side][0]
                moved = moved + found[side][1] * steps[side[0]]
            joint[key] = (inside, moved * (16 * 27) + entry, entry)
        inside, moved, entry = joint[key]
        code = jnp.int32((source * 16 + a) * 27 + k)
        if sides or across:
            taken = near[a * 27 + k + entry] * inside
            code = code + moved
        else:
            taken = near[a * 27 + k]
        listed[count] = code
        count = count + taken
    return count


def close_list(listed, count, blank):
    for i in range(GROUP):
        listed[count + i] = jnp.int32(blank)
    return lax.div(count + (GROUP - 1), jnp.int32(GROUP))


def spread_offsets(blocks, places, turned, spread):
    rank3 = blocks.shape[1] - 16
    row, lane = positions((128, 384))
    for first in range(0, len(places), 32):
        chunk = places[first : first + 32]
        turned[...] = jnp.zeros_like(turned)
        for i, s in enumerate(chunk):
            turned[4 * i : 4 * i + 4, :] = blocks[s, rank3:, :].astype(jnp.float32)[:4]
        columns = turned[...].T.astype(jnp.bfloat16)
        for i, s in enumerate(chunk):
            chosen = jnp.where(row == 4 * i + lane // 128, 1.0, 0.0).astype(jnp.bfloat16)
            values = matmul(columns, chosen, None)
            for p in range(3):
                spread[s, p] = values[:, 128 * p : 128 * (p + 1)]


def tile_rows(own, spread, rows):
    r = [own[p] - spread[p, rows, :] for p in range(3)]
    squares = [v * v for v in r]
    softened = squares[0] + squares[1] + squares[2] + EPSILON * EPSILON
    lifted = softened + EPSILON * EPSILON
    root = lax.rsqrt(softened)
    h = root * root * root
    ry, rz = r[1] * h, r[2] * h
    tiles = {(p, p): (squares[p] + lifted) * h for p in range(3)}
    tiles[0, 1], tiles[0, 2], tiles[1, 2] = r[0] * ry, r[0] * rz, r[1] * rz
    return {pq: tile.astype(jnp.bfloat16) for pq, tile in tiles.items()}


def add_pairs(groups, listed, blocks, own, spread, total):
    chunk = 16

    @pl.loop(0, groups)
    def _(group):
        for u in range(GROUP):
            code = listed[group * GROUP + u]
            pair = lax.div(code, jnp.int32(27))
            k = code - pair * 27
            source = lax.shift_right_logical(pair, jnp.int32(4))
            a = lax.bitwise_and(pair, jnp.int32(15))
            dx = lax.div(k, jnp.int32(9))
            dy = lax.div(k, jnp.int32(3)) - dx * 3
            dz = k - dx * 9 - dy * 3
            own_rows = own[a]
            placed = [
                jnp.broadcast_to(
                    own_rows[p : p + 1] + (1 - step).astype(jnp.float32), (chunk, 128)
                )
                for p, step in enumerate((dx, dy, dz))
            ]
            parts = [
                tile_rows(placed, spread.at[source], pl.ds(j, chunk))
                for j in range(0, 128, chunk)
            ]
            tiles = {
                pq: jnp.concatenate([part[pq] for part in parts], axis=0) for pq in parts[0]
            }
            matrix = jnp.concatenate(
                [
                    jnp.concatenate([tiles[min(p, q), max(p, q)] for p in range(3)], axis=1)
                    for q in range(3)
                ],
                axis=0,
            )
            rank = total.shape[1]
            sampled = jnp.concatenate(
                [blocks[source, q * rank : (q + 1) * rank, :] for q in range(3)], axis=1
            )
            total[a] += matmul(sampled, matrix, None)


def list_stage(stage, near, listed, blank):
    halos, lists = stage
    odd = lax.axis_index("gx") % 2
    size = lax.axis_size("gx")
    start = jnp.int32(0)
    for pairs, first, within in lists:
        pairs = [(a, k, source + first, sides, across) for a, k, source, sides, across in pairs]
        x_side = None
        if within is True:
            x_side = (1 - odd, jnp.int32(1))
        elif within is False:
            place = lax.axis_index("gx")
            inside = jnp.logical_and(place > 0, place < size - 1).astype(jnp.int32)
            x_side = (odd, inside)
        start = list_pairs(pairs, halos, near, listed, start, x_side)
    return close_list(listed, start, blank)


def near_stage(stage, near, own, blocks, total, listed, turned, spread):
    groups = list_stage(stage, near, listed, (total.shape[0] - 1) * 27 + 13)
    places = sorted({first + pair[2] for pairs, first, _ in stage[1] for pair in pairs})
    spread_offsets(blocks, with_far_places(places, stage), turned, spread)
    add_pairs(groups, listed, blocks, own, spread, total)


def with_far_places(places, stage):
    halos, lists = stage
    depth = SIDE + halos[2]
    found = set(places)
    for pairs, first, _ in lists:
        for _, _, source, sides, _ in pairs:
            moves = [0]
            for axis, _ in sides:
                step = {1: depth, 2: 1}[axis] * (halos[axis] - 1)
                moves = moves + [move + step for move in moves]
            found.update(first + source + move for move in moves)
    return sorted(found)


def first_kernel(stage, near, own, blocks, total, *scratch):
    total[...] = jnp.zeros_like(total)
    near_stage(stage, near, own, blocks, total, *scratch)


def next_kernel(stage, near, own, blocks, before, total, *scratch):
    total[...] = before[...]
    near_stage(stage, near, own, blocks, total, *scratch)


def last_kernel(stage, near, own, before, sketch, *rest):
    *parts, far, grams, factor, samples, z_out = rest[:-5]
    total, single, *scratch = rest[-5:]
    total[...] = before[...]
    for blocks in parts:
        near_stage(stage, near, own, blocks, total, *scratch)
    far[...] = sketch[...] - total[: far.shape[0]]
    box_level(far, grams, factor, samples, z_out, single)


def pack_kernel(samples, offsets, packed, own, *faces):
    count, rank, leaf_rows = samples.shape
    filler = jnp.zeros((13, 128), jnp.float32)
    for a in range(count):
        for q in range(3):
            packed[a, q * rank : (q + 1) * rank, :] = samples[a, :, q * 128 : (q + 1) * 128]
        rows = jnp.concatenate([offsets[a].astype(jnp.float32), filler], axis=0)
        packed[a, 3 * rank :, :] = rows.astype(jnp.bfloat16)
        own[a] = rows[:8]
    own[count] = jnp.zeros_like(own[count])
    planes = [1 - parity("gz"), parity("gz")]
    for face, plane in zip(faces, planes):
        for column in range(SIDE * SIDE):
            face[column] = packed[column * SIDE + plane]


VMEM_LIMIT = 48 * 1024 * 1024


def near_scratch(stage, count):
    length = sum(len(pairs) for pairs, _, _ in stage[1])
    return [
        pltpu.SMEM((length + GROUP + 1,), jnp.int32),
        pltpu.VMEM((128, 128), jnp.float32),
        pltpu.VMEM((count, 3, 128, 128), jnp.float32),
    ]


def cost(microseconds):
    return pl.CostEstimate(
        flops=microseconds * 1000 * 1000 * 1000, bytes_accessed=1024, transcendentals=0
    )


IN_SMEM = pl.BlockSpec(memory_space=pltpu.SMEM)
IN_VMEM = pl.BlockSpec(memory_space=pltpu.VMEM)


def box_level(far, grams_out, factor_out, samples_out, z_out, single):
    count, rank, _ = far.shape
    eye = unit(rank)
    grams = [gram_of(thirds(far[a])) for a in range(count)]
    for a in range(count):
        grams_out[a] = grams[a]
    total = sum_of(grams)
    single[...] = join([eye, 0.5 * (total + total.T)], 1)
    eliminate_single(single, rank)
    left = left_side(single[:, :rank])
    lower = upper(single[:, rank:]).T
    samples = [matmul(left, right_side(thirds(far[a])), None) for a in range(count)]
    grams = [near_gram(rows, rows) for rows in samples]
    for a in range(count):
        samples_out[a] = samples[a]
    excess = sum_of(grams) - eye
    x, z_out[...] = near_unit_factor(excess)
    factor_out[...] = lower + matmul(left_side(lower), right_side(thirds(x)), None)

    @pl.when(not_small(jnp.sum(excess * excess, keepdims=True)))
    def _():
        single[...] = join([eye, eye + excess], 1)
        eliminate_single(single, rank)
        factor_out[...] = matmul(lower, upper(single[:, rank:]).T)
        for a in range(count):
            samples_out[a] = matmul(single[:, :rank], samples_out[a])
        z_out[...] = jnp.zeros_like(eye)


def leaf_factors(grams, work):
    count, rank, _ = grams.shape
    eye = unit(rank)
    for a in range(count):
        work[pl.ds(a, rank, stride=count), :] = join([eye, grams[a]], 1)
    eliminate_batch(work, rank, count)


def leaf_kernel(far, factors, samples, box_z, leaf_out, level_out, work, blocks, es, zs):
    count, rank, leaf_rows = far.shape
    eye = unit(rank)
    inverses = [factors[pl.ds(a, rank, stride=count), :][:, :rank] for a in range(count)]
    bases = [
        matmul(left_side(inverses[a]), right_side(thirds(far[a])), None) for a in range(count)
    ]
    products = [near_gram(join([bases[a], samples[a]], 0), bases[a]) for a in range(count)]
    excesses = [product[:rank] - eye for product in products]
    for a in range(count):
        leaf_out[a] = bases[a]
        blocks[a] = products[a][rank:]
        es[a] = excesses[a]
    inverse_parts = [near_unit_factor(excess)[1] for excess in excesses]
    for a in range(count):
        zs[a] = inverse_parts[a]
    norms = [jnp.sum(excess * excess, keepdims=True) for excess in excesses]
    largest = functools.reduce(jnp.maximum, norms)

    @pl.when(not_small(largest))
    def _():
        for a in range(count):
            work[pl.ds(a, rank, stride=count), :] = join([eye, eye + es[a]], 1)
        eliminate_batch(work, rank, count)
        for a in range(count):
            inverse = work[pl.ds(a, rank, stride=count), :][:, :rank]
            leaf_out[a] = matmul(inverse, leaf_out[a])
            blocks[a] = matmul_t(blocks[a], inverse)
            zs[a] = jnp.zeros_like(eye)

    bases = [leaf_out[a] for a in range(count)]
    bases = [basis - matmul(zs[a], basis, None) for a, basis in enumerate(bases)]
    crossed = [blocks[a] for a in range(count)]
    crossed = [block - matmul_t(block, zs[a], None) for a, block in enumerate(crossed)]
    for a in range(count):
        leaf_out[a] = bases[a] * math.sqrt(leaf_rows)
    block = join(crossed, 1) * math.sqrt(count * rank)
    level_out[...] = block - matmul(box_z[...], block, None)


def group_kernel(factors, samples, box_z, nested_out, single, stack):
    count, rank, _ = factors.shape
    eye = unit(rank)
    for b in range(count):
        stack[:, b * rank : (b + 1) * rank] = factors[b]
    parts = thirds(stack[...])
    gram = gram_of(parts)
    single[...] = join([eye, 0.5 * (gram + gram.T)], 1)
    eliminate_single(single, rank)
    block = matmul(left_side(single[:, :rank]), right_side(parts), None)
    excess = near_gram(block, block) - eye
    own = block[:, :rank] * (8.0 * math.sqrt(samples.shape[2]))
    own = own - matmul(own, box_z[...], None)
    left = join(halves(own) * 2, 1)
    leaves = range(samples.shape[0])
    parts = [halves(samples[a]) for a in leaves]
    mixed = [matmul(left, join([f, f, g, g], 0), None) for f, g in parts]
    z = near_unit_factor(excess)[1]
    nested = [rows - matmul(z, rows, None) for rows in mixed]
    for a in leaves:
        nested_out[a] = nested[a]

    @pl.when(not_small(jnp.sum(excess * excess, keepdims=True)))
    def _():
        single[...] = join([eye, eye + excess], 1)
        eliminate_single(single, rank)
        left = join(halves(matmul(single[:, :rank], own)) * 2, 1)
        for a in leaves:
            f, g = halves(samples[a])
            nested_out[a] = matmul(left, join([f, f, g, g], 0), None)


def body(sketch, test_matrix, offsets, near):
    rank, leaf_rows = sketch.shape[3:]
    count = SIDE**3
    halos = [halo_count(axis) for axis in ("gx", "gy", "gz")]
    like = jax.ShapeDtypeStruct
    block = (3 * rank + 16, 128)
    params = pltpu.CompilerParams(vmem_limit_bytes=VMEM_LIMIT)
    flat_near = near.reshape(count * 27)
    flat_sketch = sketch.reshape(count, rank, leaf_rows)
    stages = pair_tables(halos)
    faces = halos[2]
    packed, own, *sent = pl.pallas_call(
        pack_kernel,
        out_shape=(
            like((count,) + block, jnp.bfloat16),
            like((count + 1, 8, 128), jnp.float32),
        )
        + (like((SIDE * SIDE,) + block, jnp.bfloat16),) * faces,
        compiler_params=params,
        name="pack",
    )(test_matrix.reshape(count, rank, leaf_rows), offsets.reshape(count, 3, 128))
    z_halos = [from_partner(sent[0], "gz", 0)]
    if faces == 2:
        size = lax.axis_size("gz")
        across = [(i, i + 1) for i in range(1, size - 1, 2)]
        across = across + [(j, i) for i, j in across]
        z_halos.append(lax.ppermute(sent[1], "gz", across))
    inner = packed.reshape((SIDE, SIDE, SIDE) + block)
    columns = [h.reshape((SIDE, SIDE, 1) + block) for h in z_halos]
    extended = join([inner] + columns, 2)
    depth = extended.shape[2]
    flat = lambda parts: [x.reshape((-1,) + block) for x in parts]
    column = (SIDE + halos[1]) * depth
    whole = like((count, rank, leaf_rows), jnp.float32)
    sums = like((count + 1, rank, leaf_rows), jnp.float32)
    squares = like((count, rank, rank), jnp.float32)
    square = like((rank, rank), jnp.float32)
    single_scratch = pltpu.VMEM((rank, 2 * rank), jnp.float32)

    def add_stage(stage, blocks, before, name, time):
        kernel = first_kernel if before is None else next_kernel
        before = [] if before is None else [before]
        return pl.pallas_call(
            functools.partial(kernel, stage),
            out_shape=sums,
            in_specs=[IN_SMEM, IN_VMEM, IN_VMEM] + [IN_VMEM] * len(before),
            scratch_shapes=near_scratch(stage, blocks.shape[0]),
            cost_estimate=cost(time),
            compiler_params=params,
            name=name,
        )(flat_near, own, blocks, *before)

    total = add_stage((halos, [(stages[0], 0, None)]), packed, None, "near_inner", 4)
    extended, total = lax.optimization_barrier((extended, total))
    y_halos = to_neighbours(extended[:, 0], extended[:, 1], "gy")
    stage = (halos, [(stages[1], 0, None)])
    blocks = extended.reshape((-1,) + block)
    total = add_stage(stage, blocks, total, "near_inner_and_z", 6)
    wide = join([extended] + [h[:, None] for h in y_halos], 1)
    wide, total = lax.optimization_barrier((wide, total))
    parts = flat(swap_across(wide[0], wide[1], "gx"))
    stage = (halos, [(stages[2], 0, None)])
    total = add_stage(stage, wide.reshape((-1,) + block), total, "near_y", 0)
    half = wide.shape[1] // 2
    blocks = [swap_within(part[0], part[1], "gx") for part in (wide[:, :half], wide[:, half:])]
    blocks = join(flat(blocks), 0)
    stage = (halos, [(stages[3], 0, True)])
    total = add_stage(stage, blocks, total, "near_x_within", 0)
    stage = (halos, [(stages[3], 0, False)])
    far, grams, factor, samples, box_z = pl.pallas_call(
        functools.partial(last_kernel, stage),
        out_shape=(whole, squares, square, whole, square),
        in_specs=[IN_SMEM, IN_VMEM, IN_VMEM, IN_VMEM] + [IN_VMEM] * len(parts),
        scratch_shapes=[pltpu.VMEM(sums.shape, jnp.float32), single_scratch]
        + near_scratch(stage, column),
        compiler_params=params,
        name="near_x_and_box_level",
    )(flat_near, own, total, flat_sketch, *parts)
    grouped = factor[None]
    grouped = join([grouped, from_partner(grouped, "gz", 0)], 0)
    factors = pl.pallas_call(
        leaf_factors,
        out_shape=like((rank * count, 2 * rank), jnp.float32),
        cost_estimate=cost(3),
        compiler_params=params,
        name="leaf_factors",
    )(grams)
    grouped, factors = lax.optimization_barrier((grouped, factors))
    grouped = join([grouped, from_partner(grouped, "gy", 0)], 0)
    leaf_t, level_t = pl.pallas_call(
        leaf_kernel,
        out_shape=(whole, like((rank, count * rank), jnp.float32)),
        scratch_shapes=[pltpu.VMEM((rank * count, 2 * rank), jnp.float32)]
        + [pltpu.VMEM((count, rank, rank), jnp.float32)] * 3,
        cost_estimate=cost(4),
        compiler_params=params,
        name="leaf_level",
    )(far, factors, samples, box_z)
    grouped, leaf_t, level_t = lax.optimization_barrier((grouped, leaf_t, level_t))
    grouped = join([grouped, from_partner(grouped, "gx", 0)], 0)
    nested = pl.pallas_call(
        group_kernel,
        out_shape=whole,
        scratch_shapes=[
            single_scratch,
            pltpu.VMEM((rank, count * rank), jnp.float32),
        ],
        compiler_params=params,
        name="group_level",
    )(grouped, samples, box_z)
    return (leaf_t.reshape(sketch.shape), level_t[None, None, None], nested.reshape(sketch.shape))


def solution(mesh):
    placed = (
        P("gx", "gy", "gz", None, None),
        P("gx", "gy", "gz", None, None),
        P("gx", "gy", "gz", None, None),
        P("gx", "gy", "gz", None),
    )
    return jax.shard_map(
        body,
        mesh=mesh,
        in_specs=placed,
        out_specs=(
            P("gx", "gy", "gz", None, None),
            P("gx", "gy", "gz", None, None),
            P("gx", "gy", "gz", None, None),
        ),
        check_vma=False,
    )
```

```python
import functools
import math

import jax
import jax.numpy as jnp
from jax import lax
from jax.experimental import pallas as pl
from jax.experimental.pallas import tpu as pltpu
from jax.sharding import PartitionSpec as P

EPSILON = 0.1
GROUP = 8
SIDE = 2
HIGHEST = lax.Precision.HIGHEST


def from_partner(x, axis, distance):
    return lax.ppermute(x, axis, [(i, i ^ 1 << distance) for i in range(lax.axis_size(axis))])


SMALL = 0.06


def matmul(a, b, precision=HIGHEST):
    return lax.dot_general(
        a, b, (((1,), (0,)), ((), ())), precision=precision, preferred_element_type=jnp.float32
    )


def matmul_t(a, b, precision=HIGHEST):
    return lax.dot_general(
        a, b, (((1,), (1,)), ((), ())), precision=precision, preferred_element_type=jnp.float32
    )


def join(parts, axis):
    return jnp.concatenate(parts, axis=axis)


def halves(x):
    high = x.astype(jnp.bfloat16)
    return high, (x - high.astype(jnp.float32)).astype(jnp.bfloat16)


def thirds(x):
    high = x.astype(jnp.bfloat16)
    rest = x - high.astype(jnp.float32)
    return (high,) + halves(rest)


def positions(shape):
    return (
        lax.broadcasted_iota(jnp.int32, shape, 0),
        lax.broadcasted_iota(jnp.int32, shape, 1),
    )


def unit(rank):
    row, column = positions((rank, rank))
    return jnp.where(row == column, 1.0, 0.0).astype(jnp.float32)


def upper(x):
    row, column = positions(x.shape)
    return jnp.where(row <= column, x, 0.0)


def half_lower(x):
    row, column = positions(x.shape)
    return jnp.where(row > column, x, jnp.where(row == column, 0.5 * x, 0.0))


def gram_of(parts):
    f, g, h = parts
    return matmul_t(join([f, f, g, g, f, h], 1), join([f, g, f, g, h, f], 1), None)


def right_side(parts):
    f, g, h = parts
    return join([f, f, g, g, h, f], 0)


def left_side(x):
    f, g, h = thirds(x)
    first = join([f, g], 1)
    return join([first, first, join([f, h], 1)], 1)


def near_gram(x, y):
    f, g = halves(x)
    u, v = halves(y)
    return matmul_t(join([f, f, g], 1), join([u, v, u], 1), None)


def near_unit_factor(excess):
    x = half_lower(excess)
    square = matmul(x, x, None)
    x = half_lower(excess - matmul_t(x, x, None))
    return x, x - square


def sum_of(parts):
    while len(parts) > 1:
        parts = [sum(parts[i : i + 2]) for i in range(0, len(parts), 2)]
    return parts[0]


def not_small(norm):
    return jnp.logical_not(norm[0, 0] <= SMALL * SMALL)


def batch_rows(work, rank, batch, low, high, width=8):
    shape = (batch, 2 * rank)

    def lane(values, index):
        return jnp.broadcast_to(values[:, rank + index : rank + index + 1], shape)

    for start in range(low, high, width):
        rows = [work[(start + i) * batch : (start + i + 1) * batch, :] for i in range(width)]
        scalars = [
            [lane(rows[i], start + j) if j >= i else None for j in range(width)]
            for i in range(width)
        ]
        for j in range(width):
            root = lax.rsqrt(scalars[j][j])
            rows[j] = rows[j] * root
            factor = [None if i <= j else scalars[j][i] * root for i in range(width)]
            for i in range(j + 1, width):
                rows[i] = rows[i] - factor[i] * rows[j]
                for k in range(i, width):
                    scalars[i][k] = scalars[i][k] - factor[i] * factor[k]
            work[(start + j) * batch : (start + j + 1) * batch, :] = rows[j]
        for lower in range(start + width, high):
            total = work[lower * batch : (lower + 1) * batch, :]
            for j in range(width):
                total = total - lane(rows[j], lower) * rows[j]
            work[lower * batch : (lower + 1) * batch, :] = total


def batch_update(work, rank, batch, low, high):
    size = high - low
    each = 128 // size
    row, column = positions((128, 128))
    for first in range(0, batch, each):
        done = join(
            [work[pl.ds(low * batch + first + i, size, stride=batch), :] for i in range(each)], 0
        )
        turned = done.T
        right = right_side(thirds(done))
        for top in range(high, rank, size):
            factor = join([turned[rank + top : rank + top + size, :]] * each, 0)
            f, g, h = thirds(jnp.where(row // size == column // size, factor, 0.0))
            change = matmul(join([f, g, f, g, f, h], 1), right, None)
            for i in range(each):
                place = pl.ds(top * batch + first + i, size, stride=batch)
                work[place, :] = work[place, :] - change[i * size : (i + 1) * size]


def eliminate_batch(work, rank, batch):
    half = rank // 2
    batch_rows(work, rank, batch, 0, half)
    batch_update(work, rank, batch, 0, half)
    batch_rows(work, rank, batch, half, rank)


def eliminate_single(work, rank):
    shape = (8, 2 * rank)
    row, _ = positions(shape)
    for start in range(0, rank, 8):
        blocks = {m: work[m : m + 8, :] for m in range(start, rank, 8)}
        columns = {
            m: [
                jnp.broadcast_to(blocks[m][:, rank + start + j : rank + start + j + 1], shape)
                for j in range(8)
            ]
            for m in blocks
        }
        done = blocks[start]
        for j in range(8):
            root = lax.rsqrt(columns[start][j][j : j + 1, :])
            line = [columns[start][i][j : j + 1, :] * root for i in range(8)]
            scaled = blocks[start][j : j + 1, :] * root
            done = jnp.where(row == j, scaled, done)
            for m in blocks:
                factor = columns[m][j] * root
                blocks[m] = blocks[m] - factor * scaled
                for i in range(j + 1, 8):
                    columns[m][i] = columns[m][i] - factor * line[i]
        work[start : start + 8, :] = done
        for m in blocks:
            if m > start:
                work[m : m + 8, :] = blocks[m]


def parity(axis):
    return lax.axis_index(axis) % 2


def to_neighbours(low, high, axis):
    size = lax.axis_size(axis)
    even = parity(axis) == 0
    received = []
    if size > 2:
        across = [(i, i + 1) for i in range(1, size - 1, 2)]
        across = across + [(j, i) for i, j in across]
        received.append(lax.ppermute(jnp.where(even, low, high), axis, across))
    pairs = [(i, i ^ 1) for i in range(size)]
    received.append(lax.ppermute(jnp.where(even, high, low), axis, pairs))
    return received[::-1]


def halo_count(axis):
    return 1 if lax.axis_size(axis) == 2 else 2


def leaf_index(x, y, z):
    return (x * SIDE + y) * SIDE + z


def pair_tables(halos):
    depth = SIDE + halos[2]
    wide = SIDE + halos[1]
    stages = ([], [], [], [])
    for a in range(SIDE**3):
        place = (a // 4, a // 2 % 2, a % 2)
        for k in range(27):
            at = [p + d for p, d in zip(place, (k // 9 - 1, k // 3 % 3 - 1, k % 3 - 1))]
            sides = tuple((axis, t) for axis, t in enumerate(at) if t in (-1, 2) and axis > 0)
            x, y, z = (2 if t == -1 else t for t in at)
            if at[0] == -1:
                stages[3].append((a, k, y * depth + z, sides, True))
            elif at[0] == 2:
                continue
            elif sides:
                stages[2].append((a, k, (x * wide + y) * depth + z, sides, False))
            else:
                stages[a * 2 // SIDE**3].append((a, k, leaf_index(x, y, z), sides, False))
    return stages


def far_sides(halos):
    found = {}
    for axis, name in enumerate(("gx", "gy", "gz")):
        place = lax.axis_index(name)
        odd = place % 2
        other = halos[axis] - 1
        found[axis, -1] = ((place > 0).astype(jnp.int32), (1 - odd) * other)
        found[axis, 2] = ((place < lax.axis_size(name) - 1).astype(jnp.int32), odd * other)
    return found


def list_pairs(pairs, halos, near, listed, count, x_side):
    found = far_sides(halos)
    depth = SIDE + halos[2]
    joint = {}
    for a, k, source, sides, across in pairs:
        key = (sides, across)
        if key not in joint:
            inside, moved, entry = jnp.int32(1), jnp.int32(0), jnp.int32(0)
            if across:
                inside = x_side[1]
                entry = x_side[0] * (4 * 27 + 18)
            steps = {1: depth, 2: 1}
            for side in sides:
                inside = inside * found[side][0]
                moved = moved + found[side][1] * steps[side[0]]
            joint[key] = (inside, moved * (16 * 27) + entry, entry)
        inside, moved, entry = joint[key]
        code = jnp.int32((source * 16 + a) * 27 + k)
        if sides or across:
            taken = near[a * 27 + k + entry] * inside
            code = code + moved
        else:
            taken = near[a * 27 + k]
        listed[count] = code
        count = count + taken
    return count


def close_list(listed, count, blank):
    for i in range(GROUP):
        listed[count + i] = jnp.int32(blank)
    return lax.div(count + (GROUP - 1), jnp.int32(GROUP))


def spread_offsets(blocks, places, turned, spread):
    rank3 = blocks.shape[1] - 8
    row, lane = positions((128, 384))
    for first in range(0, len(places), 32):
        chunk = places[first : first + 32]
        turned[...] = jnp.zeros_like(turned)
        for i, s in enumerate(chunk):
            turned[4 * i : 4 * i + 4, :] = blocks[s, rank3:, :].astype(jnp.float32)[:4]
        columns = turned[...].T.astype(jnp.bfloat16)
        for i, s in enumerate(chunk):
            chosen = jnp.where(row == 4 * i + lane // 128, 1.0, 0.0).astype(jnp.bfloat16)
            values = matmul(columns, chosen, None)
            for p in range(3):
                spread[s, p] = values[:, 128 * p : 128 * (p + 1)]


def tile_rows(own, spread, rows):
    r = [own[p] - spread[p, rows, :] for p in range(3)]
    squares = [v * v for v in r]
    softened = squares[0] + squares[1] + squares[2] + EPSILON * EPSILON
    lifted = softened + EPSILON * EPSILON
    root = lax.rsqrt(softened)
    h = root * root * root
    ry, rz = r[1] * h, r[2] * h
    tiles = {(p, p): (squares[p] + lifted) * h for p in range(3)}
    tiles[0, 1], tiles[0, 2], tiles[1, 2] = r[0] * ry, r[0] * rz, r[1] * rz
    return {pq: tile.astype(jnp.bfloat16) for pq, tile in tiles.items()}


def add_pairs(groups, listed, blocks, own, spread, total):
    chunk = 16

    @pl.loop(0, groups)
    def _(group):
        for u in range(GROUP):
            code = listed[group * GROUP + u]
            pair = lax.div(code, jnp.int32(27))
            k = code - pair * 27
            source = lax.shift_right_logical(pair, jnp.int32(4))
            a = lax.bitwise_and(pair, jnp.int32(15))
            dx = lax.div(k, jnp.int32(9))
            dy = lax.div(k, jnp.int32(3)) - dx * 3
            dz = k - dx * 9 - dy * 3
            own_rows = own[a]
            placed = [
                jnp.broadcast_to(
                    own_rows[p : p + 1] + (1 - step).astype(jnp.float32), (chunk, 128)
                )
                for p, step in enumerate((dx, dy, dz))
            ]
            parts = [
                tile_rows(placed, spread.at[source], pl.ds(j, chunk))
                for j in range(0, 128, chunk)
            ]
            tiles = {
                pq: jnp.concatenate([part[pq] for part in parts], axis=0) for pq in parts[0]
            }
            matrix = jnp.concatenate(
                [
                    jnp.concatenate([tiles[min(p, q), max(p, q)] for p in range(3)], axis=1)
                    for q in range(3)
                ],
                axis=0,
            )
            rank = total.shape[1]
            sampled = jnp.concatenate(
                [blocks[source, q * rank : (q + 1) * rank, :] for q in range(3)], axis=1
            )
            total[a] += matmul(sampled, matrix, None)


def list_stage(stage, near, listed, blank):
    halos, lists = stage
    odd = lax.axis_index("gx") % 2
    size = lax.axis_size("gx")
    start = jnp.int32(0)
    for pairs, first, within in lists:
        pairs = [(a, k, source + first, sides, across) for a, k, source, sides, across in pairs]
        x_side = None
        if within is True:
            x_side = (1 - odd, jnp.int32(1))
        elif within is False:
            place = lax.axis_index("gx")
            inside = jnp.logical_and(place > 0, place < size - 1).astype(jnp.int32)
            x_side = (odd, inside)
        start = list_pairs(pairs, halos, near, listed, start, x_side)
    return close_list(listed, start, blank)


def near_stage(stage, near, own, blocks, total, listed, turned, spread):
    groups = list_stage(stage, near, listed, (total.shape[0] - 1) * 27 + 13)
    places = sorted({first + pair[2] for pairs, first, _ in stage[1] for pair in pairs})
    spread_offsets(blocks, with_far_places(places, stage), turned, spread)
    add_pairs(groups, listed, blocks, own, spread, total)


def with_far_places(places, stage):
    halos, lists = stage
    depth = SIDE + halos[2]
    found = set(places)
    for pairs, first, _ in lists:
        for _, _, source, sides, _ in pairs:
            moves = [0]
            for axis, _ in sides:
                step = {1: depth, 2: 1}[axis] * (halos[axis] - 1)
                moves = moves + [move + step for move in moves]
            found.update(first + source + move for move in moves)
    return sorted(found)


def first_kernel(stage, near, own, blocks, total, *scratch):
    total[...] = jnp.zeros_like(total)
    near_stage(stage, near, own, blocks, total, *scratch)


def next_kernel(stage, near, own, blocks, before, total, *scratch):
    total[...] = before[...]
    near_stage(stage, near, own, blocks, total, *scratch)


def last_kernel(stage, near, own, before, sketch, *rest):
    *parts, far, grams, factor, samples, z_out = rest[:-5]
    total, single, *scratch = rest[-5:]
    total[...] = before[...]
    for blocks in parts:
        near_stage(stage, near, own, blocks, total, *scratch)
    far[...] = sketch[...] - total[: far.shape[0]]
    box_level(far, grams, factor, samples, z_out, single)


def pack_kernel(samples, offsets, packed, own, *faces):
    count, rank, leaf_rows = samples.shape
    filler = jnp.zeros((5, 128), jnp.float32)
    for a in range(count):
        for q in range(3):
            packed[a, q * rank : (q + 1) * rank, :] = samples[a, :, q * 128 : (q + 1) * 128]
        rows = jnp.concatenate([offsets[a].astype(jnp.float32), filler], axis=0)
        packed[a, 3 * rank :, :] = rows.astype(jnp.bfloat16)
        own[a] = rows
    own[count] = jnp.zeros_like(own[count])
    planes = [1 - parity("gz"), parity("gz")]
    for face, plane in zip(faces, planes):
        for column in range(SIDE * SIDE):
            face[column] = packed[column * SIDE + plane]


VMEM_LIMIT = 48 * 1024 * 1024


def near_scratch(stage, count):
    length = sum(len(pairs) for pairs, _, _ in stage[1])
    return [
        pltpu.SMEM((length + GROUP + 1,), jnp.int32),
        pltpu.VMEM((128, 128), jnp.float32),
        pltpu.VMEM((count, 3, 128, 128), jnp.float32),
    ]


def cost(microseconds):
    return pl.CostEstimate(
        flops=microseconds * 1000 * 1000 * 1000, bytes_accessed=4 * 1024 * 1024, transcendentals=0
    )


IN_SMEM = pl.BlockSpec(memory_space=pltpu.SMEM)
IN_VMEM = pl.BlockSpec(memory_space=pltpu.VMEM)


def box_level(far, grams_out, factor_out, samples_out, z_out, single):
    count, rank, _ = far.shape
    eye = unit(rank)
    grams = [gram_of(thirds(far[a])) for a in range(count)]
    for a in range(count):
        grams_out[a] = grams[a]
    total = sum_of(grams)
    single[...] = join([eye, 0.5 * (total + total.T)], 1)
    eliminate_single(single, rank)
    left = left_side(single[:, :rank])
    lower = upper(single[:, rank:]).T
    samples = [matmul(left, right_side(thirds(far[a])), None) for a in range(count)]
    grams = [near_gram(rows, rows) for rows in samples]
    for a in range(count):
        samples_out[a] = samples[a]
    excess = sum_of(grams) - eye
    x, z_out[...] = near_unit_factor(excess)
    factor_out[...] = lower + matmul(left_side(lower), right_side(thirds(x)), None)

    @pl.when(not_small(jnp.sum(excess * excess, keepdims=True)))
    def _():
        single[...] = join([eye, eye + excess], 1)
        eliminate_single(single, rank)
        factor_out[...] = matmul(lower, upper(single[:, rank:]).T)
        for a in range(count):
            samples_out[a] = matmul(single[:, :rank], samples_out[a])
        z_out[...] = jnp.zeros_like(eye)


def leaf_factors(grams, work):
    count, rank, _ = grams.shape
    eye = unit(rank)
    for a in range(count):
        work[pl.ds(a, rank, stride=count), :] = join([eye, grams[a]], 1)
    eliminate_batch(work, rank, count)


def leaf_kernel(far, factors, samples, box_z, leaf_out, level_out, work, blocks, es, zs):
    count, rank, leaf_rows = far.shape
    eye = unit(rank)
    inverses = [factors[pl.ds(a, rank, stride=count), :][:, :rank] for a in range(count)]
    bases = [
        matmul(left_side(inverses[a]), right_side(thirds(far[a])), None) for a in range(count)
    ]
    products = [near_gram(join([bases[a], samples[a]], 0), bases[a]) for a in range(count)]
    excesses = [product[:rank] - eye for product in products]
    for a in range(count):
        leaf_out[a] = bases[a]
        blocks[a] = products[a][rank:]
        es[a] = excesses[a]
    inverse_parts = [near_unit_factor(excess)[1] for excess in excesses]
    for a in range(count):
        zs[a] = inverse_parts[a]
    norms = [jnp.sum(excess * excess, keepdims=True) for excess in excesses]
    largest = functools.reduce(jnp.maximum, norms)

    @pl.when(not_small(largest))
    def _():
        for a in range(count):
            work[pl.ds(a, rank, stride=count), :] = join([eye, eye + es[a]], 1)
        eliminate_batch(work, rank, count)
        for a in range(count):
            inverse = work[pl.ds(a, rank, stride=count), :][:, :rank]
            leaf_out[a] = matmul(inverse, leaf_out[a])
            blocks[a] = matmul_t(blocks[a], inverse)
            zs[a] = jnp.zeros_like(eye)

    bases = [leaf_out[a] for a in range(count)]
    bases = [basis - matmul(zs[a], basis, None) for a, basis in enumerate(bases)]
    crossed = [blocks[a] for a in range(count)]
    crossed = [block - matmul_t(block, zs[a], None) for a, block in enumerate(crossed)]
    for a in range(count):
        leaf_out[a] = bases[a] * math.sqrt(leaf_rows)
    block = join(crossed, 1) * math.sqrt(count * rank)
    level_out[...] = block - matmul(box_z[...], block, None)


def group_kernel(factors, samples, box_z, nested_out, single, stack):
    count, rank, _ = factors.shape
    eye = unit(rank)
    for b in range(count):
        stack[:, b * rank : (b + 1) * rank] = factors[b]
    parts = thirds(stack[...])
    gram = gram_of(parts)
    single[...] = join([eye, 0.5 * (gram + gram.T)], 1)
    eliminate_single(single, rank)
    block = matmul(left_side(single[:, :rank]), right_side(parts), None)
    excess = near_gram(block, block) - eye
    own = block[:, :rank] * (8.0 * math.sqrt(samples.shape[2]))
    own = own - matmul(own, box_z[...], None)
    left = join(halves(own) * 2, 1)
    leaves = range(samples.shape[0])
    parts = [halves(samples[a]) for a in leaves]
    mixed = [matmul(left, join([f, f, g, g], 0), None) for f, g in parts]
    z = near_unit_factor(excess)[1]
    nested = [rows - matmul(z, rows, None) for rows in mixed]
    for a in leaves:
        nested_out[a] = nested[a]

    @pl.when(not_small(jnp.sum(excess * excess, keepdims=True)))
    def _():
        single[...] = join([eye, eye + excess], 1)
        eliminate_single(single, rank)
        left = join(halves(matmul(single[:, :rank], own)) * 2, 1)
        for a in leaves:
            f, g = halves(samples[a])
            nested_out[a] = matmul(left, join([f, f, g, g], 0), None)


def body(sketch, test_matrix, offsets, near):
    rank, leaf_rows = sketch.shape[3:]
    count = SIDE**3
    halos = [halo_count(axis) for axis in ("gx", "gy", "gz")]
    like = jax.ShapeDtypeStruct
    block = (3 * rank + 8, 128)
    params = pltpu.CompilerParams(vmem_limit_bytes=VMEM_LIMIT)
    flat_near = near.reshape(count * 27)
    flat_sketch = sketch.reshape(count, rank, leaf_rows)
    stages = pair_tables(halos)
    faces = halos[2]
    packed, own, *sent = pl.pallas_call(
        pack_kernel,
        out_shape=(
            like((count,) + block, jnp.bfloat16),
            like((count + 1, 8, 128), jnp.float32),
        )
        + (like((SIDE * SIDE,) + block, jnp.bfloat16),) * faces,
        compiler_params=params,
        name="pack",
    )(test_matrix.reshape(count, rank, leaf_rows), offsets.reshape(count, 3, 128))
    z_halos = [from_partner(sent[0], "gz", 0)]
    if faces == 2:
        size = lax.axis_size("gz")
        across = [(i, i + 1) for i in range(1, size - 1, 2)]
        across = across + [(j, i) for i, j in across]
        z_halos.append(lax.ppermute(sent[1], "gz", across))
    inner = packed.reshape((SIDE, SIDE, SIDE) + block)
    columns = [h.reshape((SIDE, SIDE, 1) + block) for h in z_halos]
    extended = join([inner] + columns, 2)
    depth = extended.shape[2]
    flat = lambda parts: [x.reshape((-1,) + block) for x in parts]
    column = (SIDE + halos[1]) * depth
    whole = like((count, rank, leaf_rows), jnp.float32)
    sums = like((count + 1, rank, leaf_rows), jnp.float32)
    squares = like((count, rank, rank), jnp.float32)
    square = like((rank, rank), jnp.float32)
    single_scratch = pltpu.VMEM((rank, 2 * rank), jnp.float32)

    def add_stage(stage, blocks, before, name, time):
        kernel = first_kernel if before is None else next_kernel
        before = [] if before is None else [before]
        return pl.pallas_call(
            functools.partial(kernel, stage),
            out_shape=sums,
            in_specs=[IN_SMEM, IN_VMEM, IN_VMEM] + [IN_VMEM] * len(before),
            scratch_shapes=near_scratch(stage, blocks.shape[0]),
            cost_estimate=cost(time),
            compiler_params=params,
            name=name,
        )(flat_near, own, blocks, *before)

    total = add_stage((halos, [(stages[0], 0, None)]), packed, None, "near_inner", 4)
    extended, total = lax.optimization_barrier((extended, total))
    y_halos = to_neighbours(extended[:, 0], extended[:, 1], "gy")
    total = add_stage((halos, [(stages[1], 0, None)]), packed, total, "near_inner_rest", 4)
    wide = join([extended] + [h[:, None] for h in y_halos], 1)
    wide, total = lax.optimization_barrier((wide, total))
    x_halos = to_neighbours(wide[0], wide[1], "gx")
    stage = (halos, [(stages[2], 0, None), (stages[3], SIDE * column, True)])
    blocks = join(flat([wide, x_halos[0]]), 0)
    total = add_stage(stage, blocks, total, "near_z_y_and_x", 9)
    stage = (halos, [(stages[3], 0, False)])
    parts = flat(x_halos[1:])
    far, grams, factor, samples, box_z = pl.pallas_call(
        functools.partial(last_kernel, stage),
        out_shape=(whole, squares, square, whole, square),
        in_specs=[IN_SMEM, IN_VMEM, IN_VMEM, IN_VMEM] + [IN_VMEM] * len(parts),
        scratch_shapes=[pltpu.VMEM(sums.shape, jnp.float32), single_scratch]
        + near_scratch(stage, column),
        compiler_params=params,
        name="near_x_and_box_level",
    )(flat_near, own, total, flat_sketch, *parts)
    grouped = factor[None]
    grouped = join([grouped, from_partner(grouped, "gz", 0)], 0)
    factors = pl.pallas_call(
        leaf_factors,
        out_shape=like((rank * count, 2 * rank), jnp.float32),
        cost_estimate=cost(3),
        compiler_params=params,
        name="leaf_factors",
    )(grams)
    grouped, factors = lax.optimization_barrier((grouped, factors))
    grouped = join([grouped, from_partner(grouped, "gy", 0)], 0)
    leaf_t, level_t = pl.pallas_call(
        leaf_kernel,
        out_shape=(whole, like((rank, count * rank), jnp.float32)),
        scratch_shapes=[pltpu.VMEM((rank * count, 2 * rank), jnp.float32)]
        + [pltpu.VMEM((count, rank, rank), jnp.float32)] * 3,
        cost_estimate=cost(4),
        compiler_params=params,
        name="leaf_level",
    )(far, factors, samples, box_z)
    grouped, leaf_t, level_t = lax.optimization_barrier((grouped, leaf_t, level_t))
    grouped = join([grouped, from_partner(grouped, "gx", 0)], 0)
    nested = pl.pallas_call(
        group_kernel,
        out_shape=whole,
        scratch_shapes=[
            single_scratch,
            pltpu.VMEM((rank, count * rank), jnp.float32),
        ],
        compiler_params=params,
        name="group_level",
    )(grouped, samples, box_z)
    return (leaf_t.reshape(sketch.shape), level_t[None, None, None], nested.reshape(sketch.shape))


def solution(mesh):
    placed = (
        P("gx", "gy", "gz", None, None),
        P("gx", "gy", "gz", None, None),
        P("gx", "gy", "gz", None, None),
        P("gx", "gy", "gz", None),
    )
    return jax.shard_map(
        body,
        mesh=mesh,
        in_specs=placed,
        out_specs=(
            P("gx", "gy", "gz", None, None),
            P("gx", "gy", "gz", None, None),
            P("gx", "gy", "gz", None, None),
        ),
        check_vma=False,
    )
```

```python
import functools
import math

import jax
import jax.numpy as jnp
from jax import lax
from jax.experimental import pallas as pl
from jax.experimental.pallas import tpu as pltpu
from jax.sharding import PartitionSpec as P

EPSILON = 0.1
GROUP = 8
FIRST_LEAVES = 3
SIDE = 2
HIGHEST = lax.Precision.HIGHEST


def from_partner(x, axis, distance):
    return lax.ppermute(x, axis, [(i, i ^ 1 << distance) for i in range(lax.axis_size(axis))])


SMALL = 0.06


def matmul(a, b, precision=HIGHEST):
    return lax.dot_general(
        a, b, (((1,), (0,)), ((), ())), precision=precision, preferred_element_type=jnp.float32
    )


def matmul_t(a, b, precision=HIGHEST):
    return lax.dot_general(
        a, b, (((1,), (1,)), ((), ())), precision=precision, preferred_element_type=jnp.float32
    )


def join(parts, axis):
    return jnp.concatenate(parts, axis=axis)


def halves(x):
    high = x.astype(jnp.bfloat16)
    return high, (x - high.astype(jnp.float32)).astype(jnp.bfloat16)


def thirds(x):
    high = x.astype(jnp.bfloat16)
    rest = x - high.astype(jnp.float32)
    return (high,) + halves(rest)


def positions(shape):
    return (
        lax.broadcasted_iota(jnp.int32, shape, 0),
        lax.broadcasted_iota(jnp.int32, shape, 1),
    )


def unit(rank):
    row, column = positions((rank, rank))
    return jnp.where(row == column, 1.0, 0.0).astype(jnp.float32)


def upper(x):
    row, column = positions(x.shape)
    return jnp.where(row <= column, x, 0.0)


def half_lower(x):
    row, column = positions(x.shape)
    return jnp.where(row > column, x, jnp.where(row == column, 0.5 * x, 0.0))


def gram_of(parts):
    f, g, h = parts
    return matmul_t(join([f, f, g, g, f, h], 1), join([f, g, f, g, h, f], 1), None)


def right_side(parts):
    f, g, h = parts
    return join([f, f, g, g, h, f], 0)


def left_side(x):
    f, g, h = thirds(x)
    first = join([f, g], 1)
    return join([first, first, join([f, h], 1)], 1)


def near_gram(x, y):
    f, g = halves(x)
    u, v = halves(y)
    return matmul_t(join([f, f, g], 1), join([u, v, u], 1), None)


def near_unit_factor(excess):
    x = half_lower(excess)
    square = matmul(x, x, None)
    x = half_lower(excess - matmul_t(x, x, None))
    return x, x - square


def sum_of(parts):
    while len(parts) > 1:
        parts = [sum(parts[i : i + 2]) for i in range(0, len(parts), 2)]
    return parts[0]


def not_small(norm):
    return jnp.logical_not(norm[0, 0] <= SMALL * SMALL)


def batch_rows(work, rank, batch, low, high, width=8):
    shape = (batch, 2 * rank)

    def lane(values, index):
        return jnp.broadcast_to(values[:, rank + index : rank + index + 1], shape)

    for start in range(low, high, width):
        rows = [work[(start + i) * batch : (start + i + 1) * batch, :] for i in range(width)]
        scalars = [
            [lane(rows[i], start + j) if j >= i else None for j in range(width)]
            for i in range(width)
        ]
        for j in range(width):
            root = lax.rsqrt(scalars[j][j])
            rows[j] = rows[j] * root
            factor = [None if i <= j else scalars[j][i] * root for i in range(width)]
            for i in range(j + 1, width):
                rows[i] = rows[i] - factor[i] * rows[j]
                for k in range(i, width):
                    scalars[i][k] = scalars[i][k] - factor[i] * factor[k]
            work[(start + j) * batch : (start + j + 1) * batch, :] = rows[j]
        for lower in range(start + width, high):
            total = work[lower * batch : (lower + 1) * batch, :]
            for j in range(width):
                total = total - lane(rows[j], lower) * rows[j]
            work[lower * batch : (lower + 1) * batch, :] = total


def batch_update(work, rank, batch, low, high):
    size = high - low
    each = 128 // size
    row, column = positions((128, 128))
    for first in range(0, batch, each):
        done = join(
            [work[pl.ds(low * batch + first + i, size, stride=batch), :] for i in range(each)], 0
        )
        turned = done.T
        right = right_side(thirds(done))
        for top in range(high, rank, size):
            factor = join([turned[rank + top : rank + top + size, :]] * each, 0)
            f, g, h = thirds(jnp.where(row // size == column // size, factor, 0.0))
            change = matmul(join([f, g, f, g, f, h], 1), right, None)
            for i in range(each):
                place = pl.ds(top * batch + first + i, size, stride=batch)
                work[place, :] = work[place, :] - change[i * size : (i + 1) * size]


def eliminate_batch(work, rank, batch):
    half = rank // 2
    batch_rows(work, rank, batch, 0, half)
    batch_update(work, rank, batch, 0, half)
    batch_rows(work, rank, batch, half, rank)


def eliminate_single(work, rank):
    shape = (8, 2 * rank)
    row, _ = positions(shape)
    for start in range(0, rank, 8):
        blocks = {m: work[m : m + 8, :] for m in range(start, rank, 8)}
        columns = {
            m: [
                jnp.broadcast_to(blocks[m][:, rank + start + j : rank + start + j + 1], shape)
                for j in range(8)
            ]
            for m in blocks
        }
        done = blocks[start]
        for j in range(8):
            root = lax.rsqrt(columns[start][j][j : j + 1, :])
            line = [columns[start][i][j : j + 1, :] * root for i in range(8)]
            scaled = blocks[start][j : j + 1, :] * root
            done = jnp.where(row == j, scaled, done)
            for m in blocks:
                factor = columns[m][j] * root
                blocks[m] = blocks[m] - factor * scaled
                for i in range(j + 1, 8):
                    columns[m][i] = columns[m][i] - factor * line[i]
        work[start : start + 8, :] = done
        for m in blocks:
            if m > start:
                work[m : m + 8, :] = blocks[m]


def parity(axis):
    return lax.axis_index(axis) % 2


def to_neighbours(low, high, axis):
    size = lax.axis_size(axis)
    even = parity(axis) == 0
    received = []
    if size > 2:
        across = [(i, i + 1) for i in range(1, size - 1, 2)]
        across = across + [(j, i) for i, j in across]
        received.append(lax.ppermute(jnp.where(even, low, high), axis, across))
    pairs = [(i, i ^ 1) for i in range(size)]
    received.append(lax.ppermute(jnp.where(even, high, low), axis, pairs))
    return received[::-1]


def halo_count(axis):
    return 1 if lax.axis_size(axis) == 2 else 2


def leaf_index(x, y, z):
    return (x * SIDE + y) * SIDE + z


def pair_tables(halos):
    depth = SIDE + halos[2]
    wide = SIDE + halos[1]
    stages = ([], [], [], [])
    for a in range(SIDE**3):
        place = (a // 4, a // 2 % 2, a % 2)
        for k in range(27):
            at = [p + d for p, d in zip(place, (k // 9 - 1, k // 3 % 3 - 1, k % 3 - 1))]
            sides = tuple((axis, t) for axis, t in enumerate(at) if t in (-1, 2) and axis > 0)
            x, y, z = (2 if t == -1 else t for t in at)
            if at[0] == -1:
                stages[3].append((a, k, y * depth + z, sides, True))
            elif at[0] == 2:
                continue
            elif sides:
                stages[2].append((a, k, (x * wide + y) * depth + z, sides, False))
            else:
                stages[0 if a < FIRST_LEAVES else 1].append((a, k, leaf_index(x, y, z), sides, False))
    return stages


def far_sides(halos):
    found = {}
    for axis, name in enumerate(("gx", "gy", "gz")):
        place = lax.axis_index(name)
        odd = place % 2
        other = halos[axis] - 1
        found[axis, -1] = ((place > 0).astype(jnp.int32), (1 - odd) * other)
        found[axis, 2] = ((place < lax.axis_size(name) - 1).astype(jnp.int32), odd * other)
    return found


def list_pairs(pairs, halos, near, listed, count, x_side):
    found = far_sides(halos)
    depth = SIDE + halos[2]
    joint = {}
    for a, k, source, sides, across in pairs:
        key = (sides, across)
        if key not in joint:
            inside, moved, high = jnp.int32(1), jnp.int32(0), jnp.int32(0)
            if across:
                inside = x_side[1]
                high = x_side[0]
            steps = {1: depth, 2: 1}
            for side in sides:
                inside = inside * found[side][0]
                moved = moved + found[side][1] * steps[side[0]]
            joint[key] = (inside, moved * (16 * 27) + high * (4 * 27 + 18), high)
        inside, moved, high = joint[key]
        x, y, z = a // 4, a // 2 % 2, a % 2
        code = jnp.int32((source * 16 + a) * 27 + k)
        if sides or across:
            if across:
                x, k = x + high, k + high * 18
            taken = near[x, y, z, k] * inside
            code = code + moved
        else:
            taken = near[x, y, z, k]
        listed[count] = code
        count = count + taken
    return count


def close_list(listed, count, blank):
    for i in range(GROUP):
        listed[count + i] = jnp.int32(blank)
    return lax.div(count + (GROUP - 1), jnp.int32(GROUP))


def spread_offsets(blocks, places, turned, spread):
    rank3 = blocks.shape[1] - 8
    row, lane = positions((128, 384))
    for first in range(0, len(places), 32):
        chunk = places[first : first + 32]
        turned[...] = jnp.zeros_like(turned)
        for i, s in enumerate(chunk):
            turned[4 * i : 4 * i + 4, :] = blocks[s, rank3:, :].astype(jnp.float32)[:4]
        columns = turned[...].T.astype(jnp.bfloat16)
        for i, s in enumerate(chunk):
            chosen = jnp.where(row == 4 * i + lane // 128, 1.0, 0.0).astype(jnp.bfloat16)
            values = matmul(columns, chosen, None)
            for p in range(3):
                spread[s, p] = values[:, 128 * p : 128 * (p + 1)]


def tile_rows(own, spread, rows):
    r = [own[p] - spread[p, rows, :] for p in range(3)]
    squares = [v * v for v in r]
    softened = squares[0] + squares[1] + squares[2] + EPSILON * EPSILON
    lifted = softened + EPSILON * EPSILON
    root = lax.rsqrt(softened)
    h = root * root * root
    ry, rz = r[1] * h, r[2] * h
    tiles = {(p, p): (squares[p] + lifted) * h for p in range(3)}
    tiles[0, 1], tiles[0, 2], tiles[1, 2] = r[0] * ry, r[0] * rz, r[1] * rz
    return {pq: tile.astype(jnp.bfloat16) for pq, tile in tiles.items()}


def add_pairs(groups, listed, blocks, own, spread, total):
    chunk = 16

    @pl.loop(0, groups)
    def _(group):
        for u in range(GROUP):
            code = listed[group * GROUP + u]
            pair = lax.div(code, jnp.int32(27))
            k = code - pair * 27
            source = lax.shift_right_logical(pair, jnp.int32(4))
            a = lax.bitwise_and(pair, jnp.int32(15))
            dx = lax.div(k, jnp.int32(9))
            dy = lax.div(k, jnp.int32(3)) - dx * 3
            dz = k - dx * 9 - dy * 3
            own_rows = own[a]
            placed = [
                jnp.broadcast_to(
                    own_rows[p : p + 1] + (1 - step).astype(jnp.float32), (chunk, 128)
                )
                for p, step in enumerate((dx, dy, dz))
            ]
            parts = [
                tile_rows(placed, spread.at[source], pl.ds(j, chunk))
                for j in range(0, 128, chunk)
            ]
            tiles = {
                pq: jnp.concatenate([part[pq] for part in parts], axis=0) for pq in parts[0]
            }
            matrix = jnp.concatenate(
                [
                    jnp.concatenate([tiles[min(p, q), max(p, q)] for p in range(3)], axis=1)
                    for q in range(3)
                ],
                axis=0,
            )
            rank = total.shape[1]
            sampled = jnp.concatenate(
                [blocks[source, q * rank : (q + 1) * rank, :] for q in range(3)], axis=1
            )
            total[a] += matmul(sampled, matrix, None)


def list_stage(stage, near, listed, blank):
    halos, lists = stage
    odd = lax.axis_index("gx") % 2
    size = lax.axis_size("gx")
    start = jnp.int32(0)
    for pairs, first, within in lists:
        pairs = [(a, k, source + first, sides, across) for a, k, source, sides, across in pairs]
        x_side = None
        if within is True:
            x_side = (1 - odd, jnp.int32(1))
        elif within is False:
            place = lax.axis_index("gx")
            inside = jnp.logical_and(place > 0, place < size - 1).astype(jnp.int32)
            x_side = (odd, inside)
        start = list_pairs(pairs, halos, near, listed, start, x_side)
    return close_list(listed, start, blank)


def near_stage(stage, near, own, blocks, total, listed, turned, spread):
    groups = list_stage(stage, near, listed, (total.shape[0] - 1) * 27 + 13)
    places = sorted({first + pair[2] for pairs, first, _ in stage[1] for pair in pairs})
    spread_offsets(blocks, with_far_places(places, stage), turned, spread)
    add_pairs(groups, listed, blocks, own, spread, total)


def with_far_places(places, stage):
    halos, lists = stage
    depth = SIDE + halos[2]
    found = set(places)
    for pairs, first, _ in lists:
        for _, _, source, sides, _ in pairs:
            moves = [0]
            for axis, _ in sides:
                step = {1: depth, 2: 1}[axis] * (halos[axis] - 1)
                moves = moves + [move + step for move in moves]
            found.update(first + source + move for move in moves)
    return sorted(found)


def first_kernel(stage, near, own, blocks, total, *scratch):
    total[...] = jnp.zeros_like(total)
    near_stage(stage, near, own, blocks, total, *scratch)


def next_kernel(stage, near, own, blocks, before, total, *scratch):
    total[...] = before[...]
    near_stage(stage, near, own, blocks, total, *scratch)


def last_kernel(stage, near, own, before, sketch, *rest):
    *parts, far, grams, factor, samples, z_out = rest[:-5]
    total, single, *scratch = rest[-5:]
    total[...] = before[...]
    for blocks in parts:
        near_stage(stage, near, own, blocks, total, *scratch)
    far[...] = sketch[...] - total[: far.shape[0]]
    box_level(far, grams, factor, samples, z_out, single)


def pack_kernel(samples, offsets, packed, own, *faces):
    count, rank, leaf_rows = samples.shape
    filler = jnp.zeros((5, 128), jnp.float32)
    for a in range(count):
        for q in range(3):
            packed[a, q * rank : (q + 1) * rank, :] = samples[a, :, q * 128 : (q + 1) * 128]
        rows = jnp.concatenate([offsets[a].astype(jnp.float32), filler], axis=0)
        packed[a, 3 * rank :, :] = rows.astype(jnp.bfloat16)
        own[a] = rows
    own[count] = jnp.zeros_like(own[count])
    planes = [1 - parity("gz"), parity("gz")]
    for face, plane in zip(faces, planes):
        for column in range(SIDE * SIDE):
            face[column] = packed[column * SIDE + plane]


VMEM_LIMIT = 48 * 1024 * 1024


def near_scratch(stage, count):
    length = sum(len(pairs) for pairs, _, _ in stage[1])
    return [
        pltpu.SMEM((length + GROUP + 1,), jnp.int32),
        pltpu.VMEM((128, 128), jnp.float32),
        pltpu.VMEM((count, 3, 128, 128), jnp.float32),
    ]


def cost(microseconds):
    return pl.CostEstimate(
        flops=microseconds * 1000 * 1000 * 1000, bytes_accessed=4 * 1024 * 1024, transcendentals=0
    )


IN_SMEM = pl.BlockSpec(memory_space=pltpu.SMEM)
IN_VMEM = pl.BlockSpec(memory_space=pltpu.VMEM)


def box_level(far, grams_out, factor_out, samples_out, z_out, single):
    count, rank, _ = far.shape
    eye = unit(rank)
    grams = [gram_of(thirds(far[a])) for a in range(count)]
    for a in range(count):
        grams_out[a] = grams[a]
    total = sum_of(grams)
    single[...] = join([eye, 0.5 * (total + total.T)], 1)
    eliminate_single(single, rank)
    left = left_side(single[:, :rank])
    lower = upper(single[:, rank:]).T
    samples = [matmul(left, right_side(thirds(far[a])), None) for a in range(count)]
    grams = [near_gram(rows, rows) for rows in samples]
    for a in range(count):
        samples_out[a] = samples[a]
    excess = sum_of(grams) - eye
    x, z_out[...] = near_unit_factor(excess)
    factor_out[...] = lower + matmul(left_side(lower), right_side(thirds(x)), None)

    @pl.when(not_small(jnp.sum(excess * excess, keepdims=True)))
    def _():
        single[...] = join([eye, eye + excess], 1)
        eliminate_single(single, rank)
        factor_out[...] = matmul(lower, upper(single[:, rank:]).T)
        for a in range(count):
            samples_out[a] = matmul(single[:, :rank], samples_out[a])
        z_out[...] = jnp.zeros_like(eye)


def leaf_factors(grams, work):
    count, rank, _ = grams.shape
    eye = unit(rank)
    for a in range(count):
        work[pl.ds(a, rank, stride=count), :] = join([eye, grams[a]], 1)
    eliminate_batch(work, rank, count)


def leaf_kernel(far, factors, samples, box_z, leaf_out, level_out, work, blocks, es, zs):
    count, rank, leaf_rows = far.shape
    eye = unit(rank)
    inverses = [factors[pl.ds(a, rank, stride=count), :][:, :rank] for a in range(count)]
    bases = [
        matmul(left_side(inverses[a]), right_side(thirds(far[a])), None) for a in range(count)
    ]
    products = [near_gram(join([bases[a], samples[a]], 0), bases[a]) for a in range(count)]
    excesses = [product[:rank] - eye for product in products]
    for a in range(count):
        leaf_out[a] = bases[a]
        blocks[a] = products[a][rank:]
        es[a] = excesses[a]
    inverse_parts = [near_unit_factor(excess)[1] for excess in excesses]
    for a in range(count):
        zs[a] = inverse_parts[a]
    norms = [jnp.sum(excess * excess, keepdims=True) for excess in excesses]
    largest = functools.reduce(jnp.maximum, norms)

    @pl.when(not_small(largest))
    def _():
        for a in range(count):
            work[pl.ds(a, rank, stride=count), :] = join([eye, eye + es[a]], 1)
        eliminate_batch(work, rank, count)
        for a in range(count):
            inverse = work[pl.ds(a, rank, stride=count), :][:, :rank]
            leaf_out[a] = matmul(inverse, leaf_out[a])
            blocks[a] = matmul_t(blocks[a], inverse)
            zs[a] = jnp.zeros_like(eye)

    bases = [leaf_out[a] for a in range(count)]
    bases = [basis - matmul(zs[a], basis, None) for a, basis in enumerate(bases)]
    crossed = [blocks[a] for a in range(count)]
    crossed = [block - matmul_t(block, zs[a], None) for a, block in enumerate(crossed)]
    for a in range(count):
        leaf_out[a] = bases[a] * math.sqrt(leaf_rows)
    block = join(crossed, 1) * math.sqrt(count * rank)
    level_out[...] = block - matmul(box_z[...], block, None)


def group_kernel(factors, samples, box_z, nested_out, single, stack):
    count, rank, _ = factors.shape
    eye = unit(rank)
    for b in range(count):
        stack[:, b * rank : (b + 1) * rank] = factors[b]
    parts = thirds(stack[...])
    gram = gram_of(parts)
    single[...] = join([eye, 0.5 * (gram + gram.T)], 1)
    eliminate_single(single, rank)
    block = matmul(left_side(single[:, :rank]), right_side(parts), None)
    excess = near_gram(block, block) - eye
    own = block[:, :rank] * (8.0 * math.sqrt(samples.shape[2]))
    own = own - matmul(own, box_z[...], None)
    left = join(halves(own) * 2, 1)
    leaves = range(samples.shape[0])
    parts = [halves(samples[a]) for a in leaves]
    mixed = [matmul(left, join([f, f, g, g], 0), None) for f, g in parts]
    z = near_unit_factor(excess)[1]
    nested = [rows - matmul(z, rows, None) for rows in mixed]
    for a in leaves:
        nested_out[a] = nested[a]

    @pl.when(not_small(jnp.sum(excess * excess, keepdims=True)))
    def _():
        single[...] = join([eye, eye + excess], 1)
        eliminate_single(single, rank)
        left = join(halves(matmul(single[:, :rank], own)) * 2, 1)
        for a in leaves:
            f, g = halves(samples[a])
            nested_out[a] = matmul(left, join([f, f, g, g], 0), None)


def body(sketch, test_matrix, offsets, near):
    rank, leaf_rows = sketch.shape[3:]
    count = SIDE**3
    halos = [halo_count(axis) for axis in ("gx", "gy", "gz")]
    like = jax.ShapeDtypeStruct
    block = (3 * rank + 8, 128)
    params = pltpu.CompilerParams(vmem_limit_bytes=VMEM_LIMIT)
    flat_sketch = sketch.reshape(count, rank, leaf_rows)
    stages = pair_tables(halos)
    faces = halos[2]
    packed, own, *sent = pl.pallas_call(
        pack_kernel,
        out_shape=(
            like((count,) + block, jnp.bfloat16),
            like((count + 1, 8, 128), jnp.float32),
        )
        + (like((SIDE * SIDE,) + block, jnp.bfloat16),) * faces,
        compiler_params=params,
        name="pack",
    )(test_matrix.reshape(count, rank, leaf_rows), offsets.reshape(count, 3, 128))
    z_halos = [from_partner(sent[0], "gz", 0)]
    if faces == 2:
        size = lax.axis_size("gz")
        across = [(i, i + 1) for i in range(1, size - 1, 2)]
        across = across + [(j, i) for i, j in across]
        z_halos.append(lax.ppermute(sent[1], "gz", across))
    inner = packed.reshape((SIDE, SIDE, SIDE) + block)
    columns = [h.reshape((SIDE, SIDE, 1) + block) for h in z_halos]
    extended = join([inner] + columns, 2)
    depth = extended.shape[2]
    flat = lambda parts: [x.reshape((-1,) + block) for x in parts]
    column = (SIDE + halos[1]) * depth
    whole = like((count, rank, leaf_rows), jnp.float32)
    sums = like((count + 1, rank, leaf_rows), jnp.float32)
    squares = like((count, rank, rank), jnp.float32)
    square = like((rank, rank), jnp.float32)
    single_scratch = pltpu.VMEM((rank, 2 * rank), jnp.float32)

    def add_stage(stage, blocks, before, name, time):
        kernel = first_kernel if before is None else next_kernel
        before = [] if before is None else [before]
        return pl.pallas_call(
            functools.partial(kernel, stage),
            out_shape=sums,
            in_specs=[IN_SMEM, IN_VMEM, IN_VMEM] + [IN_VMEM] * len(before),
            scratch_shapes=near_scratch(stage, blocks.shape[0]),
            cost_estimate=cost(time),
            compiler_params=params,
            name=name,
        )(near, own, blocks, *before)

    total = add_stage((halos, [(stages[0], 0, None)]), packed, None, "near_inner", 4)
    extended, total = lax.optimization_barrier((extended, total))
    y_halos = to_neighbours(extended[:, 0], extended[:, 1], "gy")
    total = add_stage((halos, [(stages[1], 0, None)]), packed, total, "near_inner_rest", 4)
    wide = join([extended] + [h[:, None] for h in y_halos], 1)
    wide, total = lax.optimization_barrier((wide, total))
    x_halos = to_neighbours(wide[0], wide[1], "gx")
    stage = (halos, [(stages[2], 0, None), (stages[3], SIDE * column, True)])
    blocks = join(flat([wide, x_halos[0]]), 0)
    total = add_stage(stage, blocks, total, "near_z_y_and_x", 9)
    stage = (halos, [(stages[3], 0, False)])
    parts = flat(x_halos[1:])
    far, grams, factor, samples, box_z = pl.pallas_call(
        functools.partial(last_kernel, stage),
        out_shape=(whole, squares, square, whole, square),
        in_specs=[IN_SMEM, IN_VMEM, IN_VMEM, IN_VMEM] + [IN_VMEM] * len(parts),
        scratch_shapes=[pltpu.VMEM(sums.shape, jnp.float32), single_scratch]
        + near_scratch(stage, column),
        compiler_params=params,
        name="near_x_and_box_level",
    )(near, own, total, flat_sketch, *parts)
    grouped = factor[None]
    grouped = join([grouped, from_partner(grouped, "gz", 0)], 0)
    factors = pl.pallas_call(
        leaf_factors,
        out_shape=like((rank * count, 2 * rank), jnp.float32),
        cost_estimate=cost(3),
        compiler_params=params,
        name="leaf_factors",
    )(grams)
    grouped, factors = lax.optimization_barrier((grouped, factors))
    grouped = join([grouped, from_partner(grouped, "gy", 0)], 0)
    leaf_t, level_t = pl.pallas_call(
        leaf_kernel,
        out_shape=(whole, like((rank, count * rank), jnp.float32)),
        scratch_shapes=[pltpu.VMEM((rank * count, 2 * rank), jnp.float32)]
        + [pltpu.VMEM((count, rank, rank), jnp.float32)] * 3,
        cost_estimate=cost(4),
        compiler_params=params,
        name="leaf_level",
    )(far, factors, samples, box_z)
    grouped, leaf_t, level_t = lax.optimization_barrier((grouped, leaf_t, level_t))
    grouped = join([grouped, from_partner(grouped, "gx", 0)], 0)
    nested = pl.pallas_call(
        group_kernel,
        out_shape=whole,
        scratch_shapes=[
            single_scratch,
            pltpu.VMEM((rank, count * rank), jnp.float32),
        ],
        compiler_params=params,
        name="group_level",
    )(grouped, samples, box_z)
    return (leaf_t.reshape(sketch.shape), level_t[None, None, None], nested.reshape(sketch.shape))


def solution(mesh):
    placed = (
        P("gx", "gy", "gz", None, None),
        P("gx", "gy", "gz", None, None),
        P("gx", "gy", "gz", None, None),
        P("gx", "gy", "gz", None),
    )
    return jax.shard_map(
        body,
        mesh=mesh,
        in_specs=placed,
        out_specs=(
            P("gx", "gy", "gz", None, None),
            P("gx", "gy", "gz", None, None),
            P("gx", "gy", "gz", None, None),
        ),
        check_vma=False,
    )
```

```python
import functools
import math

import jax
import jax.numpy as jnp
from jax import lax
from jax.experimental import pallas as pl
from jax.experimental.pallas import tpu as pltpu
from jax.sharding import PartitionSpec as P

EPSILON = 0.1
GROUP = 8
FIRST_LEAVES = 3
SIDE = 2
HIGHEST = lax.Precision.HIGHEST


def from_partner(x, axis, distance):
    return lax.ppermute(x, axis, [(i, i ^ 1 << distance) for i in range(lax.axis_size(axis))])


SMALL = 0.06


def matmul(a, b, precision=HIGHEST):
    return lax.dot_general(
        a, b, (((1,), (0,)), ((), ())), precision=precision, preferred_element_type=jnp.float32
    )


def matmul_t(a, b, precision=HIGHEST):
    return lax.dot_general(
        a, b, (((1,), (1,)), ((), ())), precision=precision, preferred_element_type=jnp.float32
    )


def join(parts, axis):
    return jnp.concatenate(parts, axis=axis)


def halves(x):
    high = x.astype(jnp.bfloat16)
    return high, (x - high.astype(jnp.float32)).astype(jnp.bfloat16)


def thirds(x):
    high = x.astype(jnp.bfloat16)
    rest = x - high.astype(jnp.float32)
    return (high,) + halves(rest)


def positions(shape):
    return (
        lax.broadcasted_iota(jnp.int32, shape, 0),
        lax.broadcasted_iota(jnp.int32, shape, 1),
    )


def unit(rank):
    row, column = positions((rank, rank))
    return jnp.where(row == column, 1.0, 0.0).astype(jnp.float32)


def upper(x):
    row, column = positions(x.shape)
    return jnp.where(row <= column, x, 0.0)


def half_lower(x):
    row, column = positions(x.shape)
    return jnp.where(row > column, x, jnp.where(row == column, 0.5 * x, 0.0))


def gram_of(parts):
    f, g, h = parts
    return matmul_t(join([f, f, g, g, f, h], 1), join([f, g, f, g, h, f], 1), None)


def right_side(parts):
    f, g, h = parts
    return join([f, f, g, g, h, f], 0)


def left_side(x):
    f, g, h = thirds(x)
    first = join([f, g], 1)
    return join([first, first, join([f, h], 1)], 1)


def near_gram(x, y):
    f, g = halves(x)
    u, v = halves(y)
    return matmul_t(join([f, f, g], 1), join([u, v, u], 1), None)


def near_unit_factor(excess):
    x = half_lower(excess)
    square = matmul(x, x, None)
    x = half_lower(excess - matmul_t(x, x, None))
    return x, x - square


def sum_of(parts):
    while len(parts) > 1:
        parts = [sum(parts[i : i + 2]) for i in range(0, len(parts), 2)]
    return parts[0]


def not_small(norm):
    return jnp.logical_not(norm[0, 0] <= SMALL * SMALL)


def batch_rows(work, rank, batch, low, high, width=8):
    shape = (batch, 2 * rank)

    def lane(values, index):
        return jnp.broadcast_to(values[:, rank + index : rank + index + 1], shape)

    for start in range(low, high, width):
        rows = [work[(start + i) * batch : (start + i + 1) * batch, :] for i in range(width)]
        scalars = [
            [lane(rows[i], start + j) if j >= i else None for j in range(width)]
            for i in range(width)
        ]
        for j in range(width):
            root = lax.rsqrt(scalars[j][j])
            rows[j] = rows[j] * root
            factor = [None if i <= j else scalars[j][i] * root for i in range(width)]
            for i in range(j + 1, width):
                rows[i] = rows[i] - factor[i] * rows[j]
                for k in range(i, width):
                    scalars[i][k] = scalars[i][k] - factor[i] * factor[k]
            work[(start + j) * batch : (start + j + 1) * batch, :] = rows[j]
        for lower in range(start + width, high):
            total = work[lower * batch : (lower + 1) * batch, :]
            for j in range(width):
                total = total - lane(rows[j], lower) * rows[j]
            work[lower * batch : (lower + 1) * batch, :] = total


def batch_update(work, rank, batch, low, high):
    size = high - low
    each = 128 // size
    row, column = positions((128, 128))
    for first in range(0, batch, each):
        done = join(
            [work[pl.ds(low * batch + first + i, size, stride=batch), :] for i in range(each)], 0
        )
        turned = done.T
        right = right_side(thirds(done))
        for top in range(high, rank, size):
            factor = join([turned[rank + top : rank + top + size, :]] * each, 0)
            f, g, h = thirds(jnp.where(row // size == column // size, factor, 0.0))
            change = matmul(join([f, g, f, g, f, h], 1), right, None)
            for i in range(each):
                place = pl.ds(top * batch + first + i, size, stride=batch)
                work[place, :] = work[place, :] - change[i * size : (i + 1) * size]


def eliminate_batch(work, rank, batch):
    half = rank // 2
    batch_rows(work, rank, batch, 0, half)
    batch_update(work, rank, batch, 0, half)
    batch_rows(work, rank, batch, half, rank)


def eliminate_single(work, rank):
    shape = (8, 2 * rank)
    row, _ = positions(shape)
    for start in range(0, rank, 8):
        blocks = {m: work[m : m + 8, :] for m in range(start, rank, 8)}
        columns = {
            m: [
                jnp.broadcast_to(blocks[m][:, rank + start + j : rank + start + j + 1], shape)
                for j in range(8)
            ]
            for m in blocks
        }
        done = blocks[start]
        for j in range(8):
            root = lax.rsqrt(columns[start][j][j : j + 1, :])
            line = [columns[start][i][j : j + 1, :] * root for i in range(8)]
            scaled = blocks[start][j : j + 1, :] * root
            done = jnp.where(row == j, scaled, done)
            for m in blocks:
                factor = columns[m][j] * root
                blocks[m] = blocks[m] - factor * scaled
                for i in range(j + 1, 8):
                    columns[m][i] = columns[m][i] - factor * line[i]
        work[start : start + 8, :] = done
        for m in blocks:
            if m > start:
                work[m : m + 8, :] = blocks[m]


def parity(axis):
    return lax.axis_index(axis) % 2


def to_neighbours(low, high, axis):
    size = lax.axis_size(axis)
    even = parity(axis) == 0
    received = []
    if size > 2:
        across = [(i, i + 1) for i in range(1, size - 1, 2)]
        across = across + [(j, i) for i, j in across]
        received.append(lax.ppermute(jnp.where(even, low, high), axis, across))
    pairs = [(i, i ^ 1) for i in range(size)]
    received.append(lax.ppermute(jnp.where(even, high, low), axis, pairs))
    return received[::-1]


def halo_count(axis):
    return 1 if lax.axis_size(axis) == 2 else 2


def leaf_index(x, y, z):
    return (x * SIDE + y) * SIDE + z


def pair_tables(halos):
    depth = SIDE + halos[2]
    wide = SIDE + halos[1]
    stages = ([], [], [], [])
    for a in range(SIDE**3):
        place = (a // 4, a // 2 % 2, a % 2)
        for k in range(27):
            at = [p + d for p, d in zip(place, (k // 9 - 1, k // 3 % 3 - 1, k % 3 - 1))]
            sides = tuple((axis, t) for axis, t in enumerate(at) if t in (-1, 2) and axis > 0)
            x, y, z = (2 if t == -1 else t for t in at)
            if at[0] == -1:
                stages[3].append((a, k, y * depth + z, sides, True))
            elif at[0] == 2:
                continue
            elif sides:
                stages[2].append((a, k, (x * wide + y) * depth + z, sides, False))
            else:
                stages[0 if a < FIRST_LEAVES else 1].append((a, k, leaf_index(x, y, z), sides, False))
    return stages


def far_sides(halos):
    found = {}
    for axis, name in enumerate(("gx", "gy", "gz")):
        place = lax.axis_index(name)
        odd = place % 2
        other = halos[axis] - 1
        found[axis, -1] = ((place > 0).astype(jnp.int32), (1 - odd) * other)
        found[axis, 2] = ((place < lax.axis_size(name) - 1).astype(jnp.int32), odd * other)
    return found


def list_pairs(pairs, halos, near, listed, count, x_side):
    found = far_sides(halos)
    depth = SIDE + halos[2]
    joint = {}
    for a, k, source, sides, across in pairs:
        key = (sides, across)
        if key not in joint:
            inside, moved, high = jnp.int32(1), jnp.int32(0), jnp.int32(0)
            if across:
                inside = x_side[1]
                high = x_side[0]
            steps = {1: depth, 2: 1}
            for side in sides:
                inside = inside * found[side][0]
                moved = moved + found[side][1] * steps[side[0]]
            joint[key] = (inside, moved * (16 * 27) + high * (4 * 27 + 18), high)
        inside, moved, high = joint[key]
        x, y, z = a // 4, a // 2 % 2, a % 2
        code = jnp.int32((source * 16 + a) * 27 + k)
        if sides or across:
            if across:
                x, k = x + high, k + high * 18
            taken = near[x, y, z, k] * inside
            code = code + moved
        else:
            taken = near[x, y, z, k]
        listed[count] = code
        count = count + taken
    return count


def close_list(listed, count, blank):
    for i in range(GROUP):
        listed[count + i] = jnp.int32(blank)
    return count


def spread_offsets(blocks, places, turned, spread):
    rank3 = blocks.shape[1] - 8
    row, lane = positions((128, 384))
    for first in range(0, len(places), 32):
        chunk = places[first : first + 32]
        turned[...] = jnp.zeros_like(turned)
        for i, s in enumerate(chunk):
            turned[4 * i : 4 * i + 4, :] = blocks[s, rank3:, :].astype(jnp.float32)[:4]
        columns = turned[...].T.astype(jnp.bfloat16)
        for i, s in enumerate(chunk):
            chosen = jnp.where(row == 4 * i + lane // 128, 1.0, 0.0).astype(jnp.bfloat16)
            values = matmul(columns, chosen, None)
            for p in range(3):
                spread[s, p] = values[:, 128 * p : 128 * (p + 1)]


def tile_rows(own, spread, rows):
    r = [own[p] - spread[p, rows, :] for p in range(3)]
    squares = [v * v for v in r]
    softened = squares[0] + squares[1] + squares[2] + EPSILON * EPSILON
    lifted = softened + EPSILON * EPSILON
    root = lax.rsqrt(softened)
    h = root * root * root
    ry, rz = r[1] * h, r[2] * h
    tiles = {(p, p): (squares[p] + lifted) * h for p in range(3)}
    tiles[0, 1], tiles[0, 2], tiles[1, 2] = r[0] * ry, r[0] * rz, r[1] * rz
    return {pq: tile.astype(jnp.bfloat16) for pq, tile in tiles.items()}


def add_pairs(count, listed, blocks, own, spread, total):
    chunk = 16

    def add_group(first, size):
        for u in range(size):
            code = listed[first + u]
            pair = lax.div(code, jnp.int32(27))
            k = code - pair * 27
            source = lax.shift_right_logical(pair, jnp.int32(4))
            a = lax.bitwise_and(pair, jnp.int32(15))
            dx = lax.div(k, jnp.int32(9))
            dy = lax.div(k, jnp.int32(3)) - dx * 3
            dz = k - dx * 9 - dy * 3
            own_rows = own[a]
            placed = [
                jnp.broadcast_to(
                    own_rows[p : p + 1] + (1 - step).astype(jnp.float32), (chunk, 128)
                )
                for p, step in enumerate((dx, dy, dz))
            ]
            parts = [
                tile_rows(placed, spread.at[source], pl.ds(j, chunk))
                for j in range(0, 128, chunk)
            ]
            tiles = {
                pq: jnp.concatenate([part[pq] for part in parts], axis=0) for pq in parts[0]
            }
            matrix = jnp.concatenate(
                [
                    jnp.concatenate([tiles[min(p, q), max(p, q)] for p in range(3)], axis=1)
                    for q in range(3)
                ],
                axis=0,
            )
            rank = total.shape[1]
            sampled = jnp.concatenate(
                [blocks[source, q * rank : (q + 1) * rank, :] for q in range(3)], axis=1
            )
            total[a] += matmul(sampled, matrix, None)

    groups = lax.div(count, jnp.int32(GROUP))
    rest = count - groups * GROUP

    @pl.loop(0, groups)
    def _(group):
        add_group(group * GROUP, GROUP)

    @pl.when(rest > GROUP // 2)
    def _():
        add_group(groups * GROUP, GROUP)

    @pl.when(jnp.logical_and(rest > 0, rest <= GROUP // 2))
    def _():
        add_group(groups * GROUP, GROUP // 2)


def list_stage(stage, near, listed, blank):
    halos, lists = stage
    odd = lax.axis_index("gx") % 2
    size = lax.axis_size("gx")
    start = jnp.int32(0)
    for pairs, first, within in lists:
        pairs = [(a, k, source + first, sides, across) for a, k, source, sides, across in pairs]
        x_side = None
        if within is True:
            x_side = (1 - odd, jnp.int32(1))
        elif within is False:
            place = lax.axis_index("gx")
            inside = jnp.logical_and(place > 0, place < size - 1).astype(jnp.int32)
            x_side = (odd, inside)
        start = list_pairs(pairs, halos, near, listed, start, x_side)
    return close_list(listed, start, blank)


def near_stage(stage, near, own, blocks, total, listed, turned, spread):
    count = list_stage(stage, near, listed, (total.shape[0] - 1) * 27 + 13)
    places = sorted({first + pair[2] for pairs, first, _ in stage[1] for pair in pairs})
    spread_offsets(blocks, with_far_places(places, stage), turned, spread)
    add_pairs(count, listed, blocks, own, spread, total)


def with_far_places(places, stage):
    halos, lists = stage
    depth = SIDE + halos[2]
    found = set(places)
    for pairs, first, _ in lists:
        for _, _, source, sides, _ in pairs:
            moves = [0]
            for axis, _ in sides:
                step = {1: depth, 2: 1}[axis] * (halos[axis] - 1)
                moves = moves + [move + step for move in moves]
            found.update(first + source + move for move in moves)
    return sorted(found)


def first_kernel(stage, near, own, blocks, total, *scratch):
    total[...] = jnp.zeros_like(total)
    near_stage(stage, near, own, blocks, total, *scratch)


def next_kernel(stage, near, own, blocks, before, total, *scratch):
    total[...] = before[...]
    near_stage(stage, near, own, blocks, total, *scratch)


def last_kernel(stage, near, own, before, sketch, *rest):
    *parts, far, grams, factor, samples, z_out = rest[:-5]
    total, single, *scratch = rest[-5:]
    total[...] = before[...]
    for blocks in parts:
        near_stage(stage, near, own, blocks, total, *scratch)
    far[...] = sketch[...] - total[: far.shape[0]]
    box_level(far, grams, factor, samples, z_out, single)


def pack_kernel(samples, offsets, packed, own, *faces):
    count, rank, leaf_rows = samples.shape
    filler = jnp.zeros((5, 128), jnp.float32)
    for a in range(count):
        for q in range(3):
            packed[a, q * rank : (q + 1) * rank, :] = samples[a, :, q * 128 : (q + 1) * 128]
        rows = jnp.concatenate([offsets[a].astype(jnp.float32), filler], axis=0)
        packed[a, 3 * rank :, :] = rows.astype(jnp.bfloat16)
        own[a] = rows
    own[count] = jnp.zeros_like(own[count])
    planes = [1 - parity("gz"), parity("gz")]
    for face, plane in zip(faces, planes):
        for column in range(SIDE * SIDE):
            face[column] = packed[column * SIDE + plane]


VMEM_LIMIT = 48 * 1024 * 1024


def near_scratch(stage, count):
    length = sum(len(pairs) for pairs, _, _ in stage[1])
    return [
        pltpu.SMEM((length + GROUP + 1,), jnp.int32),
        pltpu.VMEM((128, 128), jnp.float32),
        pltpu.VMEM((count, 3, 128, 128), jnp.float32),
    ]


def cost(microseconds):
    return pl.CostEstimate(
        flops=microseconds * 1000 * 1000 * 1000, bytes_accessed=4 * 1024 * 1024, transcendentals=0
    )


IN_SMEM = pl.BlockSpec(memory_space=pltpu.SMEM)
IN_VMEM = pl.BlockSpec(memory_space=pltpu.VMEM)


def box_level(far, grams_out, factor_out, samples_out, z_out, single):
    count, rank, _ = far.shape
    eye = unit(rank)
    grams = [gram_of(thirds(far[a])) for a in range(count)]
    for a in range(count):
        grams_out[a] = grams[a]
    total = sum_of(grams)
    single[...] = join([eye, 0.5 * (total + total.T)], 1)
    eliminate_single(single, rank)
    left = left_side(single[:, :rank])
    lower = upper(single[:, rank:]).T
    samples = [matmul(left, right_side(thirds(far[a])), None) for a in range(count)]
    grams = [near_gram(rows, rows) for rows in samples]
    for a in range(count):
        samples_out[a] = samples[a]
    excess = sum_of(grams) - eye
    x, z_out[...] = near_unit_factor(excess)
    factor_out[...] = lower + matmul(left_side(lower), right_side(thirds(x)), None)

    @pl.when(not_small(jnp.sum(excess * excess, keepdims=True)))
    def _():
        single[...] = join([eye, eye + excess], 1)
        eliminate_single(single, rank)
        factor_out[...] = matmul(lower, upper(single[:, rank:]).T)
        for a in range(count):
            samples_out[a] = matmul(single[:, :rank], samples_out[a])
        z_out[...] = jnp.zeros_like(eye)


def leaf_factors(grams, work):
    count, rank, _ = grams.shape
    eye = unit(rank)
    for a in range(count):
        work[pl.ds(a, rank, stride=count), :] = join([eye, grams[a]], 1)
    eliminate_batch(work, rank, count)


def leaf_kernel(far, factors, samples, box_z, leaf_out, level_out, work, blocks, es, zs):
    count, rank, leaf_rows = far.shape
    eye = unit(rank)
    inverses = [factors[pl.ds(a, rank, stride=count), :][:, :rank] for a in range(count)]
    bases = [
        matmul(left_side(inverses[a]), right_side(thirds(far[a])), None) for a in range(count)
    ]
    products = [near_gram(join([bases[a], samples[a]], 0), bases[a]) for a in range(count)]
    excesses = [product[:rank] - eye for product in products]
    for a in range(count):
        leaf_out[a] = bases[a]
        blocks[a] = products[a][rank:]
        es[a] = excesses[a]
    inverse_parts = [near_unit_factor(excess)[1] for excess in excesses]
    for a in range(count):
        zs[a] = inverse_parts[a]
    norms = [jnp.sum(excess * excess, keepdims=True) for excess in excesses]
    largest = functools.reduce(jnp.maximum, norms)

    @pl.when(not_small(largest))
    def _():
        for a in range(count):
            work[pl.ds(a, rank, stride=count), :] = join([eye, eye + es[a]], 1)
        eliminate_batch(work, rank, count)
        for a in range(count):
            inverse = work[pl.ds(a, rank, stride=count), :][:, :rank]
            leaf_out[a] = matmul(inverse, leaf_out[a])
            blocks[a] = matmul_t(blocks[a], inverse)
            zs[a] = jnp.zeros_like(eye)

    bases = [leaf_out[a] for a in range(count)]
    bases = [basis - matmul(zs[a], basis, None) for a, basis in enumerate(bases)]
    crossed = [blocks[a] for a in range(count)]
    crossed = [block - matmul_t(block, zs[a], None) for a, block in enumerate(crossed)]
    for a in range(count):
        leaf_out[a] = bases[a] * math.sqrt(leaf_rows)
    block = join(crossed, 1) * math.sqrt(count * rank)
    level_out[...] = block - matmul(box_z[...], block, None)


def group_kernel(factors, samples, box_z, nested_out, single, stack):
    count, rank, _ = factors.shape
    eye = unit(rank)
    for b in range(count):
        stack[:, b * rank : (b + 1) * rank] = factors[b]
    parts = thirds(stack[...])
    gram = gram_of(parts)
    single[...] = join([eye, 0.5 * (gram + gram.T)], 1)
    eliminate_single(single, rank)
    block = matmul(left_side(single[:, :rank]), right_side(parts), None)
    excess = near_gram(block, block) - eye
    own = block[:, :rank] * (8.0 * math.sqrt(samples.shape[2]))
    own = own - matmul(own, box_z[...], None)
    left = join(halves(own) * 2, 1)
    leaves = range(samples.shape[0])
    parts = [halves(samples[a]) for a in leaves]
    mixed = [matmul(left, join([f, f, g, g], 0), None) for f, g in parts]
    z = near_unit_factor(excess)[1]
    nested = [rows - matmul(z, rows, None) for rows in mixed]
    for a in leaves:
        nested_out[a] = nested[a]

    @pl.when(not_small(jnp.sum(excess * excess, keepdims=True)))
    def _():
        single[...] = join([eye, eye + excess], 1)
        eliminate_single(single, rank)
        left = join(halves(matmul(single[:, :rank], own)) * 2, 1)
        for a in leaves:
            f, g = halves(samples[a])
            nested_out[a] = matmul(left, join([f, f, g, g], 0), None)


def body(sketch, test_matrix, offsets, near):
    rank, leaf_rows = sketch.shape[3:]
    count = SIDE**3
    halos = [halo_count(axis) for axis in ("gx", "gy", "gz")]
    like = jax.ShapeDtypeStruct
    block = (3 * rank + 8, 128)
    params = pltpu.CompilerParams(vmem_limit_bytes=VMEM_LIMIT)
    flat_sketch = sketch.reshape(count, rank, leaf_rows)
    stages = pair_tables(halos)
    faces = halos[2]
    packed, own, *sent = pl.pallas_call(
        pack_kernel,
        out_shape=(
            like((count,) + block, jnp.bfloat16),
            like((count + 1, 8, 128), jnp.float32),
        )
        + (like((SIDE * SIDE,) + block, jnp.bfloat16),) * faces,
        compiler_params=params,
        name="pack",
    )(test_matrix.reshape(count, rank, leaf_rows), offsets.reshape(count, 3, 128))
    z_halos = [from_partner(sent[0], "gz", 0)]
    if faces == 2:
        size = lax.axis_size("gz")
        across = [(i, i + 1) for i in range(1, size - 1, 2)]
        across = across + [(j, i) for i, j in across]
        z_halos.append(lax.ppermute(sent[1], "gz", across))
    inner = packed.reshape((SIDE, SIDE, SIDE) + block)
    columns = [h.reshape((SIDE, SIDE, 1) + block) for h in z_halos]
    extended = join([inner] + columns, 2)
    depth = extended.shape[2]
    flat = lambda parts: [x.reshape((-1,) + block) for x in parts]
    column = (SIDE + halos[1]) * depth
    whole = like((count, rank, leaf_rows), jnp.float32)
    sums = like((count + 1, rank, leaf_rows), jnp.float32)
    squares = like((count, rank, rank), jnp.float32)
    square = like((rank, rank), jnp.float32)
    single_scratch = pltpu.VMEM((rank, 2 * rank), jnp.float32)

    def add_stage(stage, blocks, before, name, time):
        kernel = first_kernel if before is None else next_kernel
        before = [] if before is None else [before]
        return pl.pallas_call(
            functools.partial(kernel, stage),
            out_shape=sums,
            in_specs=[IN_SMEM, IN_VMEM, IN_VMEM] + [IN_VMEM] * len(before),
            scratch_shapes=near_scratch(stage, blocks.shape[0]),
            cost_estimate=cost(time),
            compiler_params=params,
            name=name,
        )(near, own, blocks, *before)

    total = add_stage((halos, [(stages[0], 0, None)]), packed, None, "near_inner", 4)
    extended, total = lax.optimization_barrier((extended, total))
    y_halos = to_neighbours(extended[:, 0], extended[:, 1], "gy")
    total = add_stage((halos, [(stages[1], 0, None)]), packed, total, "near_inner_rest", 4)
    wide = join([extended] + [h[:, None] for h in y_halos], 1)
    wide, total = lax.optimization_barrier((wide, total))
    x_halos = to_neighbours(wide[0], wide[1], "gx")
    stage = (halos, [(stages[2], 0, None), (stages[3], SIDE * column, True)])
    blocks = join(flat([wide, x_halos[0]]), 0)
    total = add_stage(stage, blocks, total, "near_z_y_and_x", 9)
    stage = (halos, [(stages[3], 0, False)])
    parts = flat(x_halos[1:])
    far, grams, factor, samples, box_z = pl.pallas_call(
        functools.partial(last_kernel, stage),
        out_shape=(whole, squares, square, whole, square),
        in_specs=[IN_SMEM, IN_VMEM, IN_VMEM, IN_VMEM] + [IN_VMEM] * len(parts),
        scratch_shapes=[pltpu.VMEM(sums.shape, jnp.float32), single_scratch]
        + near_scratch(stage, column),
        compiler_params=params,
        name="near_x_and_box_level",
    )(near, own, total, flat_sketch, *parts)
    grouped = factor[None]
    grouped = join([grouped, from_partner(grouped, "gz", 0)], 0)
    factors = pl.pallas_call(
        leaf_factors,
        out_shape=like((rank * count, 2 * rank), jnp.float32),
        cost_estimate=cost(3),
        compiler_params=params,
        name="leaf_factors",
    )(grams)
    grouped, factors = lax.optimization_barrier((grouped, factors))
    grouped = join([grouped, from_partner(grouped, "gy", 0)], 0)
    leaf_t, level_t = pl.pallas_call(
        leaf_kernel,
        out_shape=(whole, like((rank, count * rank), jnp.float32)),
        scratch_shapes=[pltpu.VMEM((rank * count, 2 * rank), jnp.float32)]
        + [pltpu.VMEM((count, rank, rank), jnp.float32)] * 3,
        cost_estimate=cost(4),
        compiler_params=params,
        name="leaf_level",
    )(far, factors, samples, box_z)
    grouped, leaf_t, level_t = lax.optimization_barrier((grouped, leaf_t, level_t))
    grouped = join([grouped, from_partner(grouped, "gx", 0)], 0)
    nested = pl.pallas_call(
        group_kernel,
        out_shape=whole,
        scratch_shapes=[
            single_scratch,
            pltpu.VMEM((rank, count * rank), jnp.float32),
        ],
        compiler_params=params,
        name="group_level",
    )(grouped, samples, box_z)
    return (leaf_t.reshape(sketch.shape), level_t[None, None, None], nested.reshape(sketch.shape))


def solution(mesh):
    placed = (
        P("gx", "gy", "gz", None, None),
        P("gx", "gy", "gz", None, None),
        P("gx", "gy", "gz", None, None),
        P("gx", "gy", "gz", None),
    )
    return jax.shard_map(
        body,
        mesh=mesh,
        in_specs=placed,
        out_specs=(
            P("gx", "gy", "gz", None, None),
            P("gx", "gy", "gz", None, None),
            P("gx", "gy", "gz", None, None),
        ),
        check_vma=False,
    )
```
